32 devices in a mesh: sector: 8 (over z, core), slab: 4 (over y, x).
Axes of the slice: x: 2, y: 2, z: 4, core: 2. Of those that a mesh axis runs over, the one named last changes fastest.
Arguments:
- volume_rhs: float32 [128, 64, 8, 256], P('sector', 'slab'), may hold values from -80 to 80
- surface_rhs: float32 [64, 64, 256], P('sector', 'slab'), may hold values from -6 to 6
- volume_guess: float32 [128, 64, 8, 256], P('sector', 'slab'), may hold values from -6 to 6
- surface_guess: float32 [64, 64, 256], P('sector', 'slab'), may hold values from -6 to 6
- bem_matrix: bfloat16 [2, 4096, 4096], P(None, 'sector', 'slab'), may hold values from -0.0625 to 0.0625
- stiffness: float32 [3, 8, 8], replicated, may hold values from -1.05 to 3, as said below
- mass_shift: float32 [128, 64, 8], P('sector', 'slab'), may hold values from -3 to 0
Outputs:
- volume_solution: float32 [128, 64, 8, 256], P('sector', 'slab')
- surface_solution: float32 [64, 64, 256], P('sector', 'slab')
The draws below stay inside these ranges and needn't reach their ends.
Inputs may be any that keep to these rules, and one draw needn't show every extreme that they name: stiffness[d] is symmetric, its diagonal entries between 1.5 and 3.
All inputs are finite; a program needn't handle non-finite values.
Results may differ from the reference program's by a relative error of at most 0.0003.
Values may be sent and summed in bfloat16 or wider, within the bound.
No kernel may reach another device: no remote copies, remote signals or barrier semaphores. Data moves between devices by JAX's collectives and lax.ppermute only.
A program may use at most 128 MiB of HBM per device.

```python
import math
import jax
import jax.numpy as jnp
from jax import lax

ORDER = 8
RADIAL = 8
SOURCES = 128
LANES = 256
NTH = 128
NZ = 64
NBEM = 4096
N_SLAB = 4


def draw_volume_rhs(key, part):
    key = jax.random.fold_in(key, 11)
    keys = jax.random.split(key, 3)
    shape = (NTH, NZ, RADIAL, LANES)
    theta = jnp.arange(NTH, dtype=jnp.float32) / NTH
    axial = jnp.arange(NZ, dtype=jnp.float32) / NZ
    base = jnp.clip(jax.random.normal(keys[0], shape, jnp.float32), -4.0, 4.0)
    growth = math.log(3.0)
    spread = jnp.exp(growth * (theta[:, None] + axial[None, :])) / 3.0
    source_scale = jnp.exp(jax.random.uniform(keys[2], (SOURCES,), jnp.float32, math.log(0.3), math.log(3.0)))
    lane_scale = jnp.concatenate([source_scale, source_scale])
    return (base * spread[:, :, None, None] * lane_scale).astype(jnp.float32)


def draw_stiffness(key, part):
    key = jax.random.fold_in(key, 23)
    keys = jax.random.split(key, 2)
    raw = jnp.clip(jax.random.normal(keys[0], (3, ORDER, ORDER), jnp.float32), -3.0, 3.0) * 0.35
    symmetric = 0.5 * (raw + jnp.swapaxes(raw, 1, 2))
    diagonal = jax.random.uniform(keys[1], (3, ORDER, 1), jnp.float32, 1.5, 3.0)
    identity = jnp.eye(ORDER, dtype=bool)
    return jnp.where(identity, diagonal, symmetric).astype(jnp.float32)


def shard_levels(rng, dims, pieces, least, top_value):
    factor_of, own = 1.0, jax.random.fold_in(rng, 6)
    for axis_at, parts in pieces:
        draws = jnp.exp(jax.random.uniform(jax.random.fold_in(own, axis_at), (parts,), jnp.float32, least / len(pieces), top_value / len(pieces)))
        factor_of = factor_of * jnp.repeat(draws, dims[axis_at] // parts).reshape([-1 if axis == axis_at else 1 for axis in range(len(dims))])
    return factor_of


def bell_draw(own_key, extent, width, reach, cuts=(), held_as=jnp.bfloat16):
    entries = jax.random.normal(own_key, extent, jnp.float32) * width
    if len(cuts) > 0:
        entries = shard_levels(own_key, extent, cuts, -0.22, 0.18) * entries
    return jnp.clip(entries, min=-reach, max=reach).astype(held_as)


def setup_inputs(seed: int = 0) -> dict:
    streams_of = jax.random.split(jax.random.key(seed), 8)
    volume_rhs = draw_volume_rhs(jax.random.fold_in(streams_of[7], 71), 0)
    surface_rhs = bell_draw(streams_of[1], (NTH // 2, NZ, LANES), 1.0, 6.0, ((0, 8), (1, 4)), jnp.float32)
    volume_guess = bell_draw(streams_of[2], (NTH, NZ, RADIAL, LANES), 1.0, 6.0, ((0, 8), (1, 4)), jnp.float32)
    surface_guess = bell_draw(streams_of[3], (NTH // 2, NZ, LANES), 1.0, 6.0, ((0, 8), (1, 4)), jnp.float32)
    bem_matrix = bell_draw(streams_of[4], (2, NBEM, NBEM), (2 * NBEM) ** -0.5, 0.0625, ((1, 8), (2, 4)))
    stiffness = draw_stiffness(jax.random.fold_in(streams_of[7], 71), 0)
    mass_shift = jnp.clip(-3.0 + 3.0 * jax.random.uniform(streams_of[6], (NTH, NZ, RADIAL), jnp.float32) ** shard_levels(streams_of[6], (NTH, NZ, RADIAL), ((0, 8), (1, 4)), -0.2, 0.2), -3.0, 0.0)
    return {"volume_rhs": volume_rhs, "surface_rhs": surface_rhs, "volume_guess": volume_guess, "surface_guess": surface_guess, "bem_matrix": bem_matrix, "stiffness": stiffness, "mass_shift": mass_shift}


PENALTY = 1.0
EPSILON = 1e-06

def element_terms(values, stiffness_d, which_axis, before, beyond):
    per_element = stiffness_d.shape[0]
    elements = values.shape[which_axis] // per_element
    split_shape = values.shape[:which_axis] + (elements, per_element) + values.shape[which_axis + 1:]
    blocks = values.reshape(split_shape)
    einsum_forms = ('pq,eqbcl->epbcl', 'pq,aeqcl->aepcl', 'pq,abeql->abepl')
    result = jnp.einsum(einsum_forms[which_axis], stiffness_d, blocks, precision=lax.Precision.HIGHEST)
    first_nodes = lax.index_in_dim(blocks, 0, which_axis + 1, keepdims=False)
    last_nodes = lax.index_in_dim(blocks, per_element - 1, which_axis + 1, keepdims=False)
    prev_last = jnp.concatenate([before, lax.slice_in_dim(last_nodes, 0, elements - 1, axis=which_axis)], which_axis)
    next_first = jnp.concatenate([lax.slice_in_dim(first_nodes, 1, elements, axis=which_axis), beyond], which_axis)
    leading = (slice(None),) * (which_axis + 1)
    result = result.at[leading + (0,)].add(PENALTY * (first_nodes - prev_last))
    result = result.at[leading + (per_element - 1,)].add(PENALTY * (last_nodes - next_first))
    return result.reshape(values.shape)

def volume_apply(volume, stiffness, mass_shift, theta_before, theta_beyond, axial_before, axial_beyond):
    radial_zero = jnp.zeros_like(volume[:, :, :1])
    total = element_terms(volume, stiffness[0], 0, theta_before, theta_beyond)
    total = total + element_terms(volume, stiffness[1], 1, axial_before, axial_beyond)
    total = total + element_terms(volume, stiffness[2], 2, radial_zero, radial_zero)
    return total + mass_shift[..., None] * volume

def face_mean(volume):
    outer = volume[:, :, -1, :]
    paired = outer.reshape(outer.shape[0] // 2, 2, outer.shape[1], outer.shape[2])
    return 0.5 * lax.optimization_barrier(jnp.sum(paired, axis=1))

def add_faces(total, surface):
    return total.at[:, :, -1, :].add(jnp.repeat(surface, 2, axis=0))

def complex_join(real_prod, imag_prod):
    half_width = real_prod.shape[-1] // 2
    return jnp.concatenate([real_prod[..., :half_width] - imag_prod[..., half_width:], real_prod[..., half_width:] + imag_prod[..., :half_width]], -1)

def split_rounded(surface):
    upper_part = surface.astype(jnp.bfloat16)
    widened = lax.optimization_barrier(upper_part).astype(jnp.float32)
    lower_part = (surface - widened).astype(jnp.bfloat16)
    return jnp.concatenate([upper_part, lower_part], -1)

def fold_halves(product):
    lane_count = product.shape[-1] // 2
    return product[..., :lane_count] + product[..., lane_count:]

def inner_terms(left_pair, right_pair):
    real_part = jnp.zeros((left_pair[0].shape[-1] // 2,), jnp.float32)
    imag_part = jnp.zeros((left_pair[0].shape[-1] // 2,), jnp.float32)
    for left, right in zip(left_pair, right_pair):
        half_width = left.shape[-1] // 2
        summed_axes = tuple(range(left.ndim - 1))
        left_real, left_imag = (left[..., :half_width], left[..., half_width:])
        right_real, right_imag = (right[..., :half_width], right[..., half_width:])
        real_part = real_part + lax.optimization_barrier(jnp.sum(left_real * right_real + left_imag * right_imag, axis=summed_axes))
        imag_part = imag_part + lax.optimization_barrier(jnp.sum(left_real * right_imag - left_imag * right_real, axis=summed_axes))
    return (real_part, imag_part)

def norm_terms(pair):
    half_width = pair[0].shape[-1] // 2
    squares = jnp.zeros((half_width,), jnp.float32)
    for values in pair:
        lane_sums = lax.optimization_barrier(jnp.sum(values * values, axis=tuple(range(values.ndim - 1))))
        squares = squares + lane_sums[:half_width] + lane_sums[half_width:]
    return squares

def scale_pair(pair, coef_real, coef_imag):
    scaled = []
    for values in pair:
        half_width = values.shape[-1] // 2
        real_part, imag_part = (values[..., :half_width], values[..., half_width:])
        scaled.append(jnp.concatenate([coef_real * real_part - coef_imag * imag_part, coef_real * imag_part + coef_imag * real_part], -1))
    return tuple(scaled)

def divide_pair(pair, norm_value):
    doubled = jnp.concatenate([norm_value, norm_value])
    return tuple((values / doubled for values in pair))

def subtract_pair(first_pair, second_pair):
    return tuple((one - two for one, two in zip(first_pair, second_pair)))

def add_pair(first_pair, second_pair):
    return tuple((one + two for one, two in zip(first_pair, second_pair)))

def least_squares(beta, diag_real, diag_imag, below, upper_real, upper_imag, inner_real, inner_imag, bottom):
    rho_first = jnp.sqrt(diag_real * diag_real + diag_imag * diag_imag + below * below)
    cos_real = diag_real / rho_first
    cos_imag = diag_imag / rho_first
    sine = below / rho_first
    top_real = cos_real * upper_real + cos_imag * upper_imag + sine * inner_real
    top_imag = cos_real * upper_imag - cos_imag * upper_real + sine * inner_imag
    turn_real = cos_real * inner_real - cos_imag * inner_imag - sine * upper_real
    turn_imag = cos_real * inner_imag + cos_imag * inner_real - sine * upper_imag
    second_sq = turn_real * turn_real + turn_imag * turn_imag + bottom * bottom
    lower_rhs = -sine * beta
    one_real = turn_real * lower_rhs / second_sq
    one_imag = -turn_imag * lower_rhs / second_sq
    zero_real = (cos_real * beta - (top_real * one_real - top_imag * one_imag)) / rho_first
    zero_imag = (-cos_imag * beta - (top_real * one_imag + top_imag * one_real)) / rho_first
    return (zero_real, zero_imag, one_real, one_imag)

def bem_product(surface, bem_matrix):
    rounded = split_rounded(surface)
    pairs_count = rounded.shape[0]
    wide = rounded.shape[-1]
    cyclic = rounded.reshape(pairs_count // N_SLAB, N_SLAB, NZ, wide).transpose(1, 0, 2, 3).reshape(NBEM, wide)
    real_prod = fold_halves(jnp.dot(bem_matrix[0], cyclic, preferred_element_type=jnp.float32))
    imag_prod = fold_halves(jnp.dot(bem_matrix[1], cyclic, preferred_element_type=jnp.float32))
    return complex_join(real_prod, imag_prod).reshape(pairs_count, NZ, LANES)

def apply_operator(volume, surface, stiffness, mass_shift, bem_matrix):
    axial_zero = jnp.zeros_like(volume[:, :1])
    total = volume_apply(volume, stiffness, mass_shift, volume[-1:], volume[:1], axial_zero, axial_zero)
    return (add_faces(total, surface), bem_product(surface, bem_matrix) - face_mean(volume))

def reference(volume_rhs, surface_rhs, volume_guess, surface_guess, bem_matrix, stiffness, mass_shift):

    def operator(pair):
        return apply_operator(pair[0], pair[1], stiffness, mass_shift, bem_matrix)
    guess = (volume_guess, surface_guess)
    image = operator(guess)
    residual = (volume_rhs - image[0], surface_rhs - image[1])
    beta = jnp.sqrt(norm_terms(residual) + EPSILON)
    basis_zero = divide_pair(residual, beta)
    image = operator(basis_zero)
    diag_real, diag_imag = inner_terms(basis_zero, image)
    remainder = subtract_pair(image, scale_pair(basis_zero, diag_real, diag_imag))
    below = jnp.sqrt(norm_terms(remainder) + EPSILON)
    basis_one = divide_pair(remainder, below)
    image = operator(basis_one)
    upper_real, upper_imag = inner_terms(basis_zero, image)
    inner_real, inner_imag = inner_terms(basis_one, image)
    remainder = subtract_pair(image, scale_pair(basis_zero, upper_real, upper_imag))
    remainder = subtract_pair(remainder, scale_pair(basis_one, inner_real, inner_imag))
    bottom = jnp.sqrt(norm_terms(remainder) + EPSILON)
    zero_real, zero_imag, one_real, one_imag = least_squares(beta, diag_real, diag_imag, below, upper_real, upper_imag, inner_real, inner_imag, bottom)
    solution = add_pair(guess, scale_pair(basis_zero, zero_real, zero_imag))
    solution = add_pair(solution, scale_pair(basis_one, one_real, one_imag))
    return (solution[0], solution[1])
```

```python
import functools
import math

import jax
import jax.numpy as jnp
from jax import lax
from jax.experimental import pallas as pl
from jax.experimental.pallas import tpu as pltpu
from jax.sharding import PartitionSpec as P

PENALTY = 1.0
EPSILON = 1e-06
F32 = jnp.float32
BF16 = jnp.bfloat16
WIRE = jnp.float16
LANES = 256
HALF = 128
VMEM_LIMIT = 48 * 1024 * 1024
WHOLE = pl.BlockSpec(memory_space=pltpu.VMEM)
SCALARS = pl.BlockSpec(memory_space=pltpu.SMEM)


def call(kernel, out_shape, n_scalars, n_arrays, scratch=(), flops=0, bytes_accessed=0, name=None):
    return pl.pallas_call(
        kernel,
        out_shape=out_shape,
        in_specs=[SCALARS] * n_scalars + [WHOLE] * n_arrays,
        out_specs=jax.tree.map(lambda _: WHOLE, out_shape),
        scratch_shapes=list(scratch),
        compiler_params=pltpu.CompilerParams(vmem_limit_bytes=VMEM_LIMIT),
        cost_estimate=pl.CostEstimate(
            flops=flops, bytes_accessed=bytes_accessed, transcendentals=0
        ),
        name=name,
    )


def shape(*dims):
    return jax.ShapeDtypeStruct(dims, F32)


def split_bf16(values):
    upper = values.astype(BF16)
    lower = (values - upper.astype(F32)).astype(BF16)
    return upper, lower


def one_hot(rows, columns, pick):
    row = lax.broadcasted_iota(jnp.int32, (rows, columns), 0)
    column = lax.broadcasted_iota(jnp.int32, (rows, columns), 1)
    return (pick(row) == column).astype(F32)


def line_matrix(stiffness, order, nodes, rows, fast):
    select = one_hot(rows, order, lambda row: (row // fast) % order)
    spread = jnp.dot(select, stiffness, precision=lax.Precision.HIGHEST)
    full = lax.dot_general(
        spread, select, (((1,), (1,)), ((), ())), precision=lax.Precision.HIGHEST
    )
    row = lax.broadcasted_iota(jnp.int32, (rows, rows), 0)
    column = lax.broadcasted_iota(jnp.int32, (rows, rows), 1)
    row_node, column_node = row // fast, column // fast
    same_fast = row % fast == column % fast
    same_element = (row_node // order == column_node // order) & same_fast
    block = jnp.where(same_element, full, 0.0)
    edge = (row_node % order == 0) | (row_node % order == order - 1)
    block = block + jnp.where((row == column) & edge, PENALTY, 0.0)
    back = (row_node % order == 0) & (column_node == row_node - 1) & same_fast
    ahead = (row_node % order == order - 1) & (column_node == row_node + 1) & same_fast
    return block - jnp.where(back | ahead, PENALTY, 0.0)


def matrices_kernel(nodes, radial, stiffness_ref, wide_ref, narrow_ref):
    order = stiffness_ref.shape[1]
    rows = nodes * radial
    theta = line_matrix(stiffness_ref[0], order, nodes, rows, radial)
    axial = line_matrix(stiffness_ref[1], order, nodes, rows, radial)
    select = one_hot(rows, order, lambda row: row % radial)
    spread = jnp.dot(select, stiffness_ref[2], precision=lax.Precision.HIGHEST)
    full = lax.dot_general(
        spread, select, (((1,), (1,)), ((), ())), precision=lax.Precision.HIGHEST
    )
    row = lax.broadcasted_iota(jnp.int32, (rows, rows), 0)
    column = lax.broadcasted_iota(jnp.int32, (rows, rows), 1)
    axial = axial + jnp.where(row // radial == column // radial, full, 0.0)
    edge = (row % radial == 0) | (row % radial == radial - 1)
    axial = axial + jnp.where((row == column) & edge, PENALTY, 0.0)
    for index, matrix in enumerate((theta, axial)):
        upper, lower = split_bf16(matrix)
        wide_ref[index, :, :rows] = upper
        wide_ref[index, :, rows:] = upper
        narrow_ref[index] = lower


def volume_matrices(stiffness, nodes, radial):
    rows = nodes * radial
    return call(
        functools.partial(matrices_kernel, nodes, radial),
        (
            jax.ShapeDtypeStruct((2, rows, 2 * rows), BF16),
            jax.ShapeDtypeStruct((2, rows, rows), BF16),
        ),
        0,
        1,
        name="volume_matrices",
    )(stiffness)


def bulk_kernel(x_ref, mass_ref, wide_ref, narrow_ref, y_ref):
    n_theta, n_axial, radial, lanes = x_ref.shape

    def product(index, values):
        upper, lower = split_bf16(values)
        both = jnp.concatenate([upper, lower], axis=0)
        return jnp.dot(wide_ref[index], both, preferred_element_type=F32) + jnp.dot(
            narrow_ref[index], upper, preferred_element_type=F32
        )

    def along_theta(z, carry):
        values = x_ref[:, z].reshape(n_theta * radial, lanes)
        y_ref[:, z] = product(0, values).reshape(n_theta, radial, lanes)
        return carry

    def along_axial(a, carry):
        values = x_ref[a].reshape(n_axial * radial, lanes)
        total = product(1, values).reshape(n_axial, radial, lanes)
        mass = mass_ref[a]
        old = y_ref[a] + total
        x = x_ref[a]
        y_ref[a, :, :, :HALF] = old[:, :, :HALF] + mass * x[:, :, :HALF]
        y_ref[a, :, :, HALF:] = old[:, :, HALF:] + mass * x[:, :, HALF:]
        return carry

    lax.fori_loop(0, n_axial, along_theta, 0, unroll=2)
    lax.fori_loop(0, n_theta, along_axial, 0, unroll=2)


def volume_bulk(x, mass, wide, narrow):
    rows = x.shape[1] * x.shape[2]
    return call(
        bulk_kernel,
        shape(*x.shape),
        0,
        4,
        flops=2 * 2 * 3 * x.size * rows,
        bytes_accessed=16 * x.size,
        name="volume_bulk",
    )(x, mass, wide, narrow)


def pair_sums(left, right):
    left_real, left_imag = left[..., :HALF], left[..., HALF:]
    right_real, right_imag = right[..., :HALF], right[..., HALF:]
    return (
        jnp.sum(left_real * right_real + left_imag * right_imag, axis=0),
        jnp.sum(left_real * right_imag - left_imag * right_real, axis=0),
    )


def square_sums(values):
    squares = values * values
    return jnp.sum(squares[..., :HALF] + squares[..., HALF:], axis=0)


def finish_row(a, bulk, s_ref, before_ref, beyond_ref, axial_before_ref, axial_beyond_ref, n_theta):
    n_axial, radial, lanes = bulk.shape
    if isinstance(a, int) and a == 0:
        bulk = bulk - before_ref[...]
    if isinstance(a, int) and a == n_theta - 1:
        bulk = bulk - beyond_ref[...]
    outer = lax.broadcasted_iota(jnp.int32, (radial, lanes), 0) == radial - 1
    tiles = []
    for z in range(n_axial):
        tile = bulk[z]
        if z == 0:
            tile = tile - axial_before_ref[a]
        if z == n_axial - 1:
            tile = tile - axial_beyond_ref[a]
        face = jnp.broadcast_to(s_ref[a // 2, z : z + 1, :], (radial, lanes))
        tiles.append(tile + jnp.where(outer, face, 0.0))
    return jnp.stack(tiles)


def over_rows(n_theta, body):
    body(0)
    lax.fori_loop(1, n_theta - 1, lambda a, carry: (body(a), carry)[1], 0)
    body(n_theta - 1)


def put_faces(u_ref, face_ref):
    radial = u_ref.shape[2]
    for pair in range(face_ref.shape[0]):
        face_ref[pair] = 0.5 * (
            u_ref[2 * pair, :, radial - 1, :] + u_ref[2 * pair + 1, :, radial - 1, :]
        )


def finish_first_kernel(
    bulk_ref, s_ref, before_ref, beyond_ref, ax_before_ref, ax_beyond_ref, rhs_ref,
    u_ref, face_ref, sums_ref,
):
    n_theta = bulk_ref.shape[0]
    sums_ref[...] = jnp.zeros_like(sums_ref)

    def body(a):
        image = finish_row(
            a, bulk_ref[a], s_ref, before_ref, beyond_ref, ax_before_ref, ax_beyond_ref, n_theta
        )
        u = rhs_ref[a] - image
        u_ref[a] = u
        sums_ref[0] += square_sums(u)

    over_rows(n_theta, body)
    put_faces(u_ref, face_ref)


def finish_second_kernel(
    bulk_ref, s_ref, before_ref, beyond_ref, ax_before_ref, ax_beyond_ref, u0_ref,
    u_ref, face_ref, sums_ref,
):
    n_theta = bulk_ref.shape[0]
    sums_ref[...] = jnp.zeros_like(sums_ref)

    def body(a):
        u = finish_row(
            a, bulk_ref[a], s_ref, before_ref, beyond_ref, ax_before_ref, ax_beyond_ref, n_theta
        )
        u_ref[a] = u
        real, imag = pair_sums(u0_ref[a], u)
        sums_ref[0] += real
        sums_ref[1] += imag
        sums_ref[2] += square_sums(u)

    over_rows(n_theta, body)
    put_faces(u_ref, face_ref)


def finish_third_kernel(
    bulk_ref, s_ref, before_ref, beyond_ref, ax_before_ref, ax_beyond_ref, u0_ref, u1_ref, sums_ref
):
    n_theta = bulk_ref.shape[0]
    sums_ref[...] = jnp.zeros_like(sums_ref)

    def body(a):
        u = finish_row(
            a, bulk_ref[a], s_ref, before_ref, beyond_ref, ax_before_ref, ax_beyond_ref, n_theta
        )
        real, imag = pair_sums(u0_ref[a], u)
        sums_ref[0] += real
        sums_ref[1] += imag
        real, imag = pair_sums(u1_ref[a], u)
        sums_ref[2] += real
        sums_ref[3] += imag
        sums_ref[4] += square_sums(u)

    over_rows(n_theta, body)


def finish(kernel, n_sums, with_result, bulk, s, halos, *others):
    n_theta, n_axial, radial, lanes = bulk.shape
    outs = (shape(n_sums, radial, HALF),)
    if with_result:
        outs = (shape(*bulk.shape), shape(n_theta // 2, n_axial, lanes)) + outs
    return call(
        kernel,
        outs,
        0,
        6 + len(others),
        flops=20 * bulk.size,
        bytes_accessed=4 * bulk.size * (2 + len(others)),
        name=kernel.__name__,
    )(bulk, s, *halos, *others)


def bem_kernel(sign, chunk, place_ref, m_ref, s_ref, add_ref, out_ref, upper_ref, lower_ref, p_ref):
    pairs, n_axial, lanes = add_ref.shape
    slabs = out_ref.shape[0]
    axial_all = p_ref.shape[1]
    columns = s_ref.shape[0]
    rows = m_ref.shape[1]
    for piece in range(columns // chunk):
        values = s_ref[piece * chunk : (piece + 1) * chunk, :]
        upper, lower = split_bf16(values)
        at = pl.ds(pl.multiple_of(place_ref[1 + piece], chunk), chunk)
        upper_ref[at, :] = upper
        lower_ref[at, :] = lower

    step = 2 * axial_all if axial_all < 128 else axial_all

    def block(index, carry):
        at = pl.ds(pl.multiple_of(index * step, step), step)
        real = m_ref[0, at, :]
        imag = m_ref[1, at, :]
        by_real = jnp.dot(real, upper_ref[...], preferred_element_type=F32) + jnp.dot(
            real, lower_ref[...], preferred_element_type=F32
        )
        by_imag = jnp.dot(imag, upper_ref[...], preferred_element_type=F32) + jnp.dot(
            imag, lower_ref[...], preferred_element_type=F32
        )
        here = pl.ds(index * (step // axial_all), step // axial_all)
        three = (step // axial_all, axial_all, HALF)
        p_ref[here, :, :HALF] = sign * (by_real[:, :HALF] - by_imag[:, HALF:]).reshape(three)
        p_ref[here, :, HALF:] = sign * (by_real[:, HALF:] + by_imag[:, :HALF]).reshape(three)
        return carry

    lax.fori_loop(0, rows // step, block, 0)
    slab = place_ref[0]
    own = pl.ds(pl.multiple_of(slab * n_axial, n_axial), n_axial)
    p_ref[:, own, :] += add_ref[...]
    for shift in range(slabs):
        target = lax.rem(slab + shift, slabs)
        for turn in range(pairs // slabs):
            out_ref[shift, turn * axial_all : (turn + 1) * axial_all, :] = p_ref[
                target + turn * slabs
            ]
        there = pl.ds(pl.multiple_of(target * n_axial, n_axial), n_axial)
        out_ref[shift, chunk:, :] = p_ref[:, there, :].reshape(pairs * n_axial, lanes)


def bem_partial(sign, place, matrix, gathered, add, slabs):
    pairs, n_axial, lanes = add.shape
    axial_all = n_axial * slabs
    chunk = pairs // slabs * axial_all
    rows, columns = matrix.shape[1:]
    return call(
        functools.partial(bem_kernel, sign, chunk),
        shape(slabs, 2 * chunk, lanes),
        1,
        3,
        scratch=[
            pltpu.VMEM((columns, lanes), BF16),
            pltpu.VMEM((columns, lanes), BF16),
            pltpu.VMEM((pairs, axial_all, lanes), F32),
        ],
        flops=2 * 4 * rows * columns * lanes,
        bytes_accessed=4 * rows * columns + 4 * columns * lanes + 8 * chunk * slabs * lanes,
        name="bem_partial",
    )(place, matrix, gathered, add)


def surface_sums(u0, u1, u2):
    sums = (square_sums(u0),) + pair_sums(u0, u1) + (square_sums(u1),)
    return sums + pair_sums(u0, u2) + pair_sums(u1, u2) + (square_sums(u2),)


def gram_kernel(first_ref, second_ref, third_ref, s0_ref, s1_ref, s2_ref, out_ref):
    volume = (
        [first_ref[0]]
        + [second_ref[row] for row in range(3)]
        + [third_ref[row] for row in range(5)]
    )
    surface = surface_sums(s0_ref[...], s1_ref[...], s2_ref[...])
    for row, (one, two) in enumerate(zip(volume, surface)):
        out_ref[row : row + 1, :] = jnp.sum(one, axis=0, keepdims=True) + jnp.sum(
            two, axis=0, keepdims=True
        )


def local_gram(first, second, third, s0, s1, s2):
    tiles = [values.reshape(-1, 8, LANES) for values in (s0, s1, s2)]
    return call(gram_kernel, shape(9, HALF), 0, 6, name="local_gram")(
        first, second, third, *tiles
    )


def times(left, right):
    return (
        left[0] * right[0] - left[1] * right[1],
        left[0] * right[1] + left[1] * right[0],
    )


def conj_times(left, right):
    return (
        left[0] * right[0] + left[1] * right[1],
        left[0] * right[1] - left[1] * right[0],
    )


def square(value):
    return value[0] * value[0] + value[1] * value[1]


def coefficients(rows):
    g00, g11, g22 = rows[0], rows[3], rows[8]
    g01, g02, g12 = (rows[1], rows[2]), (rows[4], rows[5]), (rows[6], rows[7])
    beta_sq = g00 + EPSILON
    beta = jnp.sqrt(beta_sq)
    h00 = (g01[0] / beta_sq, g01[1] / beta_sq)
    h00_sq = square(h00)
    cross = conj_times(h00, g01)[0]
    rest = jnp.maximum(g11 - 2.0 * cross + h00_sq * g00, 0.0) / beta_sq
    h10_sq = rest + EPSILON
    h10 = jnp.sqrt(h10_sq)
    over_first = 1.0 / (beta_sq * h10)
    over_second = 1.0 / (beta_sq * h10_sq)
    h00_g01 = times(h00, g01)
    h01 = tuple((g02[k] - h00_g01[k]) * over_first for k in (0, 1))
    conj_g02 = conj_times(h00, g02)
    h11 = tuple(
        (g12[k] - h00[k] * g11 - conj_g02[k] + h00_sq * g01[k]) * over_second for k in (0, 1)
    )
    image_sq = (g22 - 2.0 * conj_times(h00, g12)[0] + h00_sq * g11) * over_second
    first_sq, second_sq = g00 / beta_sq, rest / h10_sq
    overlap = (h00[0] * EPSILON * over_first, h00[1] * EPSILON * over_first)
    mixed = conj_times(h01, times(h11, overlap))[0]
    bottom_sq = (
        jnp.maximum(
            image_sq
            - (2.0 - first_sq) * square(h01)
            - (2.0 - second_sq) * square(h11)
            + 2.0 * mixed,
            0.0,
        )
        + EPSILON
    )
    rho = jnp.sqrt(h00_sq + h10_sq)
    cos = (h00[0] / rho, h00[1] / rho)
    sine = h10 / rho
    top = conj_times(cos, h01)
    top = tuple(top[k] + sine * h11[k] for k in (0, 1))
    turn = times(cos, h11)
    turn = tuple(turn[k] - sine * h01[k] for k in (0, 1))
    lower = -sine * beta / (square(turn) + bottom_sq)
    one = (turn[0] * lower, -turn[1] * lower)
    top_one = times(top, one)
    zero = ((cos[0] * beta - top_one[0]) / rho, (-cos[1] * beta - top_one[1]) / rho)
    of_second = (one[0] / (beta * h10), one[1] / (beta * h10))
    back = times(of_second, h00)
    of_first = (zero[0] / beta - back[0], zero[1] / beta - back[1])
    return of_first, of_second


def combine(first, second, guess, u0, u1):
    u0_real, u0_imag = u0[..., :HALF], u0[..., HALF:]
    u1_real, u1_imag = u1[..., :HALF], u1[..., HALF:]
    real = guess[..., :HALF] + (first[0] * u0_real - first[1] * u0_imag)
    imag = guess[..., HALF:] + (first[0] * u0_imag + first[1] * u0_real)
    real = real + (second[0] * u1_real - second[1] * u1_imag)
    imag = imag + (second[0] * u1_imag + second[1] * u1_real)
    return real, imag


def solution_kernel(
    gram_ref, x_ref, u0_ref, u1_ref, s_ref, s0_ref, s1_ref, volume_ref, surface_ref
):
    rows = [jnp.sum(gram_ref[row], axis=0, keepdims=True) for row in range(9)]
    first, second = coefficients(rows)
    real, imag = combine(first, second, s_ref[...], s0_ref[...], s1_ref[...])
    surface_ref[..., :HALF] = real
    surface_ref[..., HALF:] = imag

    def body(a, carry):
        real, imag = combine(first, second, x_ref[a], u0_ref[a], u1_ref[a])
        volume_ref[a, :, :, :HALF] = real
        volume_ref[a, :, :, HALF:] = imag
        return carry

    lax.fori_loop(0, x_ref.shape[0], body, 0)


def final_solution(gram_all, x, u0, u1, s, s0, s1):
    return call(
        solution_kernel,
        (shape(*x.shape), shape(*s.shape)),
        0,
        7,
        flops=10 * x.size,
        bytes_accessed=16 * x.size,
        name="final_solution",
    )(gram_all, x, u0, u1, s, s0, s1)


def power_scale(bound):
    return 2.0 ** math.floor(math.log2(60000.0 / bound))


def to_wire(values, scale):
    return (values * scale).astype(WIRE)


def from_wire(values, scale):
    return values.astype(F32) * (1.0 / scale)


def shift_perm(peers, shift):
    return [(i, (i + shift) % peers) for i in range(peers)]


def slab_exchange(messages):
    slabs = lax.axis_size("slab")
    return [
        lax.ppermute(messages[shift], "slab", shift_perm(slabs, shift))
        for shift in range(1, slabs)
    ]


def axial_halos(received_first, received_last, scale, tail):
    slab, slabs = lax.axis_index("slab"), lax.axis_size("slab")
    before = from_wire(received_first[-tail:], scale) * (slab > 0).astype(F32)
    beyond = from_wire(received_last[-tail:], scale) * (slab < slabs - 1).astype(F32)
    return before, beyond


def sector_gather(values, scale, layers, layer_scale):
    sectors = lax.axis_size("sector")
    chips = sectors // 2
    core = lax.rem(lax.axis_index("sector"), 2)
    chunk = values.shape[0]
    tail = layers[0].shape[0]
    own = to_wire(values, scale)
    first, last = (to_wire(layer, layer_scale) for layer in layers)
    sibling = [(i, i ^ 1) for i in range(sectors)]

    def up_down(shift):
        pairs = []
        for i in range(sectors):
            chip, c = i // 2, i % 2
            pairs.append((i, (chip + (shift if c == 0 else -shift)) % chips * 2 + c))
        return pairs

    half = [(i, (i + sectors // 2) % sectors) for i in range(sectors)]
    from_half = lax.ppermute(own, "sector", half)
    beside = lax.ppermute(jnp.concatenate([own, first, last]), "sector", sibling)
    beside_first, beside_last = beside[chunk : chunk + tail], beside[chunk + tail :]
    far = jnp.where(core == 0, beside_last, beside_first)
    near = jnp.where(core == 0, beside_first, beside_last)
    both = jnp.concatenate([own, beside[:chunk]])
    arrived = []
    for shift in range(1, chips // 2):
        message = jnp.concatenate([both, far]) if shift == 1 else both
        arrived.append(lax.ppermute(message, "sector", up_down(shift)))
    far_halo = arrived[0][2 * chunk :]
    arrived = [message[: 2 * chunk] for message in arrived]
    here = jnp.concatenate(arrived + [from_half])
    there = lax.ppermute(here, "sector", sibling)
    gathered = from_wire(jnp.concatenate([both, here, there]), scale)
    before = from_wire(jnp.where(core == 0, far_halo, near), layer_scale)
    beyond = from_wire(jnp.where(core == 0, near, far_halo), layer_scale)
    return gathered, (before, beyond)


def gather_places(chunk):
    sectors = lax.axis_size("sector")
    chips = sectors // 2
    sector = lax.axis_index("sector")
    chip, core = sector // 2, lax.rem(sector, 2)

    def place(chip_shift, other):
        source = lax.rem(chip + chip_shift + 2 * chips, chips)
        return (2 * source + jnp.where(other, 1 - core, core)) * chunk

    up = jnp.where(core == 0, -1, 1)
    places = [lax.axis_index("slab"), place(0, False), place(0, True)]
    for mirrored in (False, True):
        sign = -1 if mirrored else 1
        for shift in range(1, chips // 2):
            places.append(place(sign * up * shift, mirrored))
            places.append(place(sign * up * shift, not mirrored))
        places.append(place(chips // 2, mirrored))
    return jnp.stack([jnp.asarray(value, jnp.int32) for value in places])


def edge_rows(volume):
    lanes = volume.shape[-1]
    theta = (volume[0].reshape(-1, lanes), volume[-1].reshape(-1, lanes))
    axial = (volume[:, 0].reshape(-1, lanes), volume[:, -1].reshape(-1, lanes))
    return theta, axial


def scatter_sum(parts, scale, axial, layer_scale):
    slabs = parts.shape[0]
    rows = parts.shape[1]
    messages = [None]
    for shift in range(1, slabs):
        message = to_wire(parts[shift], scale)
        if axial is not None and shift == 1:
            message = jnp.concatenate([message, to_wire(axial[1], layer_scale)])
        if axial is not None and shift == slabs - 1:
            message = jnp.concatenate([message, to_wire(axial[0], layer_scale)])
        messages.append(message)
    received = slab_exchange(messages)
    total = parts[0]
    for message in received:
        total = total + from_wire(message[:rows], scale)
    halos = None
    if axial is not None:
        halos = axial_halos(received[0], received[-1], layer_scale, axial[0].shape[0])
    return total, halos


def per_device(
    volume_rhs, surface_rhs, volume_guess, surface_guess, bem_matrix, stiffness, mass_shift
):
    slabs, sectors = lax.axis_size("slab"), lax.axis_size("sector")
    slab = lax.axis_index("slab")
    n_theta, n_axial, radial, lanes = volume_guess.shape
    pairs = surface_guess.shape[0]
    axial_all = n_axial * slabs
    turns = pairs // slabs
    chunk = turns * axial_all
    unknowns = sectors * pairs * axial_all

    gain = 8.0 * math.sqrt(unknowns)
    stiff = 3 * (3.0 + 7 * 1.05) + 6 + 3.0
    surface_0 = 6.0
    volume_0 = 6.0
    surface_1 = gain * surface_0 + 12.0
    volume_1 = 80.0 + stiff * volume_0 + surface_0
    surface_2 = gain * surface_1 + volume_1
    volume_2 = stiff * volume_1 + surface_1
    scale_s = [power_scale(bound) for bound in (surface_0, surface_1, surface_2)]
    scale_v = [power_scale(bound) for bound in (volume_0, volume_1, volume_2)]
    scale_p = [
        power_scale(gain / slabs * surface_0 + 12.0),
        power_scale(gain / slabs * surface_1 + volume_1),
        power_scale(gain / slabs * surface_2 + volume_2),
    ]

    place = gather_places(chunk)
    wide, narrow = volume_matrices(stiffness, n_theta, radial)
    mass = jnp.broadcast_to(mass_shift[..., None], mass_shift.shape + (HALF,))

    def layers(rows, count):
        return rows.reshape(count, radial, lanes)

    def shaped(theta, axial):
        return (
            layers(theta[0], n_axial),
            layers(theta[1], n_axial),
            layers(axial[0], n_theta),
            layers(axial[1], n_theta),
        )

    theta_edges, axial_edges = edge_rows(volume_guess)
    by_owner = surface_guess.reshape(turns, slabs, n_axial, lanes)
    messages = [None]
    for shift in range(1, slabs):
        share = lax.dynamic_index_in_dim(
            by_owner, lax.rem(slab + shift, slabs), axis=1, keepdims=False
        ).reshape(turns * n_axial, lanes)
        message = to_wire(share, scale_s[0])
        if shift == 1:
            message = jnp.concatenate([message, to_wire(axial_edges[1], scale_v[0])])
        if shift == slabs - 1:
            message = jnp.concatenate([message, to_wire(axial_edges[0], scale_v[0])])
        messages.append(message)
    received = slab_exchange(messages)
    axial = axial_halos(received[0], received[-1], scale_v[0], n_theta * radial)
    share = lax.dynamic_index_in_dim(by_owner, slab, axis=1, keepdims=False)
    parts = [share] + [
        from_wire(message[: turns * n_axial], scale_s[0]).reshape(turns, n_axial, lanes)
        for message in received
    ]
    columns = jnp.concatenate(
        [
            lax.dynamic_index_in_dim(
                jnp.stack(parts), lax.rem(slab - owner + slabs, slabs), axis=0, keepdims=False
            )
            for owner in range(slabs)
        ],
        axis=1,
    ).reshape(chunk, lanes)

    bulk = volume_bulk(volume_guess, mass, wide, narrow)
    gathered, theta = sector_gather(columns, scale_s[0], theta_edges, scale_v[0])
    outer = volume_guess[:, :, radial - 1, :].reshape(pairs, 2, n_axial, lanes)
    add = surface_rhs + 0.5 * (outer[:, 0] + outer[:, 1])
    u0, face0, first = finish(
        finish_first_kernel, 1, True, bulk, surface_guess, shaped(theta, axial), volume_rhs
    )
    theta_edges, axial_edges = edge_rows(u0)
    partial = bem_partial(-1.0, place, bem_matrix, gathered, add, slabs)
    total, axial = scatter_sum(partial, scale_p[0], axial_edges, scale_v[1])
    s0_owner, s0 = total[:chunk], total[chunk:].reshape(pairs, n_axial, lanes)

    bulk = volume_bulk(u0, mass, wide, narrow)
    gathered, theta = sector_gather(s0_owner, scale_s[1], theta_edges, scale_v[1])
    u1, face1, second = finish(
        finish_second_kernel, 3, True, bulk, s0, shaped(theta, axial), u0
    )
    theta_edges, axial_edges = edge_rows(u1)
    partial = bem_partial(1.0, place, bem_matrix, gathered, -face0, slabs)
    total, axial = scatter_sum(partial, scale_p[1], axial_edges, scale_v[2])
    s1_owner, s1 = total[:chunk], total[chunk:].reshape(pairs, n_axial, lanes)

    bulk = volume_bulk(u1, mass, wide, narrow)
    gathered, theta = sector_gather(s1_owner, scale_s[2], theta_edges, scale_v[2])
    (third,) = finish(
        finish_third_kernel, 5, False, bulk, s1, shaped(theta, axial), u0, u1
    )
    partial = bem_partial(1.0, place, bem_matrix, gathered, -face1, slabs)
    total, _ = scatter_sum(partial[:, :chunk], scale_p[2], None, 1.0)

    gram = local_gram(first, second, third, s0_owner, s1_owner, total)
    devices = sectors * slabs
    copies = jnp.broadcast_to(gram.reshape(1, 1, -1), (devices, 1, gram.size))
    gram_all = lax.all_to_all(copies, ("sector", "slab"), split_axis=0, concat_axis=0, tiled=True)
    gram_all = jnp.swapaxes(gram_all.reshape(devices, 9, HALF), 0, 1)
    return final_solution(gram_all, volume_guess, u0, u1, surface_guess, s0, s1)


def solution(mesh):
    return jax.shard_map(
        per_device,
        mesh=mesh,
        in_specs=(
            P("sector", "slab", None, None),
            P("sector", "slab", None),
            P("sector", "slab", None, None),
            P("sector", "slab", None),
            P(None, "sector", "slab"),
            P(),
            P("sector", "slab", None),
        ),
        out_specs=(P("sector", "slab", None, None), P("sector", "slab", None)),
        check_vma=False,
    )
```

```python
import functools
import math

import jax
import jax.numpy as jnp
from jax import lax
from jax.experimental import pallas as pl
from jax.experimental.pallas import tpu as pltpu
from jax.sharding import PartitionSpec as P

PENALTY = 1.0
EPSILON = 1e-06
F32 = jnp.float32
BF16 = jnp.bfloat16
WIRE = jnp.float16
LANES = 256
HALF = 128
VMEM_LIMIT = 8 * 1024 * 1024
WHOLE = pl.BlockSpec(memory_space=pltpu.VMEM)
SCALARS = pl.BlockSpec(memory_space=pltpu.SMEM)
ANYWHERE = pl.BlockSpec(memory_space=pl.ANY)


def call(
    kernel, out_shape, n_scalars, n_arrays, scratch=(), flops=0, bytes_accessed=0, name=None,
    after=(), out_specs=None, aliases=None,
):
    n_read = n_scalars + n_arrays

    def body(*refs):
        kernel(*refs[:n_read], *refs[n_read + len(after) :])

    called = pl.pallas_call(
        body,
        out_shape=out_shape,
        in_specs=[SCALARS] * n_scalars + [WHOLE] * n_arrays + [ANYWHERE] * len(after),
        out_specs=out_specs or jax.tree.map(lambda _: WHOLE, out_shape),
        scratch_shapes=list(scratch),
        input_output_aliases=aliases or {},
        compiler_params=pltpu.CompilerParams(vmem_limit_bytes=VMEM_LIMIT),
        cost_estimate=pl.CostEstimate(
            flops=flops, bytes_accessed=bytes_accessed, transcendentals=0
        ),
        name=name,
    )
    return lambda *args: called(*args, *after)


def shape(*dims):
    return jax.ShapeDtypeStruct(dims, F32)


def split_bf16(values):
    upper = values.astype(BF16)
    lower = (values - upper.astype(F32)).astype(BF16)
    return upper, lower


def one_hot(rows, columns, pick):
    row = lax.broadcasted_iota(jnp.int32, (rows, columns), 0)
    column = lax.broadcasted_iota(jnp.int32, (rows, columns), 1)
    return (pick(row) == column).astype(F32)


def line_matrix(stiffness, order, nodes, rows, fast):
    select = one_hot(rows, order, lambda row: (row // fast) % order)
    spread = jnp.dot(select, stiffness, precision=lax.Precision.HIGHEST)
    full = lax.dot_general(
        spread, select, (((1,), (1,)), ((), ())), precision=lax.Precision.HIGHEST
    )
    row = lax.broadcasted_iota(jnp.int32, (rows, rows), 0)
    column = lax.broadcasted_iota(jnp.int32, (rows, rows), 1)
    row_node, column_node = row // fast, column // fast
    same_fast = row % fast == column % fast
    same_element = (row_node // order == column_node // order) & same_fast
    block = jnp.where(same_element, full, 0.0)
    edge = (row_node % order == 0) | (row_node % order == order - 1)
    block = block + jnp.where((row == column) & edge, PENALTY, 0.0)
    back = (row_node % order == 0) & (column_node == row_node - 1) & same_fast
    ahead = (row_node % order == order - 1) & (column_node == row_node + 1) & same_fast
    return block - jnp.where(back | ahead, PENALTY, 0.0)


def matrices_kernel(nodes, radial, stiffness_ref, wide_ref, narrow_ref):
    order = stiffness_ref.shape[1]
    rows = nodes * radial
    theta = line_matrix(stiffness_ref[0], order, nodes, rows, radial)
    axial = line_matrix(stiffness_ref[1], order, nodes, rows, radial)
    select = one_hot(rows, order, lambda row: row % radial)
    spread = jnp.dot(select, stiffness_ref[2], precision=lax.Precision.HIGHEST)
    full = lax.dot_general(
        spread, select, (((1,), (1,)), ((), ())), precision=lax.Precision.HIGHEST
    )
    row = lax.broadcasted_iota(jnp.int32, (rows, rows), 0)
    column = lax.broadcasted_iota(jnp.int32, (rows, rows), 1)
    axial = axial + jnp.where(row // radial == column // radial, full, 0.0)
    edge = (row % radial == 0) | (row % radial == radial - 1)
    axial = axial + jnp.where((row == column) & edge, PENALTY, 0.0)
    for index, matrix in enumerate((theta, axial)):
        upper, lower = split_bf16(matrix)
        wide_ref[index, :, :rows] = upper
        wide_ref[index, :, rows:] = upper
        narrow_ref[index] = lower


def volume_matrices(stiffness, nodes, radial):
    rows = nodes * radial
    return call(
        functools.partial(matrices_kernel, nodes, radial),
        (
            jax.ShapeDtypeStruct((2, rows, 2 * rows), BF16),
            jax.ShapeDtypeStruct((2, rows, rows), BF16),
        ),
        0,
        1,
        name="volume_matrices",
    )(stiffness)


def bulk_kernel(x_ref, mass_ref, wide_ref, narrow_ref, y_ref, *face_refs):
    n_theta, n_axial, radial, lanes = x_ref.shape

    def product(index, values):
        upper, lower = split_bf16(values)
        both = jnp.concatenate([upper, lower], axis=0)
        return jnp.dot(wide_ref[index], both, preferred_element_type=F32) + jnp.dot(
            narrow_ref[index], upper, preferred_element_type=F32
        )

    def along_theta(z, carry):
        values = x_ref[:, z].reshape(n_theta * radial, lanes)
        y_ref[:, z] = product(0, values).reshape(n_theta, radial, lanes)
        return carry

    def along_axial(a, carry):
        values = x_ref[a].reshape(n_axial * radial, lanes)
        total = product(1, values).reshape(n_axial, radial, lanes)
        mass = mass_ref[a]
        old = y_ref[a] + total
        x = x_ref[a]
        y_ref[a, :, :, :HALF] = old[:, :, :HALF] + mass * x[:, :, :HALF]
        y_ref[a, :, :, HALF:] = old[:, :, HALF:] + mass * x[:, :, HALF:]
        return carry

    lax.fori_loop(0, n_axial, along_theta, 0, unroll=2)
    lax.fori_loop(0, n_theta, along_axial, 0, unroll=2)
    for face_ref in face_refs:
        put_faces(x_ref, face_ref)


def volume_bulk(x, mass, wide, narrow, with_face=False, after=()):
    n_theta, n_axial, radial, lanes = x.shape
    outs = (shape(*x.shape),)
    if with_face:
        outs = outs + (shape(n_theta // 2, n_axial, lanes),)
    return call(
        bulk_kernel,
        outs,
        0,
        4,
        flops=2 * 2 * 3 * x.size * n_axial * radial,
        bytes_accessed=16 * x.size,
        name="volume_bulk",
        after=after,
    )(x, mass, wide, narrow)


def pair_sums(left, right):
    left_real, left_imag = left[..., :HALF], left[..., HALF:]
    right_real, right_imag = right[..., :HALF], right[..., HALF:]
    return (
        jnp.sum(left_real * right_real + left_imag * right_imag, axis=0),
        jnp.sum(left_real * right_imag - left_imag * right_real, axis=0),
    )


def square_sums(values):
    squares = values * values
    return jnp.sum(squares[..., :HALF] + squares[..., HALF:], axis=0)


def finish_row(a, bulk, s_ref, before_ref, beyond_ref, axial_before_ref, axial_beyond_ref, n_theta):
    n_axial, radial, lanes = bulk.shape
    if isinstance(a, int) and a == 0:
        bulk = bulk - before_ref[...]
    if isinstance(a, int) and a == n_theta - 1:
        bulk = bulk - beyond_ref[...]
    outer = lax.broadcasted_iota(jnp.int32, (radial, lanes), 0) == radial - 1
    tiles = []
    for z in range(n_axial):
        tile = bulk[z]
        if z == 0:
            tile = tile - axial_before_ref[a]
        if z == n_axial - 1:
            tile = tile - axial_beyond_ref[a]
        face = jnp.broadcast_to(s_ref[a // 2, z : z + 1, :], (radial, lanes))
        tiles.append(tile + jnp.where(outer, face, 0.0))
    return jnp.stack(tiles)


def over_rows(n_theta, body):
    body(0)
    lax.fori_loop(1, n_theta - 1, lambda a, carry: (body(a), carry)[1], 0)
    body(n_theta - 1)


def put_faces(u_ref, face_ref):
    radial = u_ref.shape[2]
    for pair in range(face_ref.shape[0]):
        face_ref[pair] = 0.5 * (
            u_ref[2 * pair, :, radial - 1, :] + u_ref[2 * pair + 1, :, radial - 1, :]
        )


def finish_first_kernel(
    bulk_ref, s_ref, before_ref, beyond_ref, ax_before_ref, ax_beyond_ref, rhs_ref,
    u_ref, face_ref, sums_ref,
):
    n_theta = bulk_ref.shape[0]
    sums_ref[...] = jnp.zeros_like(sums_ref)

    def body(a):
        image = finish_row(
            a, bulk_ref[a], s_ref, before_ref, beyond_ref, ax_before_ref, ax_beyond_ref, n_theta
        )
        u = rhs_ref[a] - image
        u_ref[a] = u
        sums_ref[0] += square_sums(u)

    over_rows(n_theta, body)
    put_faces(u_ref, face_ref)


def finish_second_kernel(
    bulk_ref, s_ref, before_ref, beyond_ref, ax_before_ref, ax_beyond_ref, u0_ref,
    u_ref, face_ref, sums_ref,
):
    n_theta = bulk_ref.shape[0]
    sums_ref[...] = jnp.zeros_like(sums_ref)

    def body(a):
        u = finish_row(
            a, bulk_ref[a], s_ref, before_ref, beyond_ref, ax_before_ref, ax_beyond_ref, n_theta
        )
        u_ref[a] = u
        real, imag = pair_sums(u0_ref[a], u)
        sums_ref[0] += real
        sums_ref[1] += imag
        sums_ref[2] += square_sums(u)

    over_rows(n_theta, body)
    put_faces(u_ref, face_ref)


def finish_third_kernel(
    bulk_ref, s_ref, before_ref, beyond_ref, ax_before_ref, ax_beyond_ref, u0_ref, u1_ref,
    x_ref, sums_ref, *passed_refs,
):
    n_theta = bulk_ref.shape[0]
    sums_ref[...] = jnp.zeros_like(sums_ref)

    def body(a):
        u = finish_row(
            a, bulk_ref[a], s_ref, before_ref, beyond_ref, ax_before_ref, ax_beyond_ref, n_theta
        )
        real, imag = pair_sums(u0_ref[a], u)
        sums_ref[0] += real
        sums_ref[1] += imag
        real, imag = pair_sums(u1_ref[a], u)
        sums_ref[2] += real
        sums_ref[3] += imag
        sums_ref[4] += square_sums(u)

    over_rows(n_theta, body)


def finish(kernel, n_sums, with_result, bulk, s, halos, *others, after=()):
    n_theta, n_axial, radial, lanes = bulk.shape
    outs = (shape(n_sums, radial, HALF),)
    aliases = {}
    if with_result:
        outs = (shape(*bulk.shape), shape(n_theta // 2, n_axial, lanes)) + outs
    else:
        outs = outs + (shape(*bulk.shape),) * len(others)
        aliases = {6 + index: 1 + index for index in range(len(others))}
    return call(
        kernel,
        outs,
        0,
        6 + len(others),
        flops=20 * bulk.size,
        bytes_accessed=4 * bulk.size * (2 + len(others)),
        name=kernel.__name__,
        after=after,
        aliases=aliases,
    )(bulk, s, *halos, *others)


def bem_kernel(sign, behind, place_ref, m_ref, face_ref, *rest):
    n_pieces = m_ref.shape[2] // (out_chunk := rest[-4].shape[1] // 2)
    s_refs, rhs_refs = rest[:n_pieces], rest[n_pieces:-4]
    out_ref, upper_ref, lower_ref, p_ref = rest[-4:]
    pairs, n_axial, lanes = face_ref.shape
    slabs = out_ref.shape[0]
    axial_all = p_ref.shape[1]
    rows = m_ref.shape[1]
    slab = place_ref[0]
    turns = pairs // slabs

    def place_rows(s_ref, first, count, start):
        upper, lower = split_bf16(s_ref[first : first + count, :])
        at = pl.ds(pl.multiple_of(start, count), count)
        upper_ref[at, :] = upper
        lower_ref[at, :] = lower

    for which, s_ref in enumerate(s_refs):
        start = place_ref[1 + which]
        if not behind:
            place_rows(s_ref, 0, out_chunk, start)
            continue
        for distance in range(slabs):
            source = lax.rem(slab - distance + slabs, slabs)
            for turn in range(turns):
                place_rows(
                    s_ref,
                    (distance * turns + turn) * n_axial,
                    n_axial,
                    start + turn * axial_all + source * n_axial,
                )

    step = 2 * axial_all if axial_all < 128 else axial_all

    def block(index, carry):
        at = pl.ds(pl.multiple_of(index * step, step), step)
        real = m_ref[0, at, :]
        imag = m_ref[1, at, :]
        by_real = jnp.dot(real, upper_ref[...], preferred_element_type=F32) + jnp.dot(
            real, lower_ref[...], preferred_element_type=F32
        )
        by_imag = jnp.dot(imag, upper_ref[...], preferred_element_type=F32) + jnp.dot(
            imag, lower_ref[...], preferred_element_type=F32
        )
        here = pl.ds(index * (step // axial_all), step // axial_all)
        three = (step // axial_all, axial_all, HALF)
        p_ref[here, :, :HALF] = sign * (by_real[:, :HALF] - by_imag[:, HALF:]).reshape(three)
        p_ref[here, :, HALF:] = sign * (by_real[:, HALF:] + by_imag[:, :HALF]).reshape(three)
        return carry

    lax.fori_loop(0, rows // step, block, 0)
    own = pl.ds(pl.multiple_of(slab * n_axial, n_axial), n_axial)
    add = -sign * face_ref[...]
    for rhs_ref in rhs_refs:
        add = add + rhs_ref[...]
    p_ref[:, own, :] += add
    for shift in range(slabs):
        target = lax.rem(slab + shift, slabs)
        for turn in range(turns):
            out_ref[shift, turn * axial_all : (turn + 1) * axial_all, :] = p_ref[
                target + turn * slabs
            ]
        there = pl.ds(pl.multiple_of(target * n_axial, n_axial), n_axial)
        out_ref[shift, out_chunk:, :] = p_ref[:, there, :].reshape(out_chunk, lanes)


def bem_partial(sign, behind, place, matrix, face, gathered, *rhs, after=()):
    pairs, n_axial, lanes = face.shape
    chunk = gathered[0].shape[0]
    rows, columns = matrix.shape[1:]
    axial_all = rows // pairs
    slabs = axial_all // n_axial
    return call(
        functools.partial(bem_kernel, sign, behind),
        shape(slabs, 2 * chunk, lanes),
        1,
        2 + len(gathered) + len(rhs),
        scratch=[
            pltpu.VMEM((columns, lanes), BF16),
            pltpu.VMEM((columns, lanes), BF16),
            pltpu.VMEM((pairs, axial_all, lanes), F32),
        ],
        flops=2 * 4 * rows * columns * lanes,
        bytes_accessed=4 * rows * columns + 4 * columns * lanes + 8 * chunk * slabs * lanes,
        name="bem_partial",
        after=after,
    )(place, matrix, face, *gathered, *rhs)


def surface_sums(u0, u1, u2):
    sums = (square_sums(u0),) + pair_sums(u0, u1) + (square_sums(u1),)
    return sums + pair_sums(u0, u2) + pair_sums(u1, u2) + (square_sums(u2),)


def gram_kernel(first_ref, second_ref, third_ref, s0_ref, s1_ref, s2_ref, out_ref):
    volume = (
        [first_ref[0]]
        + [second_ref[row] for row in range(3)]
        + [third_ref[row] for row in range(5)]
    )
    surface = surface_sums(s0_ref[...], s1_ref[...], s2_ref[...])
    for row, (one, two) in enumerate(zip(volume, surface)):
        out_ref[row : row + 1, :] = jnp.sum(one, axis=0, keepdims=True) + jnp.sum(
            two, axis=0, keepdims=True
        )


def local_gram(first, second, third, s0, s1, s2):
    tiles = [values.reshape(-1, 8, LANES) for values in (s0, s1, s2)]
    return call(gram_kernel, shape(9, HALF), 0, 6, name="local_gram")(
        first, second, third, *tiles
    )


def times(left, right):
    return (
        left[0] * right[0] - left[1] * right[1],
        left[0] * right[1] + left[1] * right[0],
    )


def conj_times(left, right):
    return (
        left[0] * right[0] + left[1] * right[1],
        left[0] * right[1] - left[1] * right[0],
    )


def square(value):
    return value[0] * value[0] + value[1] * value[1]


def coefficients(rows):
    g00, g11, g22 = rows[0], rows[3], rows[8]
    g01, g02, g12 = (rows[1], rows[2]), (rows[4], rows[5]), (rows[6], rows[7])
    beta_sq = g00 + EPSILON
    beta = jnp.sqrt(beta_sq)
    h00 = (g01[0] / beta_sq, g01[1] / beta_sq)
    h00_sq = square(h00)
    cross = conj_times(h00, g01)[0]
    rest = jnp.maximum(g11 - 2.0 * cross + h00_sq * g00, 0.0) / beta_sq
    h10_sq = rest + EPSILON
    h10 = jnp.sqrt(h10_sq)
    over_first = 1.0 / (beta_sq * h10)
    over_second = 1.0 / (beta_sq * h10_sq)
    h00_g01 = times(h00, g01)
    h01 = tuple((g02[k] - h00_g01[k]) * over_first for k in (0, 1))
    conj_g02 = conj_times(h00, g02)
    h11 = tuple(
        (g12[k] - h00[k] * g11 - conj_g02[k] + h00_sq * g01[k]) * over_second for k in (0, 1)
    )
    image_sq = (g22 - 2.0 * conj_times(h00, g12)[0] + h00_sq * g11) * over_second
    first_sq, second_sq = g00 / beta_sq, rest / h10_sq
    overlap = (h00[0] * EPSILON * over_first, h00[1] * EPSILON * over_first)
    mixed = conj_times(h01, times(h11, overlap))[0]
    bottom_sq = (
        jnp.maximum(
            image_sq
            - (2.0 - first_sq) * square(h01)
            - (2.0 - second_sq) * square(h11)
            + 2.0 * mixed,
            0.0,
        )
        + EPSILON
    )
    rho = jnp.sqrt(h00_sq + h10_sq)
    cos = (h00[0] / rho, h00[1] / rho)
    sine = h10 / rho
    top = conj_times(cos, h01)
    top = tuple(top[k] + sine * h11[k] for k in (0, 1))
    turn = times(cos, h11)
    turn = tuple(turn[k] - sine * h01[k] for k in (0, 1))
    lower = -sine * beta / (square(turn) + bottom_sq)
    one = (turn[0] * lower, -turn[1] * lower)
    top_one = times(top, one)
    zero = ((cos[0] * beta - top_one[0]) / rho, (-cos[1] * beta - top_one[1]) / rho)
    of_second = (one[0] / (beta * h10), one[1] / (beta * h10))
    back = times(of_second, h00)
    of_first = (zero[0] / beta - back[0], zero[1] / beta - back[1])
    return of_first, of_second


def combine(first, second, guess, u0, u1):
    u0_real, u0_imag = u0[..., :HALF], u0[..., HALF:]
    u1_real, u1_imag = u1[..., :HALF], u1[..., HALF:]
    real = guess[..., :HALF] + (first[0] * u0_real - first[1] * u0_imag)
    imag = guess[..., HALF:] + (first[0] * u0_imag + first[1] * u0_real)
    real = real + (second[0] * u1_real - second[1] * u1_imag)
    imag = imag + (second[0] * u1_imag + second[1] * u1_real)
    return real, imag


def solution_kernel(
    gram_ref, x_ref, u0_ref, u1_ref, s_ref, s0_ref, s1_ref,
    volume_ref, surface_ref, row_ref, copied,
):
    sums = [jnp.sum(gram_ref[row], axis=0, keepdims=True) for row in range(9)]
    first, second = coefficients(sums)
    n_theta = x_ref.shape[0]

    def copy(a):
        return pltpu.make_async_copy(row_ref.at[a], volume_ref.at[a], copied.at[a])

    def body(a, carry):
        real, imag = combine(first, second, x_ref[a], u0_ref[a], u1_ref[a])
        row_ref[a, :, :, :HALF] = real
        row_ref[a, :, :, HALF:] = imag
        copy(a).start()
        return carry

    lax.fori_loop(0, n_theta, body, 0)
    real, imag = combine(first, second, s_ref[...], s0_ref[...], s1_ref[...])
    surface_ref[..., :HALF] = real
    surface_ref[..., HALF:] = imag
    lax.fori_loop(0, n_theta, lambda a, carry: (copy(a).wait(), carry)[1], 0)


def final_solution(gram_all, x, u0, u1, s, s0, s1):
    return call(
        solution_kernel,
        (shape(*x.shape), shape(*s.shape)),
        0,
        7,
        scratch=[pltpu.VMEM(x.shape, F32), pltpu.SemaphoreType.DMA((x.shape[0],))],
        flops=10 * x.size,
        bytes_accessed=16 * x.size,
        name="final_solution",
        out_specs=(ANYWHERE, WHOLE),
    )(gram_all, x, u0, u1, s, s0, s1)


def power_scale(bound):
    return 2.0 ** math.floor(math.log2(60000.0 / bound))


def to_wire(values, scale):
    return (values * scale).astype(WIRE)


def from_wire(values, scale):
    return values.astype(F32) * (1.0 / scale)


def shift_perm(peers, shift):
    return [(i, (i + shift) % peers) for i in range(peers)]


def slab_exchange(messages):
    slabs = lax.axis_size("slab")
    return [
        lax.ppermute(messages[shift], "slab", shift_perm(slabs, shift))
        for shift in range(1, slabs)
    ]


def halo_exchange(volume, scale):
    def both_ways(axis, first, last):
        peers = lax.axis_size(axis)
        before = lax.ppermute(to_wire(last, scale), axis, shift_perm(peers, 1))
        beyond = lax.ppermute(to_wire(first, scale), axis, shift_perm(peers, -1))
        return from_wire(before, scale), from_wire(beyond, scale)

    theta = both_ways("sector", volume[0], volume[-1])
    before, beyond = both_ways("slab", volume[:, 0], volume[:, -1])
    slab, slabs = lax.axis_index("slab"), lax.axis_size("slab")
    return theta + (
        jnp.where(slab > 0, before, 0.0),
        jnp.where(slab < slabs - 1, beyond, 0.0),
    )


def sector_gather(own, scale):
    sectors = lax.axis_size("sector")
    sibling = [(i, i ^ 1) for i in range(sectors)]
    shares = [own]
    for shift in range(1, sectors // 2):
        shares.append(lax.ppermute(own, "sector", shift_perm(sectors, 2 * shift)))
    gathered = []
    for share in shares:
        gathered += [share, lax.ppermute(share, "sector", sibling)]
    return [from_wire(share, scale) for share in gathered]


def gather_places(chunk):
    sectors = lax.axis_size("sector")
    sector = lax.axis_index("sector")
    places = [lax.axis_index("slab")]
    for shift in range(sectors // 2):
        source = lax.rem(sector - 2 * shift + sectors, sectors)
        places += [source * chunk, (source + 1 - 2 * lax.rem(source, 2)) * chunk]
    return jnp.stack([jnp.asarray(value, jnp.int32) for value in places])


def scatter_sum(parts, scale):
    slabs = parts.shape[0]
    messages = [None] + [to_wire(parts[shift], scale) for shift in range(1, slabs)]
    total = parts[0]
    for message in slab_exchange(messages):
        total = total + from_wire(message, scale)
    return total


def per_device(
    volume_rhs, surface_rhs, volume_guess, surface_guess, bem_matrix, stiffness, mass_shift
):
    slabs, sectors = lax.axis_size("slab"), lax.axis_size("sector")
    slab = lax.axis_index("slab")
    n_theta, n_axial, radial, lanes = volume_guess.shape
    pairs = surface_guess.shape[0]
    axial_all = n_axial * slabs
    turns = pairs // slabs
    chunk = turns * axial_all
    unknowns = sectors * pairs * axial_all

    gain = 8.0 * math.sqrt(unknowns)
    stiff = 3 * (3.0 + 7 * 1.05) + 6 + 3.0
    surface_0 = 6.0
    volume_0 = 6.0
    surface_1 = gain * surface_0 + 12.0
    volume_1 = 80.0 + stiff * volume_0 + surface_0
    surface_2 = gain * surface_1 + volume_1
    volume_2 = stiff * volume_1 + surface_1
    scale_s = [power_scale(bound) for bound in (surface_0, surface_1, surface_2)]
    scale_v = [power_scale(bound) for bound in (volume_0, volume_1, volume_2)]
    scale_p = [
        power_scale(gain / slabs * surface_0 + 12.0),
        power_scale(gain / slabs * surface_1 + volume_1),
        power_scale(gain / slabs * surface_2 + volume_2),
    ]

    place = gather_places(chunk)

    by_owner = surface_guess.reshape(turns, slabs, n_axial, lanes)
    shares = [
        to_wire(
            lax.dynamic_index_in_dim(
                by_owner, lax.rem(slab + shift, slabs), axis=1, keepdims=False
            ),
            scale_s[0],
        ).reshape(turns * n_axial, lanes)
        for shift in range(slabs)
    ]
    columns = jnp.concatenate([shares[0]] + slab_exchange(shares))

    halos = halo_exchange(volume_guess, scale_v[0])
    gathered = sector_gather(columns, scale_s[0])
    wide, narrow = volume_matrices(stiffness, n_theta, radial)
    mass = jnp.broadcast_to(mass_shift[..., None], mass_shift.shape + (HALF,))
    bulk, face = volume_bulk(
        volume_guess, mass, wide, narrow, with_face=True, after=(gathered[0],)
    )
    partial = bem_partial(
        -1.0, True, place, bem_matrix, face, gathered, surface_rhs, after=(bulk,)
    )
    u0, face, first = finish(
        finish_first_kernel, 1, True, bulk, surface_guess, halos, volume_rhs, after=(partial,)
    )
    total = scatter_sum(partial, scale_p[0])
    s0_owner, s0 = total[:chunk], total[chunk:].reshape(pairs, n_axial, lanes)

    halos = halo_exchange(u0, scale_v[1])
    gathered = sector_gather(to_wire(s0_owner, scale_s[1]), scale_s[1])
    (bulk,) = volume_bulk(u0, mass, wide, narrow, after=(s0_owner,))
    partial = bem_partial(1.0, False, place, bem_matrix, face, gathered, after=(bulk,))
    u1, face, second = finish(
        finish_second_kernel, 3, True, bulk, s0, halos, u0, after=(partial,)
    )
    total = scatter_sum(partial, scale_p[1])
    s1_owner, s1 = total[:chunk], total[chunk:].reshape(pairs, n_axial, lanes)

    halos = halo_exchange(u1, scale_v[2])
    gathered = sector_gather(to_wire(s1_owner, scale_s[2]), scale_s[2])
    (bulk,) = volume_bulk(u1, mass, wide, narrow, after=(s1_owner,))
    partial = bem_partial(1.0, False, place, bem_matrix, face, gathered, after=(bulk,))
    third, u0, u1, guess = finish(
        finish_third_kernel, 5, False, bulk, s1, halos, u0, u1, volume_guess, after=(partial,)
    )
    total = scatter_sum(partial[:, :chunk], scale_p[2])

    gram = local_gram(first, second, third, s0_owner, s1_owner, total)
    devices = sectors * slabs
    copies = jnp.broadcast_to(gram.reshape(1, 1, -1), (devices, 1, gram.size))
    gram_all = lax.all_to_all(copies, ("sector", "slab"), split_axis=0, concat_axis=0, tiled=True)
    gram_all = jnp.swapaxes(gram_all.reshape(devices, 9, HALF), 0, 1)
    return final_solution(gram_all, guess, u0, u1, surface_guess, s0, s1)


def solution(mesh):
    return jax.shard_map(
        per_device,
        mesh=mesh,
        in_specs=(
            P("sector", "slab", None, None),
            P("sector", "slab", None),
            P("sector", "slab", None, None),
            P("sector", "slab", None),
            P(None, "sector", "slab"),
            P(),
            P("sector", "slab", None),
        ),
        out_specs=(P("sector", "slab", None, None), P("sector", "slab", None)),
        check_vma=False,
    )
```

```python
import functools
import math

import jax
import jax.numpy as jnp
from jax import lax
from jax.experimental import pallas as pl
from jax.experimental.pallas import tpu as pltpu
from jax.sharding import PartitionSpec as P

PENALTY = 1.0
EPSILON = 1e-06
F32 = jnp.float32
BF16 = jnp.bfloat16
WIRE = jnp.float16
LANES = 256
HALF = 128
VMEM_LIMIT = 8 * 1024 * 1024
WHOLE = pl.BlockSpec(memory_space=pltpu.VMEM)
SCALARS = pl.BlockSpec(memory_space=pltpu.SMEM)
ANYWHERE = pl.BlockSpec(memory_space=pl.ANY)


def call(
    kernel, out_shape, n_scalars, n_arrays, n_anywhere=0, scratch=(), name=None, after=(), out_specs=None, aliases=None, vmem=VMEM_LIMIT,
):
    n_read = n_scalars + n_arrays + n_anywhere

    def body(*refs):
        kernel(*refs[:n_read], *refs[n_read + len(after) :])

    called = pl.pallas_call(
        body,
        out_shape=out_shape,
        in_specs=[SCALARS] * n_scalars
        + [WHOLE] * n_arrays
        + [ANYWHERE] * (n_anywhere + len(after)),
        out_specs=out_specs or jax.tree.map(lambda _: WHOLE, out_shape),
        scratch_shapes=list(scratch),
        input_output_aliases=aliases or {},
        compiler_params=pltpu.CompilerParams(vmem_limit_bytes=vmem),
        cost_estimate=pl.CostEstimate(flops=1000, bytes_accessed=1000, transcendentals=0),
        name=name,
    )
    return lambda *args: called(*args, *after)


def shape(*dims):
    return jax.ShapeDtypeStruct(dims, F32)


def split_bf16(values):
    upper = values.astype(BF16)
    lower = (values - upper.astype(F32)).astype(BF16)
    return upper, lower


def one_hot(rows, columns, pick):
    row = lax.broadcasted_iota(jnp.int32, (rows, columns), 0)
    column = lax.broadcasted_iota(jnp.int32, (rows, columns), 1)
    return (pick(row) == column).astype(F32)


def line_matrix(stiffness, order, nodes, rows, fast):
    select = one_hot(rows, order, lambda row: (row // fast) % order)
    spread = jnp.dot(select, stiffness, precision=lax.Precision.HIGHEST)
    full = lax.dot_general(
        spread, select, (((1,), (1,)), ((), ())), precision=lax.Precision.HIGHEST
    )
    row = lax.broadcasted_iota(jnp.int32, (rows, rows), 0)
    column = lax.broadcasted_iota(jnp.int32, (rows, rows), 1)
    row_node, column_node = row // fast, column // fast
    same_fast = row % fast == column % fast
    same_element = (row_node // order == column_node // order) & same_fast
    block = jnp.where(same_element, full, 0.0)
    edge = (row_node % order == 0) | (row_node % order == order - 1)
    block = block + jnp.where((row == column) & edge, PENALTY, 0.0)
    back = (row_node % order == 0) & (column_node == row_node - 1) & same_fast
    ahead = (row_node % order == order - 1) & (column_node == row_node + 1) & same_fast
    return block - jnp.where(back | ahead, PENALTY, 0.0)


def matrices_kernel(nodes, radial, stiffness_ref, wide_ref, narrow_ref):
    order = stiffness_ref.shape[1]
    rows = nodes * radial
    theta = line_matrix(stiffness_ref[0], order, nodes, rows, radial)
    axial = line_matrix(stiffness_ref[1], order, nodes, rows, radial)
    select = one_hot(rows, order, lambda row: row % radial)
    spread = jnp.dot(select, stiffness_ref[2], precision=lax.Precision.HIGHEST)
    full = lax.dot_general(
        spread, select, (((1,), (1,)), ((), ())), precision=lax.Precision.HIGHEST
    )
    row = lax.broadcasted_iota(jnp.int32, (rows, rows), 0)
    column = lax.broadcasted_iota(jnp.int32, (rows, rows), 1)
    axial = axial + jnp.where(row // radial == column // radial, full, 0.0)
    edge = (row % radial == 0) | (row % radial == radial - 1)
    axial = axial + jnp.where((row == column) & edge, PENALTY, 0.0)
    for index, matrix in enumerate((theta, axial)):
        upper, lower = split_bf16(matrix)
        wide_ref[index, :, :rows] = upper
        wide_ref[index, :, rows:] = upper
        narrow_ref[index] = lower


def volume_matrices(stiffness, nodes, radial, after=()):
    rows = nodes * radial
    return call(
        functools.partial(matrices_kernel, nodes, radial),
        (
            jax.ShapeDtypeStruct((2, rows, 2 * rows), BF16),
            jax.ShapeDtypeStruct((2, rows, rows), BF16),
        ),
        0,
        1,
        name="volume_matrices",
        after=after,
    )(stiffness)


def bulk_kernel(x_ref, mass_ref, wide_ref, narrow_ref, own_ref, y_ref, passed_ref):
    n_theta, n_axial, radial, lanes = x_ref.shape

    def product(index, values):
        upper, lower = split_bf16(values)
        both = jnp.concatenate([upper, lower], axis=0)
        return jnp.dot(wide_ref[index], both, preferred_element_type=F32) + jnp.dot(
            narrow_ref[index], upper, preferred_element_type=F32
        )

    def along_theta(z, carry):
        values = x_ref[:, z].reshape(n_theta * radial, lanes)
        y_ref[:, z] = product(0, values).reshape(n_theta, radial, lanes)
        return carry

    def along_axial(a, carry):
        values = x_ref[a].reshape(n_axial * radial, lanes)
        total = product(1, values).reshape(n_axial, radial, lanes)
        mass = mass_ref[a]
        old = y_ref[a] + total
        x = x_ref[a]
        y_ref[a, :, :, :HALF] = old[:, :, :HALF] + mass * x[:, :, :HALF]
        y_ref[a, :, :, HALF:] = old[:, :, HALF:] + mass * x[:, :, HALF:]
        return carry

    lax.fori_loop(0, n_axial, along_theta, 0, unroll=True)
    lax.fori_loop(0, n_theta, along_axial, 0, unroll=True)


def volume_bulk(x, mass, wide, narrow, own, after=()):
    n_theta, n_axial, radial, lanes = x.shape
    return call(
        bulk_kernel,
        (shape(*x.shape), shape(*own.shape)),
        0,
        5,
        name="volume_bulk",
        aliases={4: 1},
        after=after,
    )(x, mass, wide, narrow, own)


def edges_kernel(x_ref, first_ref, last_ref, axial_first_ref, axial_last_ref, face_ref, copy_ref):
    n_theta, n_axial = x_ref.shape[:2]
    first_ref[...] = x_ref[0]
    last_ref[...] = x_ref[n_theta - 1]
    axial_first_ref[...] = x_ref[:, 0]
    axial_last_ref[...] = x_ref[:, n_axial - 1]
    put_faces(x_ref, face_ref)
    copy_ref[...] = x_ref[...]


def volume_edges(x):
    n_theta, n_axial, radial, lanes = x.shape
    theta, axial = shape(n_axial, radial, lanes), shape(n_theta, radial, lanes)
    *layers, face, copy = call(
        edges_kernel,
        (theta, theta, axial, axial, shape(n_theta // 2, n_axial, lanes), shape(*x.shape)),
        0,
        1,
        name="volume_edges",
    )(x)
    return layers, face, copy


def pass_after(values, *earlier):
    return call(
        lambda values_ref, out_ref: None,
        shape(*values.shape),
        0,
        1,
        name="pass_after",
        after=earlier,
        aliases={0: 0},
    )(values)


def pair_sums(left, right):
    left_real, left_imag = left[..., :HALF], left[..., HALF:]
    right_real, right_imag = right[..., :HALF], right[..., HALF:]
    return (
        jnp.sum(left_real * right_real + left_imag * right_imag, axis=0),
        jnp.sum(left_real * right_imag - left_imag * right_real, axis=0),
    )


def square_sums(values):
    squares = values * values
    return jnp.sum(squares[..., :HALF] + squares[..., HALF:], axis=0)


def finish_row(a, bulk, s_ref, before_ref, beyond_ref, axial_before_ref, axial_beyond_ref, n_theta):
    n_axial, radial, lanes = bulk.shape
    if isinstance(a, int) and a == 0:
        bulk = bulk - before_ref[...]
    if isinstance(a, int) and a == n_theta - 1:
        bulk = bulk - beyond_ref[...]
    outer = lax.broadcasted_iota(jnp.int32, (radial, lanes), 0) == radial - 1
    tiles = []
    for z in range(n_axial):
        tile = bulk[z]
        if z == 0:
            tile = tile - axial_before_ref[a]
        if z == n_axial - 1:
            tile = tile - axial_beyond_ref[a]
        face = jnp.broadcast_to(s_ref[a // 2, z : z + 1, :], (radial, lanes))
        tiles.append(tile + jnp.where(outer, face, 0.0))
    return jnp.stack(tiles)


def over_rows(n_theta, body):
    body(0)
    lax.fori_loop(1, n_theta - 1, lambda a, carry: (body(a), carry)[1], 0)
    body(n_theta - 1)


def put_faces(u_ref, face_ref):
    radial = u_ref.shape[2]
    for pair in range(face_ref.shape[0]):
        face_ref[pair] = 0.5 * (
            u_ref[2 * pair, :, radial - 1, :] + u_ref[2 * pair + 1, :, radial - 1, :]
        )


def finish_first_kernel(
    bulk_ref, s_ref, before_ref, beyond_ref, ax_before_ref, ax_beyond_ref, rhs_ref,
    u_ref, face_ref, sums_ref,
):
    n_theta = bulk_ref.shape[0]
    sums_ref[...] = jnp.zeros_like(sums_ref)

    def body(a):
        image = finish_row(
            a, bulk_ref[a], s_ref, before_ref, beyond_ref, ax_before_ref, ax_beyond_ref, n_theta
        )
        u = rhs_ref[a] - image
        u_ref[a] = u
        sums_ref[0] += square_sums(u)

    over_rows(n_theta, body)
    put_faces(u_ref, face_ref)


def finish_second_kernel(
    bulk_ref, s_ref, before_ref, beyond_ref, ax_before_ref, ax_beyond_ref, u0_ref,
    u_ref, face_ref, sums_ref,
):
    n_theta = bulk_ref.shape[0]
    sums_ref[...] = jnp.zeros_like(sums_ref)

    def body(a):
        u = finish_row(
            a, bulk_ref[a], s_ref, before_ref, beyond_ref, ax_before_ref, ax_beyond_ref, n_theta
        )
        u_ref[a] = u
        real, imag = pair_sums(u0_ref[a], u)
        sums_ref[0] += real
        sums_ref[1] += imag
        sums_ref[2] += square_sums(u)

    over_rows(n_theta, body)
    put_faces(u_ref, face_ref)


def finish_third_kernel(
    bulk_ref, s_ref, before_ref, beyond_ref, ax_before_ref, ax_beyond_ref, u0_ref, u1_ref,
    sums_ref,
):
    n_theta = bulk_ref.shape[0]
    sums_ref[...] = jnp.zeros_like(sums_ref)

    def body(a):
        u = finish_row(
            a, bulk_ref[a], s_ref, before_ref, beyond_ref, ax_before_ref, ax_beyond_ref, n_theta
        )
        real, imag = pair_sums(u0_ref[a], u)
        sums_ref[0] += real
        sums_ref[1] += imag
        real, imag = pair_sums(u1_ref[a], u)
        sums_ref[2] += real
        sums_ref[3] += imag
        sums_ref[4] += square_sums(u)

    over_rows(n_theta, body)


def finish(kernel, n_sums, with_result, bulk, s, halos, *others, after=()):
    n_theta, n_axial, radial, lanes = bulk.shape
    outs = (shape(n_sums, radial, HALF),)
    if with_result:
        outs = (shape(*bulk.shape), shape(n_theta // 2, n_axial, lanes)) + outs
    return call(
        kernel,
        outs,
        0,
        6 + len(others),
        name=kernel.__name__,
        after=after,
    )(bulk, s, *halos, *others)


def bem_kernel(sign, by_source, place_ref, m_ref, face_ref, *rest):
    own_ref, out_ref, upper_ref, lower_ref, p_ref = rest[-5:]
    out_chunk = own_ref.shape[0] // 2
    n_pieces = m_ref.shape[2] // out_chunk
    s_refs, rhs_refs = rest[:n_pieces], rest[n_pieces:-5]
    pairs, n_axial, lanes = face_ref.shape
    slabs = out_ref.shape[0] + 1
    axial_all = p_ref.shape[1]
    rows = m_ref.shape[1]
    slab = place_ref[0]
    turns = pairs // slabs

    def place_rows(s_ref, first, count, start):
        upper, lower = split_bf16(s_ref[first : first + count, :])
        at = pl.ds(pl.multiple_of(start, count), count)
        upper_ref[at, :] = upper
        lower_ref[at, :] = lower

    for which, s_ref in enumerate(s_refs):
        start = place_ref[1 + which]
        if not by_source:
            place_rows(s_ref, 0, out_chunk, start)
            continue
        for source in range(slabs):
            for turn in range(turns):
                place_rows(
                    s_ref,
                    (source * turns + turn) * n_axial,
                    n_axial,
                    start + turn * axial_all + source * n_axial,
                )

    step = 2 * axial_all if axial_all < 128 else axial_all

    def block(index, carry):
        at = pl.ds(pl.multiple_of(index * step, step), step)
        real = m_ref[0, at, :]
        imag = m_ref[1, at, :]
        by_real = jnp.dot(real, upper_ref[...], preferred_element_type=F32) + jnp.dot(
            real, lower_ref[...], preferred_element_type=F32
        )
        by_imag = jnp.dot(imag, upper_ref[...], preferred_element_type=F32) + jnp.dot(
            imag, lower_ref[...], preferred_element_type=F32
        )
        here = pl.ds(index * (step // axial_all), step // axial_all)
        three = (step // axial_all, axial_all, HALF)
        p_ref[here, :, :HALF] = sign * (by_real[:, :HALF] - by_imag[:, HALF:]).reshape(three)
        p_ref[here, :, HALF:] = sign * (by_real[:, HALF:] + by_imag[:, :HALF]).reshape(three)
        return carry

    lax.fori_loop(0, rows // step, block, 0, unroll=True)
    own = pl.ds(pl.multiple_of(slab * n_axial, n_axial), n_axial)
    add = -sign * face_ref[...]
    for rhs_ref in rhs_refs:
        add = add + rhs_ref[...]
    p_ref[:, own, :] += add
    for shift in range(slabs):
        target = partner(slab, shift, slabs)
        part_ref = own_ref if shift == 0 else out_ref.at[shift - 1]
        for turn in range(turns):
            part_ref[turn * axial_all : (turn + 1) * axial_all, :] = p_ref[target + turn * slabs]
        there = pl.ds(pl.multiple_of(target * n_axial, n_axial), n_axial)
        part_ref[out_chunk:, :] = p_ref[:, there, :].reshape(out_chunk, lanes)


def bem_partial(sign, by_source, place, matrix, face, gathered, *rhs, after=()):
    pairs, n_axial, lanes = face.shape
    chunk = gathered[0].shape[0]
    rows, columns = matrix.shape[1:]
    axial_all = rows // pairs
    slabs = axial_all // n_axial
    return call(
        functools.partial(bem_kernel, sign, by_source),
        (shape(2 * chunk, lanes), shape(slabs - 1, 2 * chunk, lanes)),
        1,
        2 + len(gathered) + len(rhs),
        scratch=[
            pltpu.VMEM((columns, lanes), BF16),
            pltpu.VMEM((columns, lanes), BF16),
            pltpu.VMEM((pairs, axial_all, lanes), F32),
        ],
        name="bem_partial",
        after=after,
    )(place, matrix, face, *gathered, *rhs)


def surface_sums(u0, u1, u2):
    sums = (square_sums(u0),) + pair_sums(u0, u1) + (square_sums(u1),)
    return sums + pair_sums(u0, u2) + pair_sums(u1, u2) + (square_sums(u2),)


def gram_kernel(first_ref, second_ref, third_ref, s0_ref, s1_ref, s2_ref, out_ref):
    volume = (
        [first_ref[0]]
        + [second_ref[row] for row in range(3)]
        + [third_ref[row] for row in range(5)]
    )
    surface = surface_sums(s0_ref[...], s1_ref[...], s2_ref[...])
    for row, (one, two) in enumerate(zip(volume, surface)):
        total = jnp.sum(one, axis=0, keepdims=True) + jnp.sum(two, axis=0, keepdims=True)
        for device in range(out_ref.shape[0]):
            out_ref[device, :, row * HALF : (row + 1) * HALF] = total


def local_gram(devices, first, second, third, s0, s1, s2):
    tiles = [values.reshape(-1, 8, LANES) for values in (s0, s1, s2)]
    return call(gram_kernel, shape(devices, 1, 9 * HALF), 0, 6, name="local_gram")(
        first, second, third, *tiles
    )


def times(left, right):
    return (
        left[0] * right[0] - left[1] * right[1],
        left[0] * right[1] + left[1] * right[0],
    )


def conj_times(left, right):
    return (
        left[0] * right[0] + left[1] * right[1],
        left[0] * right[1] - left[1] * right[0],
    )


def square(value):
    return value[0] * value[0] + value[1] * value[1]


def coefficients(rows):
    g00, g11, g22 = rows[0], rows[3], rows[8]
    g01, g02, g12 = (rows[1], rows[2]), (rows[4], rows[5]), (rows[6], rows[7])
    beta_sq = g00 + EPSILON
    beta = jnp.sqrt(beta_sq)
    h00 = (g01[0] / beta_sq, g01[1] / beta_sq)
    h00_sq = square(h00)
    cross = conj_times(h00, g01)[0]
    rest = jnp.maximum(g11 - 2.0 * cross + h00_sq * g00, 0.0) / beta_sq
    h10_sq = rest + EPSILON
    h10 = jnp.sqrt(h10_sq)
    over_first = 1.0 / (beta_sq * h10)
    over_second = 1.0 / (beta_sq * h10_sq)
    h00_g01 = times(h00, g01)
    h01 = tuple((g02[k] - h00_g01[k]) * over_first for k in (0, 1))
    conj_g02 = conj_times(h00, g02)
    h11 = tuple(
        (g12[k] - h00[k] * g11 - conj_g02[k] + h00_sq * g01[k]) * over_second for k in (0, 1)
    )
    image_sq = (g22 - 2.0 * conj_times(h00, g12)[0] + h00_sq * g11) * over_second
    first_sq, second_sq = g00 / beta_sq, rest / h10_sq
    overlap = (h00[0] * EPSILON * over_first, h00[1] * EPSILON * over_first)
    mixed = conj_times(h01, times(h11, overlap))[0]
    bottom_sq = (
        jnp.maximum(
            image_sq
            - (2.0 - first_sq) * square(h01)
            - (2.0 - second_sq) * square(h11)
            + 2.0 * mixed,
            0.0,
        )
        + EPSILON
    )
    rho = jnp.sqrt(h00_sq + h10_sq)
    cos = (h00[0] / rho, h00[1] / rho)
    sine = h10 / rho
    top = conj_times(cos, h01)
    top = tuple(top[k] + sine * h11[k] for k in (0, 1))
    turn = times(cos, h11)
    turn = tuple(turn[k] - sine * h01[k] for k in (0, 1))
    lower = -sine * beta / (square(turn) + bottom_sq)
    one = (turn[0] * lower, -turn[1] * lower)
    top_one = times(top, one)
    zero = ((cos[0] * beta - top_one[0]) / rho, (-cos[1] * beta - top_one[1]) / rho)
    of_second = (one[0] / (beta * h10), one[1] / (beta * h10))
    back = times(of_second, h00)
    of_first = (zero[0] / beta - back[0], zero[1] / beta - back[1])
    return of_first, of_second


def combine(first, second, guess, u0, u1):
    u0_real, u0_imag = u0[..., :HALF], u0[..., HALF:]
    u1_real, u1_imag = u1[..., :HALF], u1[..., HALF:]
    real = guess[..., :HALF] + (first[0] * u0_real - first[1] * u0_imag)
    imag = guess[..., HALF:] + (first[0] * u0_imag + first[1] * u0_real)
    real = real + (second[0] * u1_real - second[1] * u1_imag)
    imag = imag + (second[0] * u1_imag + second[1] * u1_real)
    return real, imag


def solution_kernel(
    gram_ref, x_ref, u0_ref, u1_ref, s_ref, s0_ref, s1_ref,
    volume_ref, surface_ref, row_ref, stored,
):
    total = jnp.sum(gram_ref[...], axis=0)
    sums = [total[:, row * HALF : (row + 1) * HALF] for row in range(9)]
    first, second = coefficients(sums)
    n_theta = x_ref.shape[0]

    def store(a):
        return pltpu.make_async_copy(row_ref.at[a], volume_ref.at[a], stored.at[a])

    for a in range(n_theta):
        real, imag = combine(first, second, x_ref[a], u0_ref[a], u1_ref[a])
        row_ref[a, :, :, :HALF] = real
        row_ref[a, :, :, HALF:] = imag
        store(a).start()
    real, imag = combine(first, second, s_ref[...], s0_ref[...], s1_ref[...])
    surface_ref[..., :HALF] = real
    surface_ref[..., HALF:] = imag
    for a in range(n_theta):
        store(a).wait()


def final_solution(gram_all, x, u0, u1, s, s0, s1):
    return call(
        solution_kernel,
        (shape(*x.shape), shape(*s.shape)),
        0,
        7,
        scratch=[pltpu.VMEM(x.shape, F32), pltpu.SemaphoreType.DMA((x.shape[0],))],
        name="final_solution",
        out_specs=(ANYWHERE, WHOLE),
    )(gram_all, x, u0, u1, s, s0, s1)


def power_scale(bound):
    return 2.0 ** math.floor(math.log2(60000.0 / bound))


def to_wire(values, scale):
    return (values * scale).astype(WIRE)


def from_wire(values, scale):
    return values.astype(F32) * (1.0 / scale)


def partner(index, distance, peers):
    if peers & (peers - 1) == 0:
        return index ^ distance
    return lax.rem(index + distance, peers)


def partner_perm(peers, distance):
    if peers & (peers - 1) == 0:
        return [(i, i ^ distance) for i in range(peers)]
    return [(i, (i + distance) % peers) for i in range(peers)]


def slab_exchange(messages):
    slabs = lax.axis_size("slab")
    return [
        lax.ppermute(messages[distance], "slab", partner_perm(slabs, distance))
        for distance in range(1, slabs)
    ]


def neighbour_swap(axis, first, last, scale, wrap):
    peers = lax.axis_size(axis)
    odd = lax.rem(lax.axis_index(axis), 2) == 1
    first, last = to_wire(first, scale), to_wire(last, scale)
    within = [(i, i ^ 1) for i in range(peers)]
    across = [
        pair
        for i in range(1, peers if wrap else peers - 1, 2)
        for pair in ((i, (i + 1) % peers), ((i + 1) % peers, i))
    ]
    inner = lax.ppermute(jnp.where(odd, first, last), axis, within)
    outer = lax.ppermute(jnp.where(odd, last, first), axis, across)
    before = from_wire(jnp.where(odd, inner, outer), scale)
    beyond = from_wire(jnp.where(odd, outer, inner), scale)
    return before, beyond


def theta_halos(layers, scale):
    return neighbour_swap("sector", *layers[:2], scale, True)


def axial_halos(layers, scale):
    return neighbour_swap("slab", *layers[2:], scale, False)


def edge_layers(volume):
    return volume[0], volume[-1], volume[:, 0], volume[:, -1]


def sibling_perm():
    return [(i, i ^ 1) for i in range(lax.axis_size("sector"))]


def sector_gather(own, scale):
    sectors = lax.axis_size("sector")
    shares = [own]
    for distance in range(1, sectors // 2):
        perm = [
            (2 * i + core, 2 * j + core)
            for i, j in partner_perm(sectors // 2, distance)
            for core in range(2)
        ]
        shares.append(lax.ppermute(own, "sector", perm))
    gathered = []
    for share in shares:
        gathered += [share, lax.ppermute(share, "sector", sibling_perm())]
    return [from_wire(share, scale) for share in gathered]


def gather_places(chunk):
    chips = lax.axis_size("sector") // 2
    sector = lax.axis_index("sector")
    chip, core = sector // 2, lax.rem(sector, 2)
    places = [lax.axis_index("slab")]
    for distance in range(chips):
        mutual = chips & (chips - 1) == 0
        source = chip ^ distance if mutual else lax.rem(chip - distance + chips, chips)
        places += [(2 * source + core) * chunk, (2 * source + 1 - core) * chunk]
    return jnp.stack([jnp.asarray(value, jnp.int32) for value in places])


def first_gather(surface, scale):
    sectors, slabs = lax.axis_size("sector"), lax.axis_size("slab")
    chips = sectors // 2
    pairs, n_axial, lanes = surface.shape
    turns = pairs // slabs
    by_owner = to_wire(surface, scale).reshape(turns, slabs, n_axial, lanes)
    by_owner = jnp.swapaxes(by_owner, 0, 1).reshape(1, slabs, turns * n_axial, lanes)
    messages = jnp.broadcast_to(by_owner, (chips,) + by_owner.shape[1:])
    groups = [
        [(2 * chip + core) * slabs + slab for chip in range(chips) for slab in range(slabs)]
        for core in range(2)
    ]
    mine = lax.all_to_all(
        messages.reshape(chips * slabs, turns * n_axial, lanes),
        ("sector", "slab"),
        split_axis=0,
        concat_axis=0,
        axis_index_groups=groups,
        tiled=True,
    )
    other = lax.ppermute(mine, "sector", sibling_perm())
    mine, other = (
        from_wire(values, scale).reshape(chips, slabs * turns * n_axial, lanes)
        for values in (mine, other)
    )
    return [values[chip] for chip in range(chips) for values in (mine, other)]


def first_places(chunk):
    sectors = lax.axis_size("sector")
    core = lax.rem(lax.axis_index("sector"), 2)
    places = [lax.axis_index("slab")]
    for chip in range(sectors // 2):
        places += [(2 * chip + core) * chunk, (2 * chip + 1 - core) * chunk]
    return jnp.stack([jnp.asarray(value, jnp.int32) for value in places])


def scatter(parts, scale):
    messages = [None] + [to_wire(parts[which], scale) for which in range(parts.shape[0])]
    meanwhile = lax.ppermute(messages[1][:16, :HALF], "sector", sibling_perm())
    return slab_exchange(messages), meanwhile.astype(F32)


def scatter_sum(own, received, scale):
    for message in received:
        own = own + from_wire(message, scale)
    return own


def per_device(
    volume_rhs, surface_rhs, volume_guess, surface_guess, bem_matrix, stiffness, mass_shift
):
    slabs, sectors = lax.axis_size("slab"), lax.axis_size("sector")
    slab = lax.axis_index("slab")
    n_theta, n_axial, radial, lanes = volume_guess.shape
    pairs = surface_guess.shape[0]
    axial_all = n_axial * slabs
    turns = pairs // slabs
    chunk = turns * axial_all
    unknowns = sectors * pairs * axial_all

    gain = 8.0 * math.sqrt(unknowns)
    stiff = 3 * (3.0 + 7 * 1.05) + 6 + 3.0
    surface_0 = 6.0
    volume_0 = 6.0
    surface_1 = gain * surface_0 + 12.0
    volume_1 = 80.0 + stiff * volume_0 + surface_0
    surface_2 = gain * surface_1 + volume_1
    volume_2 = stiff * volume_1 + surface_1
    scale_s = [power_scale(bound) for bound in (surface_0, surface_1, surface_2)]
    scale_v = [power_scale(bound) for bound in (volume_0, volume_1, volume_2)]
    scale_p = [
        power_scale(gain / slabs * surface_0 + 12.0),
        power_scale(gain / slabs * surface_1 + volume_1),
        power_scale(gain / slabs * surface_2 + volume_2),
    ]

    place = gather_places(chunk)

    def surface_parts(total):
        return total[:chunk], total[chunk:].reshape(pairs, n_axial, lanes)

    gathered = first_gather(surface_guess, scale_s[0])
    mass = jnp.broadcast_to(mass_shift[..., None], mass_shift.shape + (HALF,))
    wide, narrow = volume_matrices(stiffness, n_theta, radial)
    layers, face, guess = volume_edges(volume_guess)
    halos = theta_halos(layers, scale_v[0]) + axial_halos(layers, scale_v[0])
    own, parts = bem_partial(
        -1.0, True, first_places(chunk), bem_matrix, face, gathered, surface_rhs
    )
    received, meanwhile = scatter(parts, scale_p[0])
    bulk, own = volume_bulk(guess, mass, wide, narrow, own, after=(meanwhile,))
    u0, face, first = finish(
        finish_first_kernel, 1, True, bulk, surface_guess, halos, volume_rhs
    )
    theta = theta_halos(edge_layers(u0), scale_v[1])
    bulk, own = volume_bulk(u0, mass, wide, narrow, own)
    s0_owner, s0 = surface_parts(scatter_sum(own, received, scale_p[0]))

    gathered = sector_gather(to_wire(s0_owner, scale_s[1]), scale_s[1])
    u0 = pass_after(u0, gathered[1])
    halos = theta + axial_halos(edge_layers(u0), scale_v[1])
    own, parts = bem_partial(1.0, False, place, bem_matrix, face, gathered)
    received, meanwhile = scatter(parts, scale_p[1])
    u1, face, second = finish(
        finish_second_kernel, 3, True, bulk, s0, halos, u0, after=(meanwhile,)
    )
    theta = theta_halos(edge_layers(u1), scale_v[2])
    bulk, own = volume_bulk(u1, mass, wide, narrow, own)
    s1_owner, s1 = surface_parts(scatter_sum(own, received, scale_p[1]))

    gathered = sector_gather(to_wire(s1_owner, scale_s[2]), scale_s[2])
    u1 = pass_after(u1, gathered[1])
    halos = theta + axial_halos(edge_layers(u1), scale_v[2])
    own, parts = bem_partial(1.0, False, place, bem_matrix, face, gathered)
    received, meanwhile = scatter(parts[:, :chunk], scale_p[2])
    (third,) = finish(
        finish_third_kernel, 5, False, bulk, s1, halos, u0, u1, after=(meanwhile,)
    )
    total = scatter_sum(own[:chunk], received, scale_p[2])

    gram = local_gram(sectors * slabs, first, second, third, s0_owner, s1_owner, total)
    gram_all = lax.all_to_all(gram, ("sector", "slab"), split_axis=0, concat_axis=0, tiled=True)
    return final_solution(gram_all, guess, u0, u1, surface_guess, s0, s1)


def solution(mesh):
    return jax.shard_map(
        per_device,
        mesh=mesh,
        in_specs=(
            P("sector", "slab", None, None),
            P("sector", "slab", None),
            P("sector", "slab", None, None),
            P("sector", "slab", None),
            P(None, "sector", "slab"),
            P(),
            P("sector", "slab", None),
        ),
        out_specs=(P("sector", "slab", None, None), P("sector", "slab", None)),
        check_vma=False,
    )
```

```python
import functools
import math

import jax
import jax.numpy as jnp
from jax import lax
from jax.experimental import pallas as pl
from jax.experimental.pallas import tpu as pltpu
from jax.sharding import PartitionSpec as P

PENALTY = 1.0
EPSILON = 1e-06
F32 = jnp.float32
BF16 = jnp.bfloat16
WIRE = jnp.float16
LANES = 256
HALF = 128
VMEM_LIMIT = 8 * 1024 * 1024
WHOLE = pl.BlockSpec(memory_space=pltpu.VMEM)
SCALARS = pl.BlockSpec(memory_space=pltpu.SMEM)
ANYWHERE = pl.BlockSpec(memory_space=pl.ANY)


def call(
    kernel, out_shape, n_scalars, n_arrays, n_anywhere=0, scratch=(), name=None, after=(), out_specs=None, aliases=None, vmem=VMEM_LIMIT,
):
    n_read = n_scalars + n_arrays + n_anywhere

    def body(*refs):
        kernel(*refs[:n_read], *refs[n_read + len(after) :])

    called = pl.pallas_call(
        body,
        out_shape=out_shape,
        in_specs=[SCALARS] * n_scalars
        + [WHOLE] * n_arrays
        + [ANYWHERE] * (n_anywhere + len(after)),
        out_specs=out_specs or jax.tree.map(lambda _: WHOLE, out_shape),
        scratch_shapes=list(scratch),
        input_output_aliases=aliases or {},
        compiler_params=pltpu.CompilerParams(vmem_limit_bytes=vmem),
        cost_estimate=pl.CostEstimate(flops=1000, bytes_accessed=1000, transcendentals=0),
        name=name,
    )
    return lambda *args: called(*args, *after)


def shape(*dims):
    return jax.ShapeDtypeStruct(dims, F32)


def split_bf16(values):
    upper = values.astype(BF16)
    lower = (values - upper.astype(F32)).astype(BF16)
    return upper, lower


def one_hot(rows, columns, pick):
    row = lax.broadcasted_iota(jnp.int32, (rows, columns), 0)
    column = lax.broadcasted_iota(jnp.int32, (rows, columns), 1)
    return (pick(row) == column).astype(F32)


def line_matrix(stiffness, order, nodes, rows, fast):
    select = one_hot(rows, order, lambda row: (row // fast) % order)
    spread = jnp.dot(select, stiffness, precision=lax.Precision.HIGHEST)
    full = lax.dot_general(
        spread, select, (((1,), (1,)), ((), ())), precision=lax.Precision.HIGHEST
    )
    row = lax.broadcasted_iota(jnp.int32, (rows, rows), 0)
    column = lax.broadcasted_iota(jnp.int32, (rows, rows), 1)
    row_node, column_node = row // fast, column // fast
    same_fast = row % fast == column % fast
    same_element = (row_node // order == column_node // order) & same_fast
    block = jnp.where(same_element, full, 0.0)
    edge = (row_node % order == 0) | (row_node % order == order - 1)
    block = block + jnp.where((row == column) & edge, PENALTY, 0.0)
    back = (row_node % order == 0) & (column_node == row_node - 1) & same_fast
    ahead = (row_node % order == order - 1) & (column_node == row_node + 1) & same_fast
    return block - jnp.where(back | ahead, PENALTY, 0.0)


def matrices_kernel(nodes, radial, stiffness_ref, wide_ref, narrow_ref):
    order = stiffness_ref.shape[1]
    rows = nodes * radial
    theta = line_matrix(stiffness_ref[0], order, nodes, rows, radial)
    axial = line_matrix(stiffness_ref[1], order, nodes, rows, radial)
    select = one_hot(rows, order, lambda row: row % radial)
    spread = jnp.dot(select, stiffness_ref[2], precision=lax.Precision.HIGHEST)
    full = lax.dot_general(
        spread, select, (((1,), (1,)), ((), ())), precision=lax.Precision.HIGHEST
    )
    row = lax.broadcasted_iota(jnp.int32, (rows, rows), 0)
    column = lax.broadcasted_iota(jnp.int32, (rows, rows), 1)
    axial = axial + jnp.where(row // radial == column // radial, full, 0.0)
    edge = (row % radial == 0) | (row % radial == radial - 1)
    axial = axial + jnp.where((row == column) & edge, PENALTY, 0.0)
    for index, matrix in enumerate((theta, axial)):
        upper, lower = split_bf16(matrix)
        wide_ref[index, :, :rows] = upper
        wide_ref[index, :, rows:] = upper
        narrow_ref[index] = lower


def volume_matrices(stiffness, nodes, radial, after=()):
    rows = nodes * radial
    return call(
        functools.partial(matrices_kernel, nodes, radial),
        (
            jax.ShapeDtypeStruct((2, rows, 2 * rows), BF16),
            jax.ShapeDtypeStruct((2, rows, rows), BF16),
        ),
        0,
        1,
        name="volume_matrices",
        after=after,
    )(stiffness)


def bulk_kernel(
    x_ref, mass_ref, wide_ref, narrow_ref, own_ref, y_ref, passed_ref, *copy_refs
):
    n_theta, n_axial, radial, lanes = x_ref.shape

    def product(index, values):
        upper, lower = split_bf16(values)
        both = jnp.concatenate([upper, lower], axis=0)
        return jnp.dot(wide_ref[index], both, preferred_element_type=F32) + jnp.dot(
            narrow_ref[index], upper, preferred_element_type=F32
        )

    def along_theta(z, carry):
        values = x_ref[:, z].reshape(n_theta * radial, lanes)
        y_ref[:, z] = product(0, values).reshape(n_theta, radial, lanes)
        return carry

    def along_axial(a, carry):
        values = x_ref[a].reshape(n_axial * radial, lanes)
        total = product(1, values).reshape(n_axial, radial, lanes)
        mass = mass_ref[a]
        old = y_ref[a] + total
        x = x_ref[a]
        y_ref[a, :, :, :HALF] = old[:, :, :HALF] + mass * x[:, :, :HALF]
        y_ref[a, :, :, HALF:] = old[:, :, HALF:] + mass * x[:, :, HALF:]
        return carry

    lax.fori_loop(0, n_axial, along_theta, 0, unroll=True)
    lax.fori_loop(0, n_theta, along_axial, 0, unroll=True)
    for copy_ref in copy_refs:
        copy_ref[...] = x_ref[...]


def volume_bulk(x, mass, wide, narrow, own, copied=False, after=()):
    outs = (shape(*x.shape), shape(*own.shape)) + ((shape(*x.shape),) if copied else ())
    return call(
        bulk_kernel,
        outs,
        0,
        5,
        name="volume_bulk",
        aliases={4: 1},
        after=after,
    )(x, mass, wide, narrow, own)


def edges_kernel(
    x_ref, first_ref, last_ref, axial_first_ref, axial_last_ref, face_ref, outer_ref, copied
):
    n_theta, n_axial, radial, _ = x_ref.shape
    copies = [
        pltpu.make_async_copy(source, target, copied.at[index])
        for index, (source, target) in enumerate(
            (
                (x_ref.at[0], first_ref),
                (x_ref.at[n_theta - 1], last_ref),
                (x_ref.at[:, 0], axial_first_ref),
                (x_ref.at[:, n_axial - 1], axial_last_ref),
                (x_ref.at[:, :, radial - 1], outer_ref),
            )
        )
    ]
    for copy in copies:
        copy.start()
    for copy in copies:
        copy.wait()
    for pair in range(face_ref.shape[0]):
        face_ref[pair] = 0.5 * (outer_ref[2 * pair] + outer_ref[2 * pair + 1])


def volume_edges(x):
    n_theta, n_axial, radial, lanes = x.shape
    theta, axial = shape(n_axial, radial, lanes), shape(n_theta, radial, lanes)
    *layers, face = call(
        edges_kernel,
        (theta, theta, axial, axial, shape(n_theta // 2, n_axial, lanes)),
        0,
        0,
        1,
        scratch=[
            pltpu.VMEM((n_theta, n_axial, lanes), F32),
            pltpu.SemaphoreType.DMA((5,)),
        ],
        name="volume_edges",
    )(x)
    return layers, face


def pass_after(values, *earlier):
    return call(
        lambda values_ref, out_ref: None,
        shape(*values.shape),
        0,
        1,
        name="pass_after",
        after=earlier,
        aliases={0: 0},
    )(values)


def pair_sums(left, right):
    left_real, left_imag = left[..., :HALF], left[..., HALF:]
    right_real, right_imag = right[..., :HALF], right[..., HALF:]
    return (
        jnp.sum(left_real * right_real + left_imag * right_imag, axis=0),
        jnp.sum(left_real * right_imag - left_imag * right_real, axis=0),
    )


def square_sums(values):
    squares = values * values
    return jnp.sum(squares[..., :HALF] + squares[..., HALF:], axis=0)


def finish_row(a, bulk, s_ref, before_ref, beyond_ref, axial_before_ref, axial_beyond_ref, n_theta):
    n_axial, radial, lanes = bulk.shape
    if isinstance(a, int) and a == 0:
        bulk = bulk - before_ref[...]
    if isinstance(a, int) and a == n_theta - 1:
        bulk = bulk - beyond_ref[...]
    outer = lax.broadcasted_iota(jnp.int32, (radial, lanes), 0) == radial - 1
    tiles = []
    for z in range(n_axial):
        tile = bulk[z]
        if z == 0:
            tile = tile - axial_before_ref[a]
        if z == n_axial - 1:
            tile = tile - axial_beyond_ref[a]
        face = jnp.broadcast_to(s_ref[a // 2, z : z + 1, :], (radial, lanes))
        tiles.append(tile + jnp.where(outer, face, 0.0))
    return jnp.stack(tiles)


def over_rows(n_theta, body):
    body(0)
    lax.fori_loop(1, n_theta - 1, lambda a, carry: (body(a), carry)[1], 0)
    body(n_theta - 1)


def put_faces(u_ref, face_ref):
    radial = u_ref.shape[2]
    for pair in range(face_ref.shape[0]):
        face_ref[pair] = 0.5 * (
            u_ref[2 * pair, :, radial - 1, :] + u_ref[2 * pair + 1, :, radial - 1, :]
        )


def finish_first_kernel(
    bulk_ref, s_ref, before_ref, beyond_ref, ax_before_ref, ax_beyond_ref, rhs_ref,
    u_ref, face_ref, sums_ref,
):
    n_theta = bulk_ref.shape[0]
    sums_ref[...] = jnp.zeros_like(sums_ref)

    def body(a):
        image = finish_row(
            a, bulk_ref[a], s_ref, before_ref, beyond_ref, ax_before_ref, ax_beyond_ref, n_theta
        )
        u = rhs_ref[a] - image
        u_ref[a] = u
        sums_ref[0] += square_sums(u)

    over_rows(n_theta, body)
    put_faces(u_ref, face_ref)


def finish_second_kernel(
    bulk_ref, s_ref, before_ref, beyond_ref, ax_before_ref, ax_beyond_ref, u0_ref,
    u_ref, face_ref, sums_ref,
):
    n_theta = bulk_ref.shape[0]
    sums_ref[...] = jnp.zeros_like(sums_ref)

    def body(a):
        u = finish_row(
            a, bulk_ref[a], s_ref, before_ref, beyond_ref, ax_before_ref, ax_beyond_ref, n_theta
        )
        u_ref[a] = u
        real, imag = pair_sums(u0_ref[a], u)
        sums_ref[0] += real
        sums_ref[1] += imag
        sums_ref[2] += square_sums(u)

    over_rows(n_theta, body)
    put_faces(u_ref, face_ref)


def finish_third_kernel(
    bulk_ref, s_ref, before_ref, beyond_ref, ax_before_ref, ax_beyond_ref, u0_ref, u1_ref,
    sums_ref,
):
    n_theta = bulk_ref.shape[0]
    sums_ref[...] = jnp.zeros_like(sums_ref)

    def body(a):
        u = finish_row(
            a, bulk_ref[a], s_ref, before_ref, beyond_ref, ax_before_ref, ax_beyond_ref, n_theta
        )
        real, imag = pair_sums(u0_ref[a], u)
        sums_ref[0] += real
        sums_ref[1] += imag
        real, imag = pair_sums(u1_ref[a], u)
        sums_ref[2] += real
        sums_ref[3] += imag
        sums_ref[4] += square_sums(u)

    over_rows(n_theta, body)


def finish(kernel, n_sums, with_result, bulk, s, halos, *others, after=()):
    n_theta, n_axial, radial, lanes = bulk.shape
    outs = (shape(n_sums, radial, HALF),)
    if with_result:
        outs = (shape(*bulk.shape), shape(n_theta // 2, n_axial, lanes)) + outs
    return call(
        kernel,
        outs,
        0,
        6 + len(others),
        name=kernel.__name__,
        after=after,
    )(bulk, s, *halos, *others)


def bem_kernel(sign, by_source, split, place_ref, m_ref, face_ref, *rest):
    own_ref, out_ref, upper_ref, lower_ref, p_ref = rest[-5:]
    out_chunk = own_ref.shape[0] // 2
    n_pieces = m_ref.shape[2] // out_chunk
    s_refs, rhs_refs = rest[:n_pieces], rest[n_pieces:-5]
    pairs, n_axial, lanes = face_ref.shape
    slabs = out_ref.shape[0] + 1
    axial_all = p_ref.shape[1]
    rows = m_ref.shape[1]
    slab = place_ref[0]
    turns = pairs // slabs

    def place_rows(s_ref, first, count, start):
        upper, lower = split_bf16(s_ref[first : first + count, :])
        at = pl.ds(pl.multiple_of(start, count), count)
        upper_ref[at, :] = upper
        lower_ref[at, :] = lower

    for which, s_ref in enumerate(s_refs):
        start = place_ref[1 + which]
        if not by_source:
            place_rows(s_ref, 0, out_chunk, start)
            continue
        for source in range(slabs):
            for turn in range(turns):
                place_rows(
                    s_ref,
                    (source * turns + turn) * n_axial,
                    n_axial,
                    start + turn * axial_all + source * n_axial,
                )

    step = 2 * axial_all if axial_all < 128 else axial_all

    def block(index, carry):
        at = pl.ds(pl.multiple_of(index * step, step), step)
        real = m_ref[0, at, :]
        imag = m_ref[1, at, :]
        by_real = jnp.dot(real, upper_ref[...], preferred_element_type=F32)
        by_imag = jnp.dot(imag, upper_ref[...], preferred_element_type=F32)
        if split:
            by_real += jnp.dot(real, lower_ref[...], preferred_element_type=F32)
            by_imag += jnp.dot(imag, lower_ref[...], preferred_element_type=F32)
        here = pl.ds(index * (step // axial_all), step // axial_all)
        three = (step // axial_all, axial_all, HALF)
        p_ref[here, :, :HALF] = sign * (by_real[:, :HALF] - by_imag[:, HALF:]).reshape(three)
        p_ref[here, :, HALF:] = sign * (by_real[:, HALF:] + by_imag[:, :HALF]).reshape(three)
        return carry

    lax.fori_loop(0, rows // step, block, 0, unroll=True)
    own = pl.ds(pl.multiple_of(slab * n_axial, n_axial), n_axial)
    add = -sign * face_ref[...]
    for rhs_ref in rhs_refs:
        add = add + rhs_ref[...]
    p_ref[:, own, :] += add
    for shift in range(slabs):
        target = partner(slab, shift, slabs)
        part_ref = own_ref if shift == 0 else out_ref.at[shift - 1]
        for turn in range(turns):
            part_ref[turn * axial_all : (turn + 1) * axial_all, :] = p_ref[target + turn * slabs]
        there = pl.ds(pl.multiple_of(target * n_axial, n_axial), n_axial)
        part_ref[out_chunk:, :] = p_ref[:, there, :].reshape(out_chunk, lanes)


def bem_partial(sign, by_source, place, matrix, face, gathered, *rhs, split=True, after=()):
    pairs, n_axial, lanes = face.shape
    chunk = gathered[0].shape[0]
    rows, columns = matrix.shape[1:]
    axial_all = rows // pairs
    slabs = axial_all // n_axial
    return call(
        functools.partial(bem_kernel, sign, by_source, split),
        (shape(2 * chunk, lanes), shape(slabs - 1, 2 * chunk, lanes)),
        1,
        2 + len(gathered) + len(rhs),
        scratch=[
            pltpu.VMEM((columns, lanes), BF16),
            pltpu.VMEM((columns, lanes), BF16),
            pltpu.VMEM((pairs, axial_all, lanes), F32),
        ],
        name="bem_partial",
        after=after,
    )(place, matrix, face, *gathered, *rhs)


def surface_sums(u0, u1, u2):
    sums = (square_sums(u0),) + pair_sums(u0, u1) + (square_sums(u1),)
    return sums + pair_sums(u0, u2) + pair_sums(u1, u2) + (square_sums(u2),)


def gram_kernel(first_ref, second_ref, third_ref, s0_ref, s1_ref, s2_ref, out_ref):
    volume = (
        [first_ref[0]]
        + [second_ref[row] for row in range(3)]
        + [third_ref[row] for row in range(5)]
    )
    surface = surface_sums(s0_ref[...], s1_ref[...], s2_ref[...])
    for row, (one, two) in enumerate(zip(volume, surface)):
        total = jnp.sum(one, axis=0, keepdims=True) + jnp.sum(two, axis=0, keepdims=True)
        for device in range(out_ref.shape[0]):
            out_ref[device, :, row * HALF : (row + 1) * HALF] = total


def local_gram(devices, first, second, third, s0, s1, s2):
    tiles = [values.reshape(-1, 8, LANES) for values in (s0, s1, s2)]
    return call(gram_kernel, shape(devices, 1, 9 * HALF), 0, 6, name="local_gram")(
        first, second, third, *tiles
    )


def times(left, right):
    return (
        left[0] * right[0] - left[1] * right[1],
        left[0] * right[1] + left[1] * right[0],
    )


def conj_times(left, right):
    return (
        left[0] * right[0] + left[1] * right[1],
        left[0] * right[1] - left[1] * right[0],
    )


def square(value):
    return value[0] * value[0] + value[1] * value[1]


def coefficients(rows):
    g00, g11, g22 = rows[0], rows[3], rows[8]
    g01, g02, g12 = (rows[1], rows[2]), (rows[4], rows[5]), (rows[6], rows[7])
    beta_sq = g00 + EPSILON
    beta = jnp.sqrt(beta_sq)
    h00 = (g01[0] / beta_sq, g01[1] / beta_sq)
    h00_sq = square(h00)
    cross = conj_times(h00, g01)[0]
    rest = jnp.maximum(g11 - 2.0 * cross + h00_sq * g00, 0.0) / beta_sq
    h10_sq = rest + EPSILON
    h10 = jnp.sqrt(h10_sq)
    over_first = 1.0 / (beta_sq * h10)
    over_second = 1.0 / (beta_sq * h10_sq)
    h00_g01 = times(h00, g01)
    h01 = tuple((g02[k] - h00_g01[k]) * over_first for k in (0, 1))
    conj_g02 = conj_times(h00, g02)
    h11 = tuple(
        (g12[k] - h00[k] * g11 - conj_g02[k] + h00_sq * g01[k]) * over_second for k in (0, 1)
    )
    image_sq = (g22 - 2.0 * conj_times(h00, g12)[0] + h00_sq * g11) * over_second
    first_sq, second_sq = g00 / beta_sq, rest / h10_sq
    overlap = (h00[0] * EPSILON * over_first, h00[1] * EPSILON * over_first)
    mixed = conj_times(h01, times(h11, overlap))[0]
    bottom_sq = (
        jnp.maximum(
            image_sq
            - (2.0 - first_sq) * square(h01)
            - (2.0 - second_sq) * square(h11)
            + 2.0 * mixed,
            0.0,
        )
        + EPSILON
    )
    rho = jnp.sqrt(h00_sq + h10_sq)
    cos = (h00[0] / rho, h00[1] / rho)
    sine = h10 / rho
    top = conj_times(cos, h01)
    top = tuple(top[k] + sine * h11[k] for k in (0, 1))
    turn = times(cos, h11)
    turn = tuple(turn[k] - sine * h01[k] for k in (0, 1))
    lower = -sine * beta / (square(turn) + bottom_sq)
    one = (turn[0] * lower, -turn[1] * lower)
    top_one = times(top, one)
    zero = ((cos[0] * beta - top_one[0]) / rho, (-cos[1] * beta - top_one[1]) / rho)
    of_second = (one[0] / (beta * h10), one[1] / (beta * h10))
    back = times(of_second, h00)
    of_first = (zero[0] / beta - back[0], zero[1] / beta - back[1])
    return of_first, of_second


def combine(first, second, guess, u0, u1):
    u0_real, u0_imag = u0[..., :HALF], u0[..., HALF:]
    u1_real, u1_imag = u1[..., :HALF], u1[..., HALF:]
    real = guess[..., :HALF] + (first[0] * u0_real - first[1] * u0_imag)
    imag = guess[..., HALF:] + (first[0] * u0_imag + first[1] * u0_real)
    real = real + (second[0] * u1_real - second[1] * u1_imag)
    imag = imag + (second[0] * u1_imag + second[1] * u1_real)
    return real, imag


def solution_kernel(
    gram_ref, x_ref, u0_ref, u1_ref, s_ref, s0_ref, s1_ref,
    volume_ref, surface_ref, row_ref, stored,
):
    total = jnp.sum(gram_ref[...], axis=0)
    sums = [total[:, row * HALF : (row + 1) * HALF] for row in range(9)]
    first, second = coefficients(sums)
    n_theta = x_ref.shape[0]

    def store(a):
        return pltpu.make_async_copy(row_ref.at[a], volume_ref.at[a], stored.at[a])

    for a in range(n_theta):
        real, imag = combine(first, second, x_ref[a], u0_ref[a], u1_ref[a])
        row_ref[a, :, :, :HALF] = real
        row_ref[a, :, :, HALF:] = imag
        store(a).start()
    real, imag = combine(first, second, s_ref[...], s0_ref[...], s1_ref[...])
    surface_ref[..., :HALF] = real
    surface_ref[..., HALF:] = imag
    for a in range(n_theta):
        store(a).wait()


def final_solution(gram_all, x, u0, u1, s, s0, s1):
    return call(
        solution_kernel,
        (shape(*x.shape), shape(*s.shape)),
        0,
        7,
        scratch=[pltpu.VMEM(x.shape, F32), pltpu.SemaphoreType.DMA((x.shape[0],))],
        name="final_solution",
        out_specs=(ANYWHERE, WHOLE),
    )(gram_all, x, u0, u1, s, s0, s1)


def power_scale(bound):
    return 2.0 ** math.floor(math.log2(60000.0 / bound))


def to_wire(values, scale):
    return (values * scale).astype(WIRE)


def from_wire(values, scale):
    return values.astype(F32) * (1.0 / scale)


def partner(index, distance, peers):
    if peers & (peers - 1) == 0:
        return index ^ distance
    return lax.rem(index + distance, peers)


def partner_perm(peers, distance):
    if peers & (peers - 1) == 0:
        return [(i, i ^ distance) for i in range(peers)]
    return [(i, (i + distance) % peers) for i in range(peers)]


def slab_exchange(messages):
    slabs = lax.axis_size("slab")
    return [
        lax.ppermute(messages[distance], "slab", partner_perm(slabs, distance))
        for distance in range(1, slabs)
    ]


def neighbour_swap(axis, first, last, scale, wrap):
    peers = lax.axis_size(axis)
    odd = lax.rem(lax.axis_index(axis), 2) == 1
    first, last = to_wire(first, scale), to_wire(last, scale)
    within = [(i, i ^ 1) for i in range(peers)]
    across = [
        pair
        for i in range(1, peers if wrap else peers - 1, 2)
        for pair in ((i, (i + 1) % peers), ((i + 1) % peers, i))
    ]
    inner = lax.ppermute(jnp.where(odd, first, last), axis, within)
    outer = lax.ppermute(jnp.where(odd, last, first), axis, across)
    before = from_wire(jnp.where(odd, inner, outer), scale)
    beyond = from_wire(jnp.where(odd, outer, inner), scale)
    return before, beyond


def theta_halos(layers, scale):
    return neighbour_swap("sector", *layers[:2], scale, True)


def axial_halos(layers, scale):
    return neighbour_swap("slab", *layers[2:], scale, False)


def edge_layers(volume):
    return volume[0], volume[-1], volume[:, 0], volume[:, -1]


def sibling_perm():
    return [(i, i ^ 1) for i in range(lax.axis_size("sector"))]


def sector_gather(own, scale):
    sectors = lax.axis_size("sector")
    shares = [own]
    for distance in range(1, sectors // 2):
        perm = [
            (2 * i + core, 2 * j + core)
            for i, j in partner_perm(sectors // 2, distance)
            for core in range(2)
        ]
        shares.append(lax.ppermute(own, "sector", perm))
    gathered = []
    for share in shares:
        gathered += [share, lax.ppermute(share, "sector", sibling_perm())]
    return [from_wire(share, scale) for share in gathered]


def gather_places(chunk):
    chips = lax.axis_size("sector") // 2
    sector = lax.axis_index("sector")
    chip, core = sector // 2, lax.rem(sector, 2)
    places = [lax.axis_index("slab")]
    for distance in range(chips):
        mutual = chips & (chips - 1) == 0
        source = chip ^ distance if mutual else lax.rem(chip - distance + chips, chips)
        places += [(2 * source + core) * chunk, (2 * source + 1 - core) * chunk]
    return jnp.stack([jnp.asarray(value, jnp.int32) for value in places])


def first_gather(surface, scale):
    sectors, slabs = lax.axis_size("sector"), lax.axis_size("slab")
    chips = sectors // 2
    pairs, n_axial, lanes = surface.shape
    turns = pairs // slabs
    by_owner = to_wire(surface, scale).reshape(turns, slabs, n_axial, lanes)
    by_owner = jnp.swapaxes(by_owner, 0, 1).reshape(1, slabs, turns * n_axial, lanes)
    messages = jnp.broadcast_to(by_owner, (chips,) + by_owner.shape[1:])
    groups = [
        [(2 * chip + core) * slabs + slab for chip in range(chips) for slab in range(slabs)]
        for core in range(2)
    ]
    mine = lax.all_to_all(
        messages.reshape(chips * slabs, turns * n_axial, lanes),
        ("sector", "slab"),
        split_axis=0,
        concat_axis=0,
        axis_index_groups=groups,
        tiled=True,
    )
    other = lax.ppermute(mine, "sector", sibling_perm())
    mine, other = (
        from_wire(values, scale).reshape(chips, slabs * turns * n_axial, lanes)
        for values in (mine, other)
    )
    return [values[chip] for chip in range(chips) for values in (mine, other)]


def first_places(chunk):
    sectors = lax.axis_size("sector")
    core = lax.rem(lax.axis_index("sector"), 2)
    places = [lax.axis_index("slab")]
    for chip in range(sectors // 2):
        places += [(2 * chip + core) * chunk, (2 * chip + 1 - core) * chunk]
    return jnp.stack([jnp.asarray(value, jnp.int32) for value in places])


def scatter(parts, scale):
    messages = [None] + [to_wire(parts[which], scale) for which in range(parts.shape[0])]
    meanwhile = lax.ppermute(messages[1][:16, :HALF], "sector", sibling_perm())
    return slab_exchange(messages), meanwhile.astype(F32)


def scatter_sum(own, received, scale):
    for message in received:
        own = own + from_wire(message, scale)
    return own


def per_device(
    volume_rhs, surface_rhs, volume_guess, surface_guess, bem_matrix, stiffness, mass_shift
):
    slabs, sectors = lax.axis_size("slab"), lax.axis_size("sector")
    slab = lax.axis_index("slab")
    n_theta, n_axial, radial, lanes = volume_guess.shape
    pairs = surface_guess.shape[0]
    axial_all = n_axial * slabs
    turns = pairs // slabs
    chunk = turns * axial_all
    unknowns = sectors * pairs * axial_all

    gain = 8.0 * math.sqrt(unknowns)
    stiff = 3 * (3.0 + 7 * 1.05) + 6 + 3.0
    surface_0 = 6.0
    volume_0 = 6.0
    surface_1 = gain * surface_0 + 12.0
    volume_1 = 80.0 + stiff * volume_0 + surface_0
    surface_2 = gain * surface_1 + volume_1
    volume_2 = stiff * volume_1 + surface_1
    scale_s = [power_scale(bound) for bound in (surface_0, surface_1, surface_2)]
    scale_v = [power_scale(bound) for bound in (volume_0, volume_1, volume_2)]
    scale_p = [
        power_scale(gain / slabs * surface_0 + 12.0),
        power_scale(gain / slabs * surface_1 + volume_1),
        power_scale(gain / slabs * surface_2 + volume_2),
    ]

    place = gather_places(chunk)

    def surface_parts(total):
        return total[:chunk], total[chunk:].reshape(pairs, n_axial, lanes)

    gathered = first_gather(surface_guess, scale_s[0])
    mass = jnp.broadcast_to(mass_shift[..., None], mass_shift.shape + (HALF,))
    wide, narrow = volume_matrices(stiffness, n_theta, radial)
    layers, face = volume_edges(volume_guess)
    halos = theta_halos(layers, scale_v[0]) + axial_halos(layers, scale_v[0])
    own, parts = bem_partial(
        -1.0, True, first_places(chunk), bem_matrix, face, gathered, surface_rhs
    )
    received, meanwhile = scatter(parts, scale_p[0])
    bulk, own, guess = volume_bulk(
        volume_guess, mass, wide, narrow, own, copied=True, after=(meanwhile,)
    )
    u0, face, first = finish(
        finish_first_kernel, 1, True, bulk, surface_guess, halos, volume_rhs
    )
    theta = theta_halos(edge_layers(u0), scale_v[1])
    bulk, own = volume_bulk(u0, mass, wide, narrow, own)
    s0_owner, s0 = surface_parts(scatter_sum(own, received, scale_p[0]))

    gathered = sector_gather(to_wire(s0_owner, scale_s[1]), scale_s[1])
    u0 = pass_after(u0, gathered[1])
    halos = theta + axial_halos(edge_layers(u0), scale_v[1])
    own, parts = bem_partial(1.0, False, place, bem_matrix, face, gathered)
    received, meanwhile = scatter(parts, scale_p[1])
    u1, face, second = finish(
        finish_second_kernel, 3, True, bulk, s0, halos, u0, after=(meanwhile,)
    )
    theta = theta_halos(edge_layers(u1), scale_v[2])
    bulk, own = volume_bulk(u1, mass, wide, narrow, own)
    s1_owner, s1 = surface_parts(scatter_sum(own, received, scale_p[1]))

    gathered = sector_gather(to_wire(s1_owner, scale_s[2]), scale_s[2])
    u1 = pass_after(u1, gathered[1])
    halos = theta + axial_halos(edge_layers(u1), scale_v[2])
    own, parts = bem_partial(1.0, False, place, bem_matrix, face, gathered, split=False)
    received, meanwhile = scatter(parts[:, :chunk], scale_p[2])
    (third,) = finish(
        finish_third_kernel, 5, False, bulk, s1, halos, u0, u1, after=(meanwhile,)
    )
    total = scatter_sum(own[:chunk], received, scale_p[2])

    gram = local_gram(sectors * slabs, first, second, third, s0_owner, s1_owner, total)
    gram_all = lax.all_to_all(gram, ("sector", "slab"), split_axis=0, concat_axis=0, tiled=True)
    return final_solution(gram_all, guess, u0, u1, surface_guess, s0, s1)


def solution(mesh):
    return jax.shard_map(
        per_device,
        mesh=mesh,
        in_specs=(
            P("sector", "slab", None, None),
            P("sector", "slab", None),
            P("sector", "slab", None, None),
            P("sector", "slab", None),
            P(None, "sector", "slab"),
            P(),
            P("sector", "slab", None),
        ),
        out_specs=(P("sector", "slab", None, None), P("sector", "slab", None)),
        check_vma=False,
    )
```

```python
import functools
import math

import jax
import jax.numpy as jnp
from jax import lax
from jax.experimental import pallas as pl
from jax.experimental.pallas import tpu as pltpu
from jax.sharding import PartitionSpec as P

PENALTY = 1.0
EPSILON = 1e-06
F32 = jnp.float32
BF16 = jnp.bfloat16
WIRE = jnp.float16
LANES = 256
HALF = 128
VMEM_LIMIT = 8 * 1024 * 1024
WHOLE = pl.BlockSpec(memory_space=pltpu.VMEM)
SCALARS = pl.BlockSpec(memory_space=pltpu.SMEM)
ANYWHERE = pl.BlockSpec(memory_space=pl.ANY)


def call(
    kernel, out_shape, n_scalars, n_arrays, n_anywhere=0, scratch=(), name=None, after=(), out_specs=None, aliases=None, vmem=VMEM_LIMIT,
):
    n_read = n_scalars + n_arrays + n_anywhere

    def body(*refs):
        kernel(*refs[:n_read], *refs[n_read + len(after) :])

    called = pl.pallas_call(
        body,
        out_shape=out_shape,
        in_specs=[SCALARS] * n_scalars
        + [WHOLE] * n_arrays
        + [ANYWHERE] * (n_anywhere + len(after)),
        out_specs=out_specs or jax.tree.map(lambda _: WHOLE, out_shape),
        scratch_shapes=list(scratch),
        input_output_aliases=aliases or {},
        compiler_params=pltpu.CompilerParams(vmem_limit_bytes=vmem),
        cost_estimate=pl.CostEstimate(flops=1000, bytes_accessed=1000, transcendentals=0),
        name=name,
    )
    return lambda *args: called(*args, *after)


def shape(*dims):
    return jax.ShapeDtypeStruct(dims, F32)


def split_bf16(values):
    upper = values.astype(BF16)
    lower = (values - upper.astype(F32)).astype(BF16)
    return upper, lower


def one_hot(rows, columns, pick):
    row = lax.broadcasted_iota(jnp.int32, (rows, columns), 0)
    column = lax.broadcasted_iota(jnp.int32, (rows, columns), 1)
    return (pick(row) == column).astype(F32)


def line_matrix(stiffness, order, nodes, rows, fast):
    select = one_hot(rows, order, lambda row: (row // fast) % order)
    spread = jnp.dot(select, stiffness, precision=lax.Precision.HIGHEST)
    full = lax.dot_general(
        spread, select, (((1,), (1,)), ((), ())), precision=lax.Precision.HIGHEST
    )
    row = lax.broadcasted_iota(jnp.int32, (rows, rows), 0)
    column = lax.broadcasted_iota(jnp.int32, (rows, rows), 1)
    row_node, column_node = row // fast, column // fast
    same_fast = row % fast == column % fast
    same_element = (row_node // order == column_node // order) & same_fast
    block = jnp.where(same_element, full, 0.0)
    edge = (row_node % order == 0) | (row_node % order == order - 1)
    block = block + jnp.where((row == column) & edge, PENALTY, 0.0)
    back = (row_node % order == 0) & (column_node == row_node - 1) & same_fast
    ahead = (row_node % order == order - 1) & (column_node == row_node + 1) & same_fast
    return block - jnp.where(back | ahead, PENALTY, 0.0)


def matrices_kernel(nodes, radial, stiffness_ref, wide_ref, narrow_ref):
    order = stiffness_ref.shape[1]
    rows = nodes * radial
    theta = line_matrix(stiffness_ref[0], order, nodes, rows, radial)
    axial = line_matrix(stiffness_ref[1], order, nodes, rows, radial)
    select = one_hot(rows, order, lambda row: row % radial)
    spread = jnp.dot(select, stiffness_ref[2], precision=lax.Precision.HIGHEST)
    full = lax.dot_general(
        spread, select, (((1,), (1,)), ((), ())), precision=lax.Precision.HIGHEST
    )
    row = lax.broadcasted_iota(jnp.int32, (rows, rows), 0)
    column = lax.broadcasted_iota(jnp.int32, (rows, rows), 1)
    axial = axial + jnp.where(row // radial == column // radial, full, 0.0)
    edge = (row % radial == 0) | (row % radial == radial - 1)
    axial = axial + jnp.where((row == column) & edge, PENALTY, 0.0)
    for index, matrix in enumerate((theta, axial)):
        upper, lower = split_bf16(matrix)
        wide_ref[index, :, :rows] = upper
        wide_ref[index, :, rows:] = upper
        narrow_ref[index] = lower


def volume_matrices(stiffness, nodes, radial, after=()):
    rows = nodes * radial
    return call(
        functools.partial(matrices_kernel, nodes, radial),
        (
            jax.ShapeDtypeStruct((2, rows, 2 * rows), BF16),
            jax.ShapeDtypeStruct((2, rows, rows), BF16),
        ),
        0,
        1,
        name="volume_matrices",
        after=after,
    )(stiffness)


def bulk_kernel(
    x_ref, mass_ref, wide_ref, narrow_ref, own_ref, y_ref, passed_ref, *copy_refs
):
    n_theta, n_axial, radial, lanes = x_ref.shape

    def product(index, values):
        upper, lower = split_bf16(values)
        both = jnp.concatenate([upper, lower], axis=0)
        return jnp.dot(wide_ref[index], both, preferred_element_type=F32) + jnp.dot(
            narrow_ref[index], upper, preferred_element_type=F32
        )

    def along_theta(z, carry):
        values = x_ref[:, z].reshape(n_theta * radial, lanes)
        y_ref[:, z] = product(0, values).reshape(n_theta, radial, lanes)
        return carry

    def along_axial(a, carry):
        values = x_ref[a].reshape(n_axial * radial, lanes)
        total = product(1, values).reshape(n_axial, radial, lanes)
        mass = mass_ref[a]
        old = y_ref[a] + total
        x = x_ref[a]
        y_ref[a, :, :, :HALF] = old[:, :, :HALF] + mass * x[:, :, :HALF]
        y_ref[a, :, :, HALF:] = old[:, :, HALF:] + mass * x[:, :, HALF:]
        return carry

    lax.fori_loop(0, n_axial, along_theta, 0, unroll=True)
    lax.fori_loop(0, n_theta, along_axial, 0, unroll=True)
    for copy_ref in copy_refs:
        copy_ref[...] = x_ref[...]


def volume_bulk(x, mass, wide, narrow, own, copied=False, after=()):
    outs = (shape(*x.shape), shape(*own.shape)) + ((shape(*x.shape),) if copied else ())
    return call(
        bulk_kernel,
        outs,
        0,
        5,
        name="volume_bulk",
        aliases={4: 1},
        after=after,
    )(x, mass, wide, narrow, own)


def edges_kernel(
    x_ref, first_ref, last_ref, axial_first_ref, axial_last_ref, face_ref, outer_ref, copied
):
    n_theta, n_axial, radial, _ = x_ref.shape
    copies = [
        pltpu.make_async_copy(source, target, copied.at[index])
        for index, (source, target) in enumerate(
            (
                (x_ref.at[0], first_ref),
                (x_ref.at[n_theta - 1], last_ref),
                (x_ref.at[:, 0], axial_first_ref),
                (x_ref.at[:, n_axial - 1], axial_last_ref),
                (x_ref.at[:, :, radial - 1], outer_ref),
            )
        )
    ]
    for copy in copies:
        copy.start()
    for copy in copies:
        copy.wait()
    for pair in range(face_ref.shape[0]):
        face_ref[pair] = 0.5 * (outer_ref[2 * pair] + outer_ref[2 * pair + 1])


def volume_edges(x):
    n_theta, n_axial, radial, lanes = x.shape
    theta, axial = shape(n_axial, radial, lanes), shape(n_theta, radial, lanes)
    *layers, face = call(
        edges_kernel,
        (theta, theta, axial, axial, shape(n_theta // 2, n_axial, lanes)),
        0,
        0,
        1,
        scratch=[
            pltpu.VMEM((n_theta, n_axial, lanes), F32),
            pltpu.SemaphoreType.DMA((5,)),
        ],
        name="volume_edges",
    )(x)
    return layers, face


def pass_after(values, *earlier):
    return call(
        lambda values_ref, out_ref: None,
        shape(*values.shape),
        0,
        1,
        name="pass_after",
        after=earlier,
        aliases={0: 0},
    )(values)


def pair_sums(left, right):
    left_real, left_imag = left[..., :HALF], left[..., HALF:]
    right_real, right_imag = right[..., :HALF], right[..., HALF:]
    return (
        jnp.sum(left_real * right_real + left_imag * right_imag, axis=0),
        jnp.sum(left_real * right_imag - left_imag * right_real, axis=0),
    )


def square_sums(values):
    squares = values * values
    return jnp.sum(squares[..., :HALF] + squares[..., HALF:], axis=0)


def finish_row(a, bulk, s_ref, before_ref, beyond_ref, axial_before_ref, axial_beyond_ref, n_theta):
    n_axial, radial, lanes = bulk.shape
    if isinstance(a, int) and a == 0:
        bulk = bulk - before_ref[...]
    if isinstance(a, int) and a == n_theta - 1:
        bulk = bulk - beyond_ref[...]
    outer = lax.broadcasted_iota(jnp.int32, (radial, lanes), 0) == radial - 1
    tiles = []
    for z in range(n_axial):
        tile = bulk[z]
        if z == 0:
            tile = tile - axial_before_ref[a]
        if z == n_axial - 1:
            tile = tile - axial_beyond_ref[a]
        face = jnp.broadcast_to(s_ref[a // 2, z : z + 1, :], (radial, lanes))
        tiles.append(tile + jnp.where(outer, face, 0.0))
    return jnp.stack(tiles)


def over_rows(n_theta, body):
    body(0)
    lax.fori_loop(1, n_theta - 1, lambda a, carry: (body(a), carry)[1], 0)
    body(n_theta - 1)


def put_faces(u_ref, face_ref):
    radial = u_ref.shape[2]
    for pair in range(face_ref.shape[0]):
        face_ref[pair] = 0.5 * (
            u_ref[2 * pair, :, radial - 1, :] + u_ref[2 * pair + 1, :, radial - 1, :]
        )


def finish_first_kernel(
    bulk_ref, s_ref, before_ref, beyond_ref, ax_before_ref, ax_beyond_ref, rhs_ref,
    u_ref, face_ref, sums_ref,
):
    n_theta = bulk_ref.shape[0]
    sums_ref[...] = jnp.zeros_like(sums_ref)

    def body(a):
        image = finish_row(
            a, bulk_ref[a], s_ref, before_ref, beyond_ref, ax_before_ref, ax_beyond_ref, n_theta
        )
        u = rhs_ref[a] - image
        u_ref[a] = u
        sums_ref[0] += square_sums(u)

    over_rows(n_theta, body)
    put_faces(u_ref, face_ref)


def finish_second_kernel(
    bulk_ref, s_ref, before_ref, beyond_ref, ax_before_ref, ax_beyond_ref, u0_ref,
    u_ref, face_ref, sums_ref,
):
    n_theta = bulk_ref.shape[0]
    sums_ref[...] = jnp.zeros_like(sums_ref)

    def body(a):
        u = finish_row(
            a, bulk_ref[a], s_ref, before_ref, beyond_ref, ax_before_ref, ax_beyond_ref, n_theta
        )
        u_ref[a] = u
        real, imag = pair_sums(u0_ref[a], u)
        sums_ref[0] += real
        sums_ref[1] += imag
        sums_ref[2] += square_sums(u)

    over_rows(n_theta, body)
    put_faces(u_ref, face_ref)


def finish_third_kernel(
    bulk_ref, s_ref, before_ref, beyond_ref, ax_before_ref, ax_beyond_ref, u0_ref, u1_ref,
    sums_ref,
):
    n_theta = bulk_ref.shape[0]
    sums_ref[...] = jnp.zeros_like(sums_ref)

    def body(a):
        u = finish_row(
            a, bulk_ref[a], s_ref, before_ref, beyond_ref, ax_before_ref, ax_beyond_ref, n_theta
        )
        real, imag = pair_sums(u0_ref[a], u)
        sums_ref[0] += real
        sums_ref[1] += imag
        real, imag = pair_sums(u1_ref[a], u)
        sums_ref[2] += real
        sums_ref[3] += imag
        sums_ref[4] += square_sums(u)

    over_rows(n_theta, body)


def finish(kernel, n_sums, with_result, bulk, s, halos, *others, after=()):
    n_theta, n_axial, radial, lanes = bulk.shape
    outs = (shape(n_sums, radial, HALF),)
    if with_result:
        outs = (shape(*bulk.shape), shape(n_theta // 2, n_axial, lanes)) + outs
    return call(
        kernel,
        outs,
        0,
        6 + len(others),
        name=kernel.__name__,
        after=after,
    )(bulk, s, *halos, *others)


def bem_kernel(sign, by_source, split, place_ref, m_ref, face_ref, *rest):
    own_ref, out_ref, upper_ref, lower_ref, p_ref = rest[-5:]
    out_chunk = own_ref.shape[0] // 2
    n_pieces = m_ref.shape[2] // out_chunk
    s_refs, rhs_refs = rest[:n_pieces], rest[n_pieces:-5]
    pairs, n_axial, lanes = face_ref.shape
    slabs = out_ref.shape[0] + 1
    axial_all = p_ref.shape[1]
    rows = m_ref.shape[1]
    slab = place_ref[0]
    turns = pairs // slabs

    def place_rows(s_ref, first, count, start):
        upper, lower = split_bf16(s_ref[first : first + count, :])
        at = pl.ds(pl.multiple_of(start, count), count)
        upper_ref[at, :] = upper
        lower_ref[at, :] = lower

    for which, s_ref in enumerate(s_refs):
        start = place_ref[1 + which]
        if not by_source:
            place_rows(s_ref, 0, out_chunk, start)
            continue
        for source in range(slabs):
            for turn in range(turns):
                place_rows(
                    s_ref,
                    (source * turns + turn) * n_axial,
                    n_axial,
                    start + turn * axial_all + source * n_axial,
                )

    step = 2 * axial_all if axial_all < 128 else axial_all

    def block(index, carry):
        at = pl.ds(pl.multiple_of(index * step, step), step)
        real = m_ref[0, at, :]
        imag = m_ref[1, at, :]
        by_real = jnp.dot(real, upper_ref[...], preferred_element_type=F32)
        by_imag = jnp.dot(imag, upper_ref[...], preferred_element_type=F32)
        if split:
            by_real += jnp.dot(real, lower_ref[...], preferred_element_type=F32)
            by_imag += jnp.dot(imag, lower_ref[...], preferred_element_type=F32)
        here = pl.ds(index * (step // axial_all), step // axial_all)
        three = (step // axial_all, axial_all, HALF)
        p_ref[here, :, :HALF] = sign * (by_real[:, :HALF] - by_imag[:, HALF:]).reshape(three)
        p_ref[here, :, HALF:] = sign * (by_real[:, HALF:] + by_imag[:, :HALF]).reshape(three)
        return carry

    lax.fori_loop(0, rows // step, block, 0, unroll=True)
    own = pl.ds(pl.multiple_of(slab * n_axial, n_axial), n_axial)
    add = -sign * face_ref[...]
    for rhs_ref in rhs_refs:
        add = add + rhs_ref[...]
    p_ref[:, own, :] += add
    for shift in range(slabs):
        target = partner(slab, shift, slabs)
        part_ref = own_ref if shift == 0 else out_ref.at[shift - 1]
        for turn in range(turns):
            part_ref[turn * axial_all : (turn + 1) * axial_all, :] = p_ref[target + turn * slabs]
        there = pl.ds(pl.multiple_of(target * n_axial, n_axial), n_axial)
        part_ref[out_chunk:, :] = p_ref[:, there, :].reshape(out_chunk, lanes)


def bem_partial(sign, by_source, place, matrix, face, gathered, *rhs, split=True, after=()):
    pairs, n_axial, lanes = face.shape
    chunk = gathered[0].shape[0]
    rows, columns = matrix.shape[1:]
    axial_all = rows // pairs
    slabs = axial_all // n_axial
    return call(
        functools.partial(bem_kernel, sign, by_source, split),
        (shape(2 * chunk, lanes), shape(slabs - 1, 2 * chunk, lanes)),
        1,
        2 + len(gathered) + len(rhs),
        scratch=[
            pltpu.VMEM((columns, lanes), BF16),
            pltpu.VMEM((columns, lanes), BF16),
            pltpu.VMEM((pairs, axial_all, lanes), F32),
        ],
        name="bem_partial",
        after=after,
    )(place, matrix, face, *gathered, *rhs)


def surface_sums(u0, u1, u2):
    sums = (square_sums(u0),) + pair_sums(u0, u1) + (square_sums(u1),)
    return sums + pair_sums(u0, u2) + pair_sums(u1, u2) + (square_sums(u2),)


def gram_kernel(first_ref, second_ref, third_ref, s0_ref, s1_ref, s2_ref, out_ref):
    volume = (
        [first_ref[0]]
        + [second_ref[row] for row in range(3)]
        + [third_ref[row] for row in range(5)]
    )
    surface = surface_sums(s0_ref[...], s1_ref[...], s2_ref[...])
    for row, (one, two) in enumerate(zip(volume, surface)):
        total = jnp.sum(one, axis=0, keepdims=True) + jnp.sum(two, axis=0, keepdims=True)
        for device in range(out_ref.shape[0]):
            out_ref[device, :, row * HALF : (row + 1) * HALF] = total


def local_gram(devices, first, second, third, s0, s1, s2):
    tiles = [values.reshape(-1, 8, LANES) for values in (s0, s1, s2)]
    return call(gram_kernel, shape(devices, 1, 9 * HALF), 0, 6, name="local_gram")(
        first, second, third, *tiles
    )


def times(left, right):
    return (
        left[0] * right[0] - left[1] * right[1],
        left[0] * right[1] + left[1] * right[0],
    )


def conj_times(left, right):
    return (
        left[0] * right[0] + left[1] * right[1],
        left[0] * right[1] - left[1] * right[0],
    )


def square(value):
    return value[0] * value[0] + value[1] * value[1]


def coefficients(rows):
    g00, g11, g22 = rows[0], rows[3], rows[8]
    g01, g02, g12 = (rows[1], rows[2]), (rows[4], rows[5]), (rows[6], rows[7])
    beta_sq = g00 + EPSILON
    beta = jnp.sqrt(beta_sq)
    h00 = (g01[0] / beta_sq, g01[1] / beta_sq)
    h00_sq = square(h00)
    cross = conj_times(h00, g01)[0]
    rest = jnp.maximum(g11 - 2.0 * cross + h00_sq * g00, 0.0) / beta_sq
    h10_sq = rest + EPSILON
    h10 = jnp.sqrt(h10_sq)
    over_first = 1.0 / (beta_sq * h10)
    over_second = 1.0 / (beta_sq * h10_sq)
    h00_g01 = times(h00, g01)
    h01 = tuple((g02[k] - h00_g01[k]) * over_first for k in (0, 1))
    conj_g02 = conj_times(h00, g02)
    h11 = tuple(
        (g12[k] - h00[k] * g11 - conj_g02[k] + h00_sq * g01[k]) * over_second for k in (0, 1)
    )
    image_sq = (g22 - 2.0 * conj_times(h00, g12)[0] + h00_sq * g11) * over_second
    first_sq, second_sq = g00 / beta_sq, rest / h10_sq
    overlap = (h00[0] * EPSILON * over_first, h00[1] * EPSILON * over_first)
    mixed = conj_times(h01, times(h11, overlap))[0]
    bottom_sq = (
        jnp.maximum(
            image_sq
            - (2.0 - first_sq) * square(h01)
            - (2.0 - second_sq) * square(h11)
            + 2.0 * mixed,
            0.0,
        )
        + EPSILON
    )
    rho = jnp.sqrt(h00_sq + h10_sq)
    cos = (h00[0] / rho, h00[1] / rho)
    sine = h10 / rho
    top = conj_times(cos, h01)
    top = tuple(top[k] + sine * h11[k] for k in (0, 1))
    turn = times(cos, h11)
    turn = tuple(turn[k] - sine * h01[k] for k in (0, 1))
    lower = -sine * beta / (square(turn) + bottom_sq)
    one = (turn[0] * lower, -turn[1] * lower)
    top_one = times(top, one)
    zero = ((cos[0] * beta - top_one[0]) / rho, (-cos[1] * beta - top_one[1]) / rho)
    of_second = (one[0] / (beta * h10), one[1] / (beta * h10))
    back = times(of_second, h00)
    of_first = (zero[0] / beta - back[0], zero[1] / beta - back[1])
    return of_first, of_second


def combine(first, second, guess, u0, u1):
    u0_real, u0_imag = u0[..., :HALF], u0[..., HALF:]
    u1_real, u1_imag = u1[..., :HALF], u1[..., HALF:]
    real = guess[..., :HALF] + (first[0] * u0_real - first[1] * u0_imag)
    imag = guess[..., HALF:] + (first[0] * u0_imag + first[1] * u0_real)
    real = real + (second[0] * u1_real - second[1] * u1_imag)
    imag = imag + (second[0] * u1_imag + second[1] * u1_real)
    return real, imag


def solution_kernel(
    gram_ref, x_ref, u0_ref, u1_ref, s_ref, s0_ref, s1_ref,
    volume_ref, surface_ref, row_ref, stored,
):
    total = jnp.sum(gram_ref[...], axis=0)
    sums = [total[:, row * HALF : (row + 1) * HALF] for row in range(9)]
    first, second = coefficients(sums)
    n_theta = x_ref.shape[0]

    def store(a):
        return pltpu.make_async_copy(row_ref.at[a], volume_ref.at[a], stored.at[a])

    for a in range(n_theta):
        real, imag = combine(first, second, x_ref[a], u0_ref[a], u1_ref[a])
        row_ref[a, :, :, :HALF] = real
        row_ref[a, :, :, HALF:] = imag
        store(a).start()
    real, imag = combine(first, second, s_ref[...], s0_ref[...], s1_ref[...])
    surface_ref[..., :HALF] = real
    surface_ref[..., HALF:] = imag
    for a in range(n_theta):
        store(a).wait()


def final_solution(gram_all, x, u0, u1, s, s0, s1):
    return call(
        solution_kernel,
        (shape(*x.shape), shape(*s.shape)),
        0,
        7,
        scratch=[pltpu.VMEM(x.shape, F32), pltpu.SemaphoreType.DMA((x.shape[0],))],
        name="final_solution",
        out_specs=(ANYWHERE, WHOLE),
    )(gram_all, x, u0, u1, s, s0, s1)


def power_scale(bound):
    return 2.0 ** math.floor(math.log2(60000.0 / bound))


def to_wire(values, scale):
    return (values * scale).astype(WIRE)


def from_wire(values, scale):
    return values.astype(F32) * (1.0 / scale)


def partner(index, distance, peers):
    if peers & (peers - 1) == 0:
        return index ^ distance
    return lax.rem(index + distance, peers)


def partner_perm(peers, distance):
    if peers & (peers - 1) == 0:
        return [(i, i ^ distance) for i in range(peers)]
    return [(i, (i + distance) % peers) for i in range(peers)]


def slab_exchange(messages):
    slabs = lax.axis_size("slab")
    return [
        lax.ppermute(messages[distance], "slab", partner_perm(slabs, distance))
        for distance in range(1, slabs)
    ]


def neighbour_swap(axis, first, last, scale, wrap):
    peers = lax.axis_size(axis)
    odd = lax.rem(lax.axis_index(axis), 2) == 1
    first, last = to_wire(first, scale), to_wire(last, scale)
    within = [(i, i ^ 1) for i in range(peers)]
    across = [
        pair
        for i in range(1, peers if wrap else peers - 1, 2)
        for pair in ((i, (i + 1) % peers), ((i + 1) % peers, i))
    ]
    inner = lax.ppermute(jnp.where(odd, first, last), axis, within)
    outer = lax.ppermute(jnp.where(odd, last, first), axis, across)
    before = from_wire(jnp.where(odd, inner, outer), scale)
    beyond = from_wire(jnp.where(odd, outer, inner), scale)
    return before, beyond


def theta_halos(layers, scale):
    return neighbour_swap("sector", *layers[:2], scale, True)


def axial_halos(layers, scale):
    return neighbour_swap("slab", *layers[2:], scale, False)


def edge_layers(volume):
    return volume[0], volume[-1], volume[:, 0], volume[:, -1]


def sibling_perm():
    return [(i, i ^ 1) for i in range(lax.axis_size("sector"))]


def sector_gather(own, scale):
    sectors = lax.axis_size("sector")
    shares = [own]
    for distance in range(1, sectors // 2):
        perm = [
            (2 * i + core, 2 * j + core)
            for i, j in [(i, (i + distance) % (sectors // 2)) for i in range(sectors // 2)]
            for core in range(2)
        ]
        shares.append(lax.ppermute(own, "sector", perm))
    gathered = []
    for share in shares:
        gathered += [share, lax.ppermute(share, "sector", sibling_perm())]
    return [from_wire(share, scale) for share in gathered]


def gather_places(chunk):
    chips = lax.axis_size("sector") // 2
    sector = lax.axis_index("sector")
    chip, core = sector // 2, lax.rem(sector, 2)
    places = [lax.axis_index("slab")]
    for distance in range(chips):
        mutual = False
        source = chip ^ distance if mutual else lax.rem(chip - distance + chips, chips)
        places += [(2 * source + core) * chunk, (2 * source + 1 - core) * chunk]
    return jnp.stack([jnp.asarray(value, jnp.int32) for value in places])


def first_gather(surface, scale):
    sectors, slabs = lax.axis_size("sector"), lax.axis_size("slab")
    chips = sectors // 2
    pairs, n_axial, lanes = surface.shape
    turns = pairs // slabs
    by_owner = to_wire(surface, scale).reshape(turns, slabs, n_axial, lanes)
    by_owner = jnp.swapaxes(by_owner, 0, 1).reshape(1, slabs, turns * n_axial, lanes)
    messages = jnp.broadcast_to(by_owner, (chips,) + by_owner.shape[1:])
    groups = [
        [(2 * chip + core) * slabs + slab for chip in range(chips) for slab in range(slabs)]
        for core in range(2)
    ]
    mine = lax.all_to_all(
        messages.reshape(chips * slabs, turns * n_axial, lanes),
        ("sector", "slab"),
        split_axis=0,
        concat_axis=0,
        axis_index_groups=groups,
        tiled=True,
    )
    other = lax.ppermute(mine, "sector", sibling_perm())
    mine, other = (
        from_wire(values, scale).reshape(chips, slabs * turns * n_axial, lanes)
        for values in (mine, other)
    )
    return [values[chip] for chip in range(chips) for values in (mine, other)]


def first_places(chunk):
    sectors = lax.axis_size("sector")
    core = lax.rem(lax.axis_index("sector"), 2)
    places = [lax.axis_index("slab")]
    for chip in range(sectors // 2):
        places += [(2 * chip + core) * chunk, (2 * chip + 1 - core) * chunk]
    return jnp.stack([jnp.asarray(value, jnp.int32) for value in places])


def scatter(parts, scale):
    messages = [None] + [to_wire(parts[which], scale) for which in range(parts.shape[0])]
    meanwhile = lax.ppermute(messages[1][:16, :HALF], "sector", sibling_perm())
    return slab_exchange(messages), meanwhile.astype(F32)


def scatter_sum(own, received, scale):
    for message in received:
        own = own + from_wire(message, scale)
    return own


def per_device(
    volume_rhs, surface_rhs, volume_guess, surface_guess, bem_matrix, stiffness, mass_shift
):
    slabs, sectors = lax.axis_size("slab"), lax.axis_size("sector")
    slab = lax.axis_index("slab")
    n_theta, n_axial, radial, lanes = volume_guess.shape
    pairs = surface_guess.shape[0]
    axial_all = n_axial * slabs
    turns = pairs // slabs
    chunk = turns * axial_all
    unknowns = sectors * pairs * axial_all

    gain = 8.0 * math.sqrt(unknowns)
    stiff = 3 * (3.0 + 7 * 1.05) + 6 + 3.0
    surface_0 = 6.0
    volume_0 = 6.0
    surface_1 = gain * surface_0 + 12.0
    volume_1 = 80.0 + stiff * volume_0 + surface_0
    surface_2 = gain * surface_1 + volume_1
    volume_2 = stiff * volume_1 + surface_1
    scale_s = [power_scale(bound) for bound in (surface_0, surface_1, surface_2)]
    scale_v = [power_scale(bound) for bound in (volume_0, volume_1, volume_2)]
    scale_p = [
        power_scale(gain / slabs * surface_0 + 12.0),
        power_scale(gain / slabs * surface_1 + volume_1),
        power_scale(gain / slabs * surface_2 + volume_2),
    ]

    place = gather_places(chunk)

    def surface_parts(total):
        return total[:chunk], total[chunk:].reshape(pairs, n_axial, lanes)

    gathered = first_gather(surface_guess, scale_s[0])
    mass = jnp.broadcast_to(mass_shift[..., None], mass_shift.shape + (HALF,))
    layers, face = volume_edges(volume_guess)
    halos = theta_halos(layers, scale_v[0]) + axial_halos(layers, scale_v[0])
    own, parts = bem_partial(
        -1.0, True, first_places(chunk), bem_matrix, face, gathered, surface_rhs
    )
    received, meanwhile = scatter(parts, scale_p[0])
    wide, narrow = volume_matrices(stiffness, n_theta, radial, after=(meanwhile,))
    bulk, own, guess = volume_bulk(
        volume_guess, mass, wide, narrow, own, copied=True, after=(meanwhile,)
    )
    u0, face, first = finish(
        finish_first_kernel, 1, True, bulk, surface_guess, halos, volume_rhs
    )
    theta = theta_halos(edge_layers(u0), scale_v[1])
    bulk, own = volume_bulk(u0, mass, wide, narrow, own)
    s0_owner, s0 = surface_parts(scatter_sum(own, received, scale_p[0]))

    gathered = sector_gather(to_wire(s0_owner, scale_s[1]), scale_s[1])
    u0 = pass_after(u0, gathered[1])
    halos = theta + axial_halos(edge_layers(u0), scale_v[1])
    own, parts = bem_partial(1.0, False, place, bem_matrix, face, gathered)
    received, meanwhile = scatter(parts, scale_p[1])
    u1, face, second = finish(
        finish_second_kernel, 3, True, bulk, s0, halos, u0, after=(meanwhile,)
    )
    theta = theta_halos(edge_layers(u1), scale_v[2])
    bulk, own = volume_bulk(u1, mass, wide, narrow, own)
    s1_owner, s1 = surface_parts(scatter_sum(own, received, scale_p[1]))

    gathered = sector_gather(to_wire(s1_owner, scale_s[2]), scale_s[2])
    u1 = pass_after(u1, gathered[1])
    halos = theta + axial_halos(edge_layers(u1), scale_v[2])
    own, parts = bem_partial(1.0, False, place, bem_matrix, face, gathered, split=False)
    received, meanwhile = scatter(parts[:, :chunk], scale_p[2])
    (third,) = finish(
        finish_third_kernel, 5, False, bulk, s1, halos, u0, u1, after=(meanwhile,)
    )
    total = scatter_sum(own[:chunk], received, scale_p[2])

    gram = local_gram(sectors * slabs, first, second, third, s0_owner, s1_owner, total)
    gram_all = lax.all_to_all(gram, ("sector", "slab"), split_axis=0, concat_axis=0, tiled=True)
    return final_solution(gram_all, guess, u0, u1, surface_guess, s0, s1)


def solution(mesh):
    return jax.shard_map(
        per_device,
        mesh=mesh,
        in_specs=(
            P("sector", "slab", None, None),
            P("sector", "slab", None),
            P("sector", "slab", None, None),
            P("sector", "slab", None),
            P(None, "sector", "slab"),
            P(),
            P("sector", "slab", None),
        ),
        out_specs=(P("sector", "slab", None, None), P("sector", "slab", None)),
        check_vma=False,
    )
```

```python
import functools
import math

import jax
import jax.numpy as jnp
from jax import lax
from jax.experimental import pallas as pl
from jax.experimental.pallas import tpu as pltpu
from jax.sharding import PartitionSpec as P

PENALTY = 1.0
EPSILON = 1e-06
F32 = jnp.float32
BF16 = jnp.bfloat16
WIRE = jnp.float16
LANES = 256
HALF = 128
VMEM_LIMIT = 8 * 1024 * 1024
WHOLE = pl.BlockSpec(memory_space=pltpu.VMEM)
SCALARS = pl.BlockSpec(memory_space=pltpu.SMEM)
ANYWHERE = pl.BlockSpec(memory_space=pl.ANY)


def call(
    kernel, out_shape, n_scalars, n_arrays, n_anywhere=0, scratch=(), name=None, after=(), out_specs=None, aliases=None, vmem=VMEM_LIMIT,
):
    n_read = n_scalars + n_arrays + n_anywhere

    def body(*refs):
        kernel(*refs[:n_read], *refs[n_read + len(after) :])

    called = pl.pallas_call(
        body,
        out_shape=out_shape,
        in_specs=[SCALARS] * n_scalars
        + [WHOLE] * n_arrays
        + [ANYWHERE] * (n_anywhere + len(after)),
        out_specs=out_specs or jax.tree.map(lambda _: WHOLE, out_shape),
        scratch_shapes=list(scratch),
        input_output_aliases=aliases or {},
        compiler_params=pltpu.CompilerParams(vmem_limit_bytes=vmem),
        cost_estimate=pl.CostEstimate(flops=1000, bytes_accessed=1000, transcendentals=0),
        name=name,
    )
    return lambda *args: called(*args, *after)


def shape(*dims):
    return jax.ShapeDtypeStruct(dims, F32)


def split_bf16(values):
    upper = values.astype(BF16)
    lower = (values - upper.astype(F32)).astype(BF16)
    return upper, lower


def one_hot(rows, columns, pick):
    row = lax.broadcasted_iota(jnp.int32, (rows, columns), 0)
    column = lax.broadcasted_iota(jnp.int32, (rows, columns), 1)
    return (pick(row) == column).astype(F32)


def line_matrix(stiffness, order, nodes, rows, fast):
    select = one_hot(rows, order, lambda row: (row // fast) % order)
    spread = jnp.dot(select, stiffness, precision=lax.Precision.HIGHEST)
    full = lax.dot_general(
        spread, select, (((1,), (1,)), ((), ())), precision=lax.Precision.HIGHEST
    )
    row = lax.broadcasted_iota(jnp.int32, (rows, rows), 0)
    column = lax.broadcasted_iota(jnp.int32, (rows, rows), 1)
    row_node, column_node = row // fast, column // fast
    same_fast = row % fast == column % fast
    same_element = (row_node // order == column_node // order) & same_fast
    block = jnp.where(same_element, full, 0.0)
    edge = (row_node % order == 0) | (row_node % order == order - 1)
    block = block + jnp.where((row == column) & edge, PENALTY, 0.0)
    back = (row_node % order == 0) & (column_node == row_node - 1) & same_fast
    ahead = (row_node % order == order - 1) & (column_node == row_node + 1) & same_fast
    return block - jnp.where(back | ahead, PENALTY, 0.0)


def matrices_kernel(nodes, radial, stiffness_ref, wide_ref, narrow_ref):
    order = stiffness_ref.shape[1]
    rows = nodes * radial
    theta = line_matrix(stiffness_ref[0], order, nodes, rows, radial)
    axial = line_matrix(stiffness_ref[1], order, nodes, rows, radial)
    select = one_hot(rows, order, lambda row: row % radial)
    spread = jnp.dot(select, stiffness_ref[2], precision=lax.Precision.HIGHEST)
    full = lax.dot_general(
        spread, select, (((1,), (1,)), ((), ())), precision=lax.Precision.HIGHEST
    )
    row = lax.broadcasted_iota(jnp.int32, (rows, rows), 0)
    column = lax.broadcasted_iota(jnp.int32, (rows, rows), 1)
    axial = axial + jnp.where(row // radial == column // radial, full, 0.0)
    edge = (row % radial == 0) | (row % radial == radial - 1)
    axial = axial + jnp.where((row == column) & edge, PENALTY, 0.0)
    for index, matrix in enumerate((theta, axial)):
        upper, lower = split_bf16(matrix)
        wide_ref[index, :, :rows] = upper
        wide_ref[index, :, rows:] = upper
        narrow_ref[index] = lower


def volume_matrices(stiffness, nodes, radial, after=()):
    rows = nodes * radial
    return call(
        functools.partial(matrices_kernel, nodes, radial),
        (
            jax.ShapeDtypeStruct((2, rows, 2 * rows), BF16),
            jax.ShapeDtypeStruct((2, rows, rows), BF16),
        ),
        0,
        1,
        name="volume_matrices",
        after=after,
    )(stiffness)


def bulk_kernel(
    x_ref, mass_ref, wide_ref, narrow_ref, own_ref, y_ref, passed_ref, *copy_refs
):
    n_theta, n_axial, radial, lanes = x_ref.shape

    def product(index, values):
        upper, lower = split_bf16(values)
        both = jnp.concatenate([upper, lower], axis=0)
        return jnp.dot(wide_ref[index], both, preferred_element_type=F32) + jnp.dot(
            narrow_ref[index], upper, preferred_element_type=F32
        )

    def along_theta(z, carry):
        values = x_ref[:, z].reshape(n_theta * radial, lanes)
        y_ref[:, z] = product(0, values).reshape(n_theta, radial, lanes)
        return carry

    def along_axial(a, carry):
        values = x_ref[a].reshape(n_axial * radial, lanes)
        total = product(1, values).reshape(n_axial, radial, lanes)
        mass = mass_ref[a]
        old = y_ref[a] + total
        x = x_ref[a]
        y_ref[a, :, :, :HALF] = old[:, :, :HALF] + mass * x[:, :, :HALF]
        y_ref[a, :, :, HALF:] = old[:, :, HALF:] + mass * x[:, :, HALF:]
        return carry

    lax.fori_loop(0, n_axial, along_theta, 0, unroll=True)
    lax.fori_loop(0, n_theta, along_axial, 0, unroll=True)
    for copy_ref in copy_refs:
        copy_ref[...] = x_ref[...]


def volume_bulk(x, mass, wide, narrow, own, copied=False, after=()):
    outs = (shape(*x.shape), shape(*own.shape)) + ((shape(*x.shape),) if copied else ())
    return call(
        bulk_kernel,
        outs,
        0,
        5,
        name="volume_bulk",
        aliases={4: 1},
        after=after,
    )(x, mass, wide, narrow, own)


def edges_kernel(
    x_ref, first_ref, last_ref, axial_first_ref, axial_last_ref, face_ref, outer_ref, copied
):
    n_theta, n_axial, radial, _ = x_ref.shape
    copies = [
        pltpu.make_async_copy(source, target, copied.at[index])
        for index, (source, target) in enumerate(
            (
                (x_ref.at[0], first_ref),
                (x_ref.at[n_theta - 1], last_ref),
                (x_ref.at[:, 0], axial_first_ref),
                (x_ref.at[:, n_axial - 1], axial_last_ref),
                (x_ref.at[:, :, radial - 1], outer_ref),
            )
        )
    ]
    for copy in copies:
        copy.start()
    for copy in copies:
        copy.wait()
    for pair in range(face_ref.shape[0]):
        face_ref[pair] = 0.5 * (outer_ref[2 * pair] + outer_ref[2 * pair + 1])


def volume_edges(x):
    n_theta, n_axial, radial, lanes = x.shape
    theta, axial = shape(n_axial, radial, lanes), shape(n_theta, radial, lanes)
    *layers, face = call(
        edges_kernel,
        (theta, theta, axial, axial, shape(n_theta // 2, n_axial, lanes)),
        0,
        0,
        1,
        scratch=[
            pltpu.VMEM((n_theta, n_axial, lanes), F32),
            pltpu.SemaphoreType.DMA((5,)),
        ],
        name="volume_edges",
    )(x)
    return layers, face


def pass_after(values, *earlier):
    return call(
        lambda values_ref, out_ref: None,
        shape(*values.shape),
        0,
        1,
        name="pass_after",
        after=earlier,
        aliases={0: 0},
    )(values)


def pair_sums(left, right):
    left_real, left_imag = left[..., :HALF], left[..., HALF:]
    right_real, right_imag = right[..., :HALF], right[..., HALF:]
    return (
        jnp.sum(left_real * right_real + left_imag * right_imag, axis=0),
        jnp.sum(left_real * right_imag - left_imag * right_real, axis=0),
    )


def square_sums(values):
    squares = values * values
    return jnp.sum(squares[..., :HALF] + squares[..., HALF:], axis=0)


def finish_row(a, bulk, s_ref, before_ref, beyond_ref, axial_before_ref, axial_beyond_ref, n_theta):
    n_axial, radial, lanes = bulk.shape
    if isinstance(a, int) and a == 0:
        bulk = bulk - before_ref[...]
    if isinstance(a, int) and a == n_theta - 1:
        bulk = bulk - beyond_ref[...]
    outer = lax.broadcasted_iota(jnp.int32, (radial, lanes), 0) == radial - 1
    tiles = []
    for z in range(n_axial):
        tile = bulk[z]
        if z == 0:
            tile = tile - axial_before_ref[a]
        if z == n_axial - 1:
            tile = tile - axial_beyond_ref[a]
        face = jnp.broadcast_to(s_ref[a // 2, z : z + 1, :], (radial, lanes))
        tiles.append(tile + jnp.where(outer, face, 0.0))
    return jnp.stack(tiles)


def over_rows(n_theta, body):
    body(0)
    lax.fori_loop(1, n_theta - 1, lambda a, carry: (body(a), carry)[1], 0)
    body(n_theta - 1)


def put_faces(u_ref, face_ref):
    radial = u_ref.shape[2]
    for pair in range(face_ref.shape[0]):
        face_ref[pair] = 0.5 * (
            u_ref[2 * pair, :, radial - 1, :] + u_ref[2 * pair + 1, :, radial - 1, :]
        )


def finish_first_kernel(
    bulk_ref, s_ref, before_ref, beyond_ref, ax_before_ref, ax_beyond_ref, rhs_ref,
    u_ref, face_ref, sums_ref,
):
    n_theta = bulk_ref.shape[0]
    sums_ref[...] = jnp.zeros_like(sums_ref)

    def body(a):
        image = finish_row(
            a, bulk_ref[a], s_ref, before_ref, beyond_ref, ax_before_ref, ax_beyond_ref, n_theta
        )
        u = rhs_ref[a] - image
        u_ref[a] = u
        sums_ref[0] += square_sums(u)

    over_rows(n_theta, body)
    put_faces(u_ref, face_ref)


def finish_second_kernel(
    bulk_ref, s_ref, before_ref, beyond_ref, ax_before_ref, ax_beyond_ref, u0_ref,
    u_ref, face_ref, sums_ref,
):
    n_theta = bulk_ref.shape[0]
    sums_ref[...] = jnp.zeros_like(sums_ref)

    def body(a):
        u = finish_row(
            a, bulk_ref[a], s_ref, before_ref, beyond_ref, ax_before_ref, ax_beyond_ref, n_theta
        )
        u_ref[a] = u
        real, imag = pair_sums(u0_ref[a], u)
        sums_ref[0] += real
        sums_ref[1] += imag
        sums_ref[2] += square_sums(u)

    over_rows(n_theta, body)
    put_faces(u_ref, face_ref)


def finish_third_kernel(
    bulk_ref, s_ref, before_ref, beyond_ref, ax_before_ref, ax_beyond_ref, u0_ref, u1_ref,
    sums_ref,
):
    n_theta = bulk_ref.shape[0]
    sums_ref[...] = jnp.zeros_like(sums_ref)

    def body(a):
        u = finish_row(
            a, bulk_ref[a], s_ref, before_ref, beyond_ref, ax_before_ref, ax_beyond_ref, n_theta
        )
        real, imag = pair_sums(u0_ref[a], u)
        sums_ref[0] += real
        sums_ref[1] += imag
        real, imag = pair_sums(u1_ref[a], u)
        sums_ref[2] += real
        sums_ref[3] += imag
        sums_ref[4] += square_sums(u)

    over_rows(n_theta, body)


def finish(kernel, n_sums, with_result, bulk, s, halos, *others, after=()):
    n_theta, n_axial, radial, lanes = bulk.shape
    outs = (shape(n_sums, radial, HALF),)
    if with_result:
        outs = (shape(*bulk.shape), shape(n_theta // 2, n_axial, lanes)) + outs
    return call(
        kernel,
        outs,
        0,
        6 + len(others),
        name=kernel.__name__,
        after=after,
    )(bulk, s, *halos, *others)


def bem_kernel(sign, by_source, split, place_ref, m_ref, face_ref, *rest):
    own_ref, out_ref, upper_ref, lower_ref, p_ref = rest[-5:]
    out_chunk = own_ref.shape[0] // 2
    n_pieces = m_ref.shape[2] // out_chunk
    s_refs, rhs_refs = rest[:n_pieces], rest[n_pieces:-5]
    pairs, n_axial, lanes = face_ref.shape
    slabs = out_ref.shape[0] + 1
    axial_all = p_ref.shape[1]
    rows = m_ref.shape[1]
    slab = place_ref[0]
    turns = pairs // slabs

    def place_rows(s_ref, first, count, start):
        upper, lower = split_bf16(s_ref[first : first + count, :])
        at = pl.ds(pl.multiple_of(start, count), count)
        upper_ref[at, :] = upper
        lower_ref[at, :] = lower

    for which, s_ref in enumerate(s_refs):
        start = place_ref[1 + which]
        if not by_source:
            place_rows(s_ref, 0, out_chunk, start)
            continue
        for source in range(slabs):
            for turn in range(turns):
                place_rows(
                    s_ref,
                    (source * turns + turn) * n_axial,
                    n_axial,
                    start + turn * axial_all + source * n_axial,
                )

    step = 2 * axial_all if axial_all < 128 else axial_all

    def block(index, carry):
        at = pl.ds(pl.multiple_of(index * step, step), step)
        real = m_ref[0, at, :]
        imag = m_ref[1, at, :]
        by_real = jnp.dot(real, upper_ref[...], preferred_element_type=F32)
        by_imag = jnp.dot(imag, upper_ref[...], preferred_element_type=F32)
        if split:
            by_real += jnp.dot(real, lower_ref[...], preferred_element_type=F32)
            by_imag += jnp.dot(imag, lower_ref[...], preferred_element_type=F32)
        here = pl.ds(index * (step // axial_all), step // axial_all)
        three = (step // axial_all, axial_all, HALF)
        p_ref[here, :, :HALF] = sign * (by_real[:, :HALF] - by_imag[:, HALF:]).reshape(three)
        p_ref[here, :, HALF:] = sign * (by_real[:, HALF:] + by_imag[:, :HALF]).reshape(three)
        return carry

    lax.fori_loop(0, rows // step, block, 0, unroll=True)
    own = pl.ds(pl.multiple_of(slab * n_axial, n_axial), n_axial)
    add = -sign * face_ref[...]
    for rhs_ref in rhs_refs:
        add = add + rhs_ref[...]
    p_ref[:, own, :] += add
    for shift in range(slabs):
        target = partner(slab, shift, slabs)
        part_ref = own_ref if shift == 0 else out_ref.at[shift - 1]
        for turn in range(turns):
            part_ref[turn * axial_all : (turn + 1) * axial_all, :] = p_ref[target + turn * slabs]
        there = pl.ds(pl.multiple_of(target * n_axial, n_axial), n_axial)
        part_ref[out_chunk:, :] = p_ref[:, there, :].reshape(out_chunk, lanes)


def bem_partial(sign, by_source, place, matrix, face, gathered, *rhs, split=True, after=()):
    pairs, n_axial, lanes = face.shape
    chunk = gathered[0].shape[0]
    rows, columns = matrix.shape[1:]
    axial_all = rows // pairs
    slabs = axial_all // n_axial
    return call(
        functools.partial(bem_kernel, sign, by_source, split),
        (shape(2 * chunk, lanes), shape(slabs - 1, 2 * chunk, lanes)),
        1,
        2 + len(gathered) + len(rhs),
        scratch=[
            pltpu.VMEM((columns, lanes), BF16),
            pltpu.VMEM((columns, lanes), BF16),
            pltpu.VMEM((pairs, axial_all, lanes), F32),
        ],
        name="bem_partial",
        after=after,
    )(place, matrix, face, *gathered, *rhs)


def surface_sums(u0, u1, u2):
    sums = (square_sums(u0),) + pair_sums(u0, u1) + (square_sums(u1),)
    return sums + pair_sums(u0, u2) + pair_sums(u1, u2) + (square_sums(u2),)


def gram_kernel(first_ref, second_ref, third_ref, s0_ref, s1_ref, s2_ref, out_ref):
    volume = (
        [first_ref[0]]
        + [second_ref[row] for row in range(3)]
        + [third_ref[row] for row in range(5)]
    )
    surface = surface_sums(s0_ref[...], s1_ref[...], s2_ref[...])
    for row, (one, two) in enumerate(zip(volume, surface)):
        total = jnp.sum(one, axis=0, keepdims=True) + jnp.sum(two, axis=0, keepdims=True)
        for device in range(out_ref.shape[0]):
            out_ref[device, :, row * HALF : (row + 1) * HALF] = total


def local_gram(devices, first, second, third, s0, s1, s2):
    tiles = [values.reshape(-1, 8, LANES) for values in (s0, s1, s2)]
    return call(gram_kernel, shape(devices, 1, 9 * HALF), 0, 6, name="local_gram")(
        first, second, third, *tiles
    )


def times(left, right):
    return (
        left[0] * right[0] - left[1] * right[1],
        left[0] * right[1] + left[1] * right[0],
    )


def conj_times(left, right):
    return (
        left[0] * right[0] + left[1] * right[1],
        left[0] * right[1] - left[1] * right[0],
    )


def square(value):
    return value[0] * value[0] + value[1] * value[1]


def coefficients(rows):
    g00, g11, g22 = rows[0], rows[3], rows[8]
    g01, g02, g12 = (rows[1], rows[2]), (rows[4], rows[5]), (rows[6], rows[7])
    beta_sq = g00 + EPSILON
    beta = jnp.sqrt(beta_sq)
    h00 = (g01[0] / beta_sq, g01[1] / beta_sq)
    h00_sq = square(h00)
    cross = conj_times(h00, g01)[0]
    rest = jnp.maximum(g11 - 2.0 * cross + h00_sq * g00, 0.0) / beta_sq
    h10_sq = rest + EPSILON
    h10 = jnp.sqrt(h10_sq)
    over_first = 1.0 / (beta_sq * h10)
    over_second = 1.0 / (beta_sq * h10_sq)
    h00_g01 = times(h00, g01)
    h01 = tuple((g02[k] - h00_g01[k]) * over_first for k in (0, 1))
    conj_g02 = conj_times(h00, g02)
    h11 = tuple(
        (g12[k] - h00[k] * g11 - conj_g02[k] + h00_sq * g01[k]) * over_second for k in (0, 1)
    )
    image_sq = (g22 - 2.0 * conj_times(h00, g12)[0] + h00_sq * g11) * over_second
    first_sq, second_sq = g00 / beta_sq, rest / h10_sq
    overlap = (h00[0] * EPSILON * over_first, h00[1] * EPSILON * over_first)
    mixed = conj_times(h01, times(h11, overlap))[0]
    bottom_sq = (
        jnp.maximum(
            image_sq
            - (2.0 - first_sq) * square(h01)
            - (2.0 - second_sq) * square(h11)
            + 2.0 * mixed,
            0.0,
        )
        + EPSILON
    )
    rho = jnp.sqrt(h00_sq + h10_sq)
    cos = (h00[0] / rho, h00[1] / rho)
    sine = h10 / rho
    top = conj_times(cos, h01)
    top = tuple(top[k] + sine * h11[k] for k in (0, 1))
    turn = times(cos, h11)
    turn = tuple(turn[k] - sine * h01[k] for k in (0, 1))
    lower = -sine * beta / (square(turn) + bottom_sq)
    one = (turn[0] * lower, -turn[1] * lower)
    top_one = times(top, one)
    zero = ((cos[0] * beta - top_one[0]) / rho, (-cos[1] * beta - top_one[1]) / rho)
    of_second = (one[0] / (beta * h10), one[1] / (beta * h10))
    back = times(of_second, h00)
    of_first = (zero[0] / beta - back[0], zero[1] / beta - back[1])
    return of_first, of_second


def combine(first, second, guess, u0, u1):
    u0_real, u0_imag = u0[..., :HALF], u0[..., HALF:]
    u1_real, u1_imag = u1[..., :HALF], u1[..., HALF:]
    real = guess[..., :HALF] + (first[0] * u0_real - first[1] * u0_imag)
    imag = guess[..., HALF:] + (first[0] * u0_imag + first[1] * u0_real)
    real = real + (second[0] * u1_real - second[1] * u1_imag)
    imag = imag + (second[0] * u1_imag + second[1] * u1_real)
    return real, imag


def solution_kernel(
    gram_ref, x_ref, u0_ref, u1_ref, s_ref, s0_ref, s1_ref,
    volume_ref, surface_ref, row_ref, stored,
):
    total = jnp.sum(gram_ref[...], axis=0)
    sums = [total[:, row * HALF : (row + 1) * HALF] for row in range(9)]
    first, second = coefficients(sums)
    n_theta = x_ref.shape[0]

    def store(a):
        return pltpu.make_async_copy(row_ref.at[a], volume_ref.at[a], stored.at[a])

    for a in range(n_theta):
        real, imag = combine(first, second, x_ref[a], u0_ref[a], u1_ref[a])
        row_ref[a, :, :, :HALF] = real
        row_ref[a, :, :, HALF:] = imag
        store(a).start()
    real, imag = combine(first, second, s_ref[...], s0_ref[...], s1_ref[...])
    surface_ref[..., :HALF] = real
    surface_ref[..., HALF:] = imag
    for a in range(n_theta):
        store(a).wait()


def final_solution(gram_all, x, u0, u1, s, s0, s1):
    return call(
        solution_kernel,
        (shape(*x.shape), shape(*s.shape)),
        0,
        7,
        scratch=[pltpu.VMEM(x.shape, F32), pltpu.SemaphoreType.DMA((x.shape[0],))],
        name="final_solution",
        out_specs=(ANYWHERE, WHOLE),
    )(gram_all, x, u0, u1, s, s0, s1)


def power_scale(bound):
    return 2.0 ** math.floor(math.log2(60000.0 / bound))


def to_wire(values, scale):
    return (values * scale).astype(WIRE)


def from_wire(values, scale):
    return values.astype(F32) * (1.0 / scale)


def partner(index, distance, peers):
    if peers & (peers - 1) == 0:
        return index ^ distance
    return lax.rem(index + distance, peers)


def partner_perm(peers, distance):
    if peers & (peers - 1) == 0:
        return [(i, i ^ distance) for i in range(peers)]
    return [(i, (i + distance) % peers) for i in range(peers)]


def slab_exchange(messages):
    slabs = lax.axis_size("slab")
    received = [
        lax.ppermute(messages[distance], "slab", partner_perm(slabs, distance))
        for distance in reversed(range(1, slabs))
    ]
    return received[::-1]


def neighbour_swap(axis, first, last, scale, wrap):
    peers = lax.axis_size(axis)
    odd = lax.rem(lax.axis_index(axis), 2) == 1
    first, last = to_wire(first, scale), to_wire(last, scale)
    within = [(i, i ^ 1) for i in range(peers)]
    across = [
        pair
        for i in range(1, peers if wrap else peers - 1, 2)
        for pair in ((i, (i + 1) % peers), ((i + 1) % peers, i))
    ]
    inner = lax.ppermute(jnp.where(odd, first, last), axis, within)
    outer = lax.ppermute(jnp.where(odd, last, first), axis, across)
    before = from_wire(jnp.where(odd, inner, outer), scale)
    beyond = from_wire(jnp.where(odd, outer, inner), scale)
    return before, beyond


def theta_halos(layers, scale):
    return neighbour_swap("sector", *layers[:2], scale, True)


def axial_halos(layers, scale):
    return neighbour_swap("slab", *layers[2:], scale, False)


def edge_layers(volume):
    return volume[0], volume[-1], volume[:, 0], volume[:, -1]


def sibling_perm():
    return [(i, i ^ 1) for i in range(lax.axis_size("sector"))]


def sector_gather(own, scale):
    sectors = lax.axis_size("sector")
    shares = [own]
    for distance in reversed(range(1, sectors // 2)):
        perm = [
            (2 * i + core, 2 * j + core)
            for i, j in [(i, (i + distance) % (sectors // 2)) for i in range(sectors // 2)]
            for core in range(2)
        ]
        shares.append(lax.ppermute(own, "sector", perm))
    gathered = []
    for share in shares:
        gathered += [share, lax.ppermute(share, "sector", sibling_perm())]
    return [from_wire(share, scale) for share in gathered]


def gather_places(chunk):
    chips = lax.axis_size("sector") // 2
    sector = lax.axis_index("sector")
    chip, core = sector // 2, lax.rem(sector, 2)
    places = [lax.axis_index("slab")]
    for distance in [0] + list(reversed(range(1, chips))):
        source = lax.rem(chip - distance + chips, chips)
        places += [(2 * source + core) * chunk, (2 * source + 1 - core) * chunk]
    return jnp.stack([jnp.asarray(value, jnp.int32) for value in places])


def first_gather(surface, scale):
    sectors, slabs = lax.axis_size("sector"), lax.axis_size("slab")
    chips = sectors // 2
    pairs, n_axial, lanes = surface.shape
    turns = pairs // slabs
    by_owner = to_wire(surface, scale).reshape(turns, slabs, n_axial, lanes)
    by_owner = jnp.swapaxes(by_owner, 0, 1).reshape(1, slabs, turns * n_axial, lanes)
    messages = jnp.broadcast_to(by_owner, (chips,) + by_owner.shape[1:])
    groups = [
        [(2 * chip + core) * slabs + slab for chip in range(chips) for slab in range(slabs)]
        for core in range(2)
    ]
    mine = lax.all_to_all(
        messages.reshape(chips * slabs, turns * n_axial, lanes),
        ("sector", "slab"),
        split_axis=0,
        concat_axis=0,
        axis_index_groups=groups,
        tiled=True,
    )
    other = lax.ppermute(mine, "sector", sibling_perm())
    mine, other = (
        from_wire(values, scale).reshape(chips, slabs * turns * n_axial, lanes)
        for values in (mine, other)
    )
    return [values[chip] for chip in range(chips) for values in (mine, other)]


def first_places(chunk):
    sectors = lax.axis_size("sector")
    core = lax.rem(lax.axis_index("sector"), 2)
    places = [lax.axis_index("slab")]
    for chip in range(sectors // 2):
        places += [(2 * chip + core) * chunk, (2 * chip + 1 - core) * chunk]
    return jnp.stack([jnp.asarray(value, jnp.int32) for value in places])


def scatter(parts, scale):
    messages = [None] + [to_wire(parts[which], scale) for which in range(parts.shape[0])]
    meanwhile = lax.ppermute(messages[-1][:16, :HALF], "sector", sibling_perm())
    return slab_exchange(messages), meanwhile.astype(F32)


def scatter_sum(own, received, scale):
    for message in received:
        own = own + from_wire(message, scale)
    return own


def per_device(
    volume_rhs, surface_rhs, volume_guess, surface_guess, bem_matrix, stiffness, mass_shift
):
    slabs, sectors = lax.axis_size("slab"), lax.axis_size("sector")
    slab = lax.axis_index("slab")
    n_theta, n_axial, radial, lanes = volume_guess.shape
    pairs = surface_guess.shape[0]
    axial_all = n_axial * slabs
    turns = pairs // slabs
    chunk = turns * axial_all
    unknowns = sectors * pairs * axial_all

    gain = 8.0 * math.sqrt(unknowns)
    stiff = 3 * stiffness.shape[1] * 3.0 + 6 + 3.0
    surface_0 = 6.0
    volume_0 = 6.0
    surface_1 = gain * surface_0 + 12.0
    volume_1 = 80.0 + stiff * volume_0 + surface_0
    surface_2 = gain * surface_1 + volume_1
    volume_2 = stiff * volume_1 + surface_1
    scale_s = [power_scale(bound) for bound in (surface_0, surface_1, surface_2)]
    scale_v = [power_scale(bound) for bound in (volume_0, volume_1, volume_2)]
    scale_p = [
        power_scale(gain / slabs * surface_0 + 12.0),
        power_scale(gain / slabs * surface_1 + volume_1),
        power_scale(gain / slabs * surface_2 + volume_2),
    ]

    place = gather_places(chunk)

    def surface_parts(total):
        return total[:chunk], total[chunk:].reshape(pairs, n_axial, lanes)

    gathered = first_gather(surface_guess, scale_s[0])
    mass = jnp.broadcast_to(mass_shift[..., None], mass_shift.shape + (HALF,))
    layers, face = volume_edges(volume_guess)
    halos = theta_halos(layers, scale_v[0]) + axial_halos(layers, scale_v[0])
    own, parts = bem_partial(
        -1.0, True, first_places(chunk), bem_matrix, face, gathered, surface_rhs
    )
    received, meanwhile = scatter(parts, scale_p[0])
    wide, narrow = volume_matrices(stiffness, n_theta, radial, after=(meanwhile,))
    bulk, own, guess = volume_bulk(
        volume_guess, mass, wide, narrow, own, copied=True, after=(meanwhile,)
    )
    u0, face, first = finish(
        finish_first_kernel, 1, True, bulk, surface_guess, halos, volume_rhs
    )
    theta = theta_halos(edge_layers(u0), scale_v[1])
    bulk, own = volume_bulk(u0, mass, wide, narrow, own)
    s0_owner, s0 = surface_parts(scatter_sum(own, received, scale_p[0]))

    gathered = sector_gather(to_wire(s0_owner, scale_s[1]), scale_s[1])
    u0 = pass_after(u0, gathered[1])
    halos = theta + axial_halos(edge_layers(u0), scale_v[1])
    own, parts = bem_partial(1.0, False, place, bem_matrix, face, gathered)
    received, meanwhile = scatter(parts, scale_p[1])
    u1, face, second = finish(
        finish_second_kernel, 3, True, bulk, s0, halos, u0, after=(meanwhile,)
    )
    theta = theta_halos(edge_layers(u1), scale_v[2])
    bulk, own = volume_bulk(u1, mass, wide, narrow, own)
    s1_owner, s1 = surface_parts(scatter_sum(own, received, scale_p[1]))

    gathered = sector_gather(to_wire(s1_owner, scale_s[2]), scale_s[2])
    u1 = pass_after(u1, gathered[1])
    halos = theta + axial_halos(edge_layers(u1), scale_v[2])
    own, parts = bem_partial(1.0, False, place, bem_matrix, face, gathered, split=False)
    received, meanwhile = scatter(parts[:, :chunk], scale_p[2])
    (third,) = finish(
        finish_third_kernel, 5, False, bulk, s1, halos, u0, u1, after=(meanwhile,)
    )
    total = scatter_sum(own[:chunk], received, scale_p[2])

    gram = local_gram(sectors * slabs, first, second, third, s0_owner, s1_owner, total)
    gram_all = lax.all_to_all(gram, ("sector", "slab"), split_axis=0, concat_axis=0, tiled=True)
    return final_solution(gram_all, guess, u0, u1, surface_guess, s0, s1)


def solution(mesh):
    return jax.shard_map(
        per_device,
        mesh=mesh,
        in_specs=(
            P("sector", "slab", None, None),
            P("sector", "slab", None),
            P("sector", "slab", None, None),
            P("sector", "slab", None),
            P(None, "sector", "slab"),
            P(),
            P("sector", "slab", None),
        ),
        out_specs=(P("sector", "slab", None, None), P("sector", "slab", None)),
        check_vma=False,
    )
```

```python
import functools
import math

import jax
import jax.numpy as jnp
from jax import lax
from jax.experimental import pallas as pl
from jax.experimental.pallas import tpu as pltpu
from jax.sharding import PartitionSpec as P

PENALTY = 1.0
EPSILON = 1e-06
F32 = jnp.float32
BF16 = jnp.bfloat16
WIRE = jnp.float16
LANES = 256
HALF = 128
VMEM_LIMIT = 8 * 1024 * 1024
WHOLE = pl.BlockSpec(memory_space=pltpu.VMEM)
SCALARS = pl.BlockSpec(memory_space=pltpu.SMEM)
ANYWHERE = pl.BlockSpec(memory_space=pl.ANY)


def call(
    kernel, out_shape, n_scalars, n_arrays, n_anywhere=0, scratch=(), name=None, after=(), out_specs=None, aliases=None, vmem=VMEM_LIMIT,
):
    n_read = n_scalars + n_arrays + n_anywhere

    def body(*refs):
        kernel(*refs[:n_read], *refs[n_read + len(after) :])

    called = pl.pallas_call(
        body,
        out_shape=out_shape,
        in_specs=[SCALARS] * n_scalars
        + [WHOLE] * n_arrays
        + [ANYWHERE] * (n_anywhere + len(after)),
        out_specs=out_specs or jax.tree.map(lambda _: WHOLE, out_shape),
        scratch_shapes=list(scratch),
        input_output_aliases=aliases or {},
        compiler_params=pltpu.CompilerParams(vmem_limit_bytes=vmem),
        cost_estimate=pl.CostEstimate(flops=1000, bytes_accessed=1000, transcendentals=0),
        name=name,
    )
    return lambda *args: called(*args, *after)


def shape(*dims):
    return jax.ShapeDtypeStruct(dims, F32)


def split_bf16(values):
    upper = values.astype(BF16)
    lower = (values - upper.astype(F32)).astype(BF16)
    return upper, lower


def one_hot(rows, columns, pick):
    row = lax.broadcasted_iota(jnp.int32, (rows, columns), 0)
    column = lax.broadcasted_iota(jnp.int32, (rows, columns), 1)
    return (pick(row) == column).astype(F32)


def line_matrix(stiffness, order, nodes, rows, fast):
    select = one_hot(rows, order, lambda row: (row // fast) % order)
    spread = jnp.dot(select, stiffness, precision=lax.Precision.HIGHEST)
    full = lax.dot_general(
        spread, select, (((1,), (1,)), ((), ())), precision=lax.Precision.HIGHEST
    )
    row = lax.broadcasted_iota(jnp.int32, (rows, rows), 0)
    column = lax.broadcasted_iota(jnp.int32, (rows, rows), 1)
    row_node, column_node = row // fast, column // fast
    same_fast = row % fast == column % fast
    same_element = (row_node // order == column_node // order) & same_fast
    block = jnp.where(same_element, full, 0.0)
    edge = (row_node % order == 0) | (row_node % order == order - 1)
    block = block + jnp.where((row == column) & edge, PENALTY, 0.0)
    back = (row_node % order == 0) & (column_node == row_node - 1) & same_fast
    ahead = (row_node % order == order - 1) & (column_node == row_node + 1) & same_fast
    return block - jnp.where(back | ahead, PENALTY, 0.0)


def matrices_kernel(nodes, radial, stiffness_ref, wide_ref, narrow_ref):
    order = stiffness_ref.shape[1]
    rows = nodes * radial
    theta = line_matrix(stiffness_ref[0], order, nodes, rows, radial)
    axial = line_matrix(stiffness_ref[1], order, nodes, rows, radial)
    select = one_hot(rows, order, lambda row: row % radial)
    spread = jnp.dot(select, stiffness_ref[2], precision=lax.Precision.HIGHEST)
    full = lax.dot_general(
        spread, select, (((1,), (1,)), ((), ())), precision=lax.Precision.HIGHEST
    )
    row = lax.broadcasted_iota(jnp.int32, (rows, rows), 0)
    column = lax.broadcasted_iota(jnp.int32, (rows, rows), 1)
    axial = axial + jnp.where(row // radial == column // radial, full, 0.0)
    edge = (row % radial == 0) | (row % radial == radial - 1)
    axial = axial + jnp.where((row == column) & edge, PENALTY, 0.0)
    for index, matrix in enumerate((theta, axial)):
        upper, lower = split_bf16(matrix)
        wide_ref[index, :, :rows] = upper
        wide_ref[index, :, rows:] = upper
        narrow_ref[index] = lower


def volume_matrices(stiffness, nodes, radial, after=()):
    rows = nodes * radial
    return call(
        functools.partial(matrices_kernel, nodes, radial),
        (
            jax.ShapeDtypeStruct((2, rows, 2 * rows), BF16),
            jax.ShapeDtypeStruct((2, rows, rows), BF16),
        ),
        0,
        1,
        name="volume_matrices",
        after=after,
    )(stiffness)


def bulk_kernel(
    x_ref, mass_ref, wide_ref, narrow_ref, own_ref, y_ref, passed_ref, *copy_refs
):
    n_theta, n_axial, radial, lanes = x_ref.shape

    def product(index, values):
        upper, lower = split_bf16(values)
        both = jnp.concatenate([upper, lower], axis=0)
        return jnp.dot(wide_ref[index], both, preferred_element_type=F32) + jnp.dot(
            narrow_ref[index], upper, preferred_element_type=F32
        )

    def along_theta(z, carry):
        values = x_ref[:, z].reshape(n_theta * radial, lanes)
        y_ref[:, z] = product(0, values).reshape(n_theta, radial, lanes)
        return carry

    def along_axial(a, carry):
        values = x_ref[a].reshape(n_axial * radial, lanes)
        total = product(1, values).reshape(n_axial, radial, lanes)
        mass = mass_ref[a]
        old = y_ref[a] + total
        x = x_ref[a]
        y_ref[a, :, :, :HALF] = old[:, :, :HALF] + mass * x[:, :, :HALF]
        y_ref[a, :, :, HALF:] = old[:, :, HALF:] + mass * x[:, :, HALF:]
        return carry

    lax.fori_loop(0, n_axial, along_theta, 0, unroll=True)
    lax.fori_loop(0, n_theta, along_axial, 0, unroll=True)
    for copy_ref in copy_refs:
        copy_ref[...] = x_ref[...]


def volume_bulk(x, mass, wide, narrow, own, copied=False, after=()):
    outs = (shape(*x.shape), shape(*own.shape)) + ((shape(*x.shape),) if copied else ())
    return call(
        bulk_kernel,
        outs,
        0,
        5,
        name="volume_bulk",
        aliases={4: 1},
        after=after,
    )(x, mass, wide, narrow, own)


def edges_kernel(
    x_ref, first_ref, last_ref, axial_first_ref, axial_last_ref, face_ref, outer_ref, copied
):
    n_theta, n_axial, radial, _ = x_ref.shape
    copies = [
        pltpu.make_async_copy(source, target, copied.at[index])
        for index, (source, target) in enumerate(
            (
                (x_ref.at[0], first_ref),
                (x_ref.at[n_theta - 1], last_ref),
                (x_ref.at[:, 0], axial_first_ref),
                (x_ref.at[:, n_axial - 1], axial_last_ref),
                (x_ref.at[:, :, radial - 1], outer_ref),
            )
        )
    ]
    for copy in copies:
        copy.start()
    for copy in copies:
        copy.wait()
    for pair in range(face_ref.shape[0]):
        face_ref[pair] = 0.5 * (outer_ref[2 * pair] + outer_ref[2 * pair + 1])


def volume_edges(x):
    n_theta, n_axial, radial, lanes = x.shape
    theta, axial = shape(n_axial, radial, lanes), shape(n_theta, radial, lanes)
    *layers, face = call(
        edges_kernel,
        (theta, theta, axial, axial, shape(n_theta // 2, n_axial, lanes)),
        0,
        0,
        1,
        scratch=[
            pltpu.VMEM((n_theta, n_axial, lanes), F32),
            pltpu.SemaphoreType.DMA((5,)),
        ],
        name="volume_edges",
    )(x)
    return layers, face


def pass_after(values, *earlier):
    return call(
        lambda values_ref, out_ref: None,
        shape(*values.shape),
        0,
        1,
        name="pass_after",
        after=earlier,
        aliases={0: 0},
    )(values)


def pair_sums(left, right):
    left_real, left_imag = left[..., :HALF], left[..., HALF:]
    right_real, right_imag = right[..., :HALF], right[..., HALF:]
    return (
        jnp.sum(left_real * right_real + left_imag * right_imag, axis=0),
        jnp.sum(left_real * right_imag - left_imag * right_real, axis=0),
    )


def square_sums(values):
    squares = values * values
    return jnp.sum(squares[..., :HALF] + squares[..., HALF:], axis=0)


def finish_row(a, bulk, s_ref, before_ref, beyond_ref, axial_before_ref, axial_beyond_ref, n_theta):
    n_axial, radial, lanes = bulk.shape
    if isinstance(a, int) and a == 0:
        bulk = bulk - before_ref[...]
    if isinstance(a, int) and a == n_theta - 1:
        bulk = bulk - beyond_ref[...]
    outer = lax.broadcasted_iota(jnp.int32, (radial, lanes), 0) == radial - 1
    tiles = []
    for z in range(n_axial):
        tile = bulk[z]
        if z == 0:
            tile = tile - axial_before_ref[a]
        if z == n_axial - 1:
            tile = tile - axial_beyond_ref[a]
        face = jnp.broadcast_to(s_ref[a // 2, z : z + 1, :], (radial, lanes))
        tiles.append(tile + jnp.where(outer, face, 0.0))
    return jnp.stack(tiles)


def over_rows(n_theta, body):
    body(0)
    lax.fori_loop(1, n_theta - 1, lambda a, carry: (body(a), carry)[1], 0)
    body(n_theta - 1)


def put_faces(u_ref, face_ref):
    radial = u_ref.shape[2]
    for pair in range(face_ref.shape[0]):
        face_ref[pair] = 0.5 * (
            u_ref[2 * pair, :, radial - 1, :] + u_ref[2 * pair + 1, :, radial - 1, :]
        )


def finish_first_kernel(
    bulk_ref, s_ref, before_ref, beyond_ref, ax_before_ref, ax_beyond_ref, rhs_ref,
    u_ref, face_ref, sums_ref,
):
    n_theta = bulk_ref.shape[0]
    sums_ref[...] = jnp.zeros_like(sums_ref)

    def body(a):
        image = finish_row(
            a, bulk_ref[a], s_ref, before_ref, beyond_ref, ax_before_ref, ax_beyond_ref, n_theta
        )
        u = rhs_ref[a] - image
        u_ref[a] = u
        sums_ref[0] += square_sums(u)

    over_rows(n_theta, body)
    put_faces(u_ref, face_ref)


def finish_second_kernel(
    bulk_ref, s_ref, before_ref, beyond_ref, ax_before_ref, ax_beyond_ref, u0_ref,
    u_ref, face_ref, sums_ref,
):
    n_theta = bulk_ref.shape[0]
    sums_ref[...] = jnp.zeros_like(sums_ref)

    def body(a):
        u = finish_row(
            a, bulk_ref[a], s_ref, before_ref, beyond_ref, ax_before_ref, ax_beyond_ref, n_theta
        )
        u_ref[a] = u
        real, imag = pair_sums(u0_ref[a], u)
        sums_ref[0] += real
        sums_ref[1] += imag
        sums_ref[2] += square_sums(u)

    over_rows(n_theta, body)
    put_faces(u_ref, face_ref)


def finish_third_kernel(
    bulk_ref, s_ref, before_ref, beyond_ref, ax_before_ref, ax_beyond_ref, u0_ref, u1_ref,
    sums_ref,
):
    n_theta = bulk_ref.shape[0]
    sums_ref[...] = jnp.zeros_like(sums_ref)

    def body(a):
        u = finish_row(
            a, bulk_ref[a], s_ref, before_ref, beyond_ref, ax_before_ref, ax_beyond_ref, n_theta
        )
        real, imag = pair_sums(u0_ref[a], u)
        sums_ref[0] += real
        sums_ref[1] += imag
        real, imag = pair_sums(u1_ref[a], u)
        sums_ref[2] += real
        sums_ref[3] += imag
        sums_ref[4] += square_sums(u)

    over_rows(n_theta, body)


def finish(kernel, n_sums, with_result, bulk, s, halos, *others, after=()):
    n_theta, n_axial, radial, lanes = bulk.shape
    outs = (shape(n_sums, radial, HALF),)
    if with_result:
        outs = (shape(*bulk.shape), shape(n_theta // 2, n_axial, lanes)) + outs
    return call(
        kernel,
        outs,
        0,
        6 + len(others),
        name=kernel.__name__,
        after=after,
    )(bulk, s, *halos, *others)


def bem_kernel(sign, by_source, split, place_ref, m_ref, face_ref, *rest):
    own_ref, out_ref, upper_ref, lower_ref, p_ref = rest[-5:]
    out_chunk = own_ref.shape[0] // 2
    n_pieces = m_ref.shape[2] // out_chunk
    s_refs, rhs_refs = rest[:n_pieces], rest[n_pieces:-5]
    pairs, n_axial, lanes = face_ref.shape
    slabs = out_ref.shape[0] + 1
    axial_all = p_ref.shape[1]
    rows = m_ref.shape[1]
    slab = place_ref[0]
    turns = pairs // slabs

    def place_rows(s_ref, first, count, start):
        upper, lower = split_bf16(s_ref[first : first + count, :])
        at = pl.ds(pl.multiple_of(start, count), count)
        upper_ref[at, :] = upper
        if split:
            lower_ref[at, :] = lower

    for which, s_ref in enumerate(s_refs):
        start = place_ref[1 + which]
        if not by_source:
            place_rows(s_ref, 0, out_chunk, start)
            continue
        for source in range(slabs):
            for turn in range(turns):
                place_rows(
                    s_ref,
                    (source * turns + turn) * n_axial,
                    n_axial,
                    start + turn * axial_all + source * n_axial,
                )

    step = 2 * axial_all if axial_all < 128 else axial_all

    def block(index, carry):
        at = pl.ds(pl.multiple_of(index * step, step), step)
        real = m_ref[0, at, :]
        imag = m_ref[1, at, :]
        by_real = jnp.dot(real, upper_ref[...], preferred_element_type=F32)
        by_imag = jnp.dot(imag, upper_ref[...], preferred_element_type=F32)
        if split:
            by_real += jnp.dot(real, lower_ref[...], preferred_element_type=F32)
            by_imag += jnp.dot(imag, lower_ref[...], preferred_element_type=F32)
        here = pl.ds(index * (step // axial_all), step // axial_all)
        three = (step // axial_all, axial_all, HALF)
        p_ref[here, :, :HALF] = sign * (by_real[:, :HALF] - by_imag[:, HALF:]).reshape(three)
        p_ref[here, :, HALF:] = sign * (by_real[:, HALF:] + by_imag[:, :HALF]).reshape(three)
        return carry

    lax.fori_loop(0, rows // step, block, 0, unroll=True)
    own = pl.ds(pl.multiple_of(slab * n_axial, n_axial), n_axial)
    add = -sign * face_ref[...]
    for rhs_ref in rhs_refs:
        add = add + rhs_ref[...]
    p_ref[:, own, :] += add
    for shift in range(slabs):
        target = partner(slab, shift, slabs)
        part_ref = own_ref if shift == 0 else out_ref.at[shift - 1]
        for turn in range(turns):
            part_ref[turn * axial_all : (turn + 1) * axial_all, :] = p_ref[target + turn * slabs]
        there = pl.ds(pl.multiple_of(target * n_axial, n_axial), n_axial)
        part_ref[out_chunk:, :] = p_ref[:, there, :].reshape(out_chunk, lanes)


def bem_partial(sign, by_source, place, matrix, face, gathered, *rhs, split=True, after=()):
    pairs, n_axial, lanes = face.shape
    chunk = gathered[0].shape[0]
    rows, columns = matrix.shape[1:]
    axial_all = rows // pairs
    slabs = axial_all // n_axial
    return call(
        functools.partial(bem_kernel, sign, by_source, split),
        (shape(2 * chunk, lanes), shape(slabs - 1, 2 * chunk, lanes)),
        1,
        2 + len(gathered) + len(rhs),
        scratch=[
            pltpu.VMEM((columns, lanes), BF16),
            pltpu.VMEM((columns, lanes), BF16),
            pltpu.VMEM((pairs, axial_all, lanes), F32),
        ],
        name="bem_partial",
        after=after,
    )(place, matrix, face, *gathered, *rhs)


def surface_sums(u0, u1, u2):
    sums = (square_sums(u0),) + pair_sums(u0, u1) + (square_sums(u1),)
    return sums + pair_sums(u0, u2) + pair_sums(u1, u2) + (square_sums(u2),)


def gram_kernel(first_ref, second_ref, third_ref, s0_ref, s1_ref, s2_ref, out_ref):
    volume = (
        [first_ref[0]]
        + [second_ref[row] for row in range(3)]
        + [third_ref[row] for row in range(5)]
    )
    surface = surface_sums(s0_ref[...], s1_ref[...], s2_ref[...])
    for row, (one, two) in enumerate(zip(volume, surface)):
        total = jnp.sum(one, axis=0, keepdims=True) + jnp.sum(two, axis=0, keepdims=True)
        for device in range(out_ref.shape[0]):
            out_ref[device, :, row * HALF : (row + 1) * HALF] = total


def local_gram(devices, first, second, third, s0, s1, s2):
    tiles = [values.reshape(-1, 8, LANES) for values in (s0, s1, s2)]
    return call(gram_kernel, shape(devices, 1, 9 * HALF), 0, 6, name="local_gram")(
        first, second, third, *tiles
    )


def times(left, right):
    return (
        left[0] * right[0] - left[1] * right[1],
        left[0] * right[1] + left[1] * right[0],
    )


def conj_times(left, right):
    return (
        left[0] * right[0] + left[1] * right[1],
        left[0] * right[1] - left[1] * right[0],
    )


def square(value):
    return value[0] * value[0] + value[1] * value[1]


def coefficients(rows):
    g00, g11, g22 = rows[0], rows[3], rows[8]
    g01, g02, g12 = (rows[1], rows[2]), (rows[4], rows[5]), (rows[6], rows[7])
    beta_sq = g00 + EPSILON
    beta = jnp.sqrt(beta_sq)
    h00 = (g01[0] / beta_sq, g01[1] / beta_sq)
    h00_sq = square(h00)
    cross = conj_times(h00, g01)[0]
    rest = jnp.maximum(g11 - 2.0 * cross + h00_sq * g00, 0.0) / beta_sq
    h10_sq = rest + EPSILON
    h10 = jnp.sqrt(h10_sq)
    over_first = 1.0 / (beta_sq * h10)
    over_second = 1.0 / (beta_sq * h10_sq)
    h00_g01 = times(h00, g01)
    h01 = tuple((g02[k] - h00_g01[k]) * over_first for k in (0, 1))
    conj_g02 = conj_times(h00, g02)
    h11 = tuple(
        (g12[k] - h00[k] * g11 - conj_g02[k] + h00_sq * g01[k]) * over_second for k in (0, 1)
    )
    image_sq = (g22 - 2.0 * conj_times(h00, g12)[0] + h00_sq * g11) * over_second
    first_sq, second_sq = g00 / beta_sq, rest / h10_sq
    overlap = (h00[0] * EPSILON * over_first, h00[1] * EPSILON * over_first)
    mixed = conj_times(h01, times(h11, overlap))[0]
    bottom_sq = (
        jnp.maximum(
            image_sq
            - (2.0 - first_sq) * square(h01)
            - (2.0 - second_sq) * square(h11)
            + 2.0 * mixed,
            0.0,
        )
        + EPSILON
    )
    rho = jnp.sqrt(h00_sq + h10_sq)
    cos = (h00[0] / rho, h00[1] / rho)
    sine = h10 / rho
    top = conj_times(cos, h01)
    top = tuple(top[k] + sine * h11[k] for k in (0, 1))
    turn = times(cos, h11)
    turn = tuple(turn[k] - sine * h01[k] for k in (0, 1))
    lower = -sine * beta / (square(turn) + bottom_sq)
    one = (turn[0] * lower, -turn[1] * lower)
    top_one = times(top, one)
    zero = ((cos[0] * beta - top_one[0]) / rho, (-cos[1] * beta - top_one[1]) / rho)
    of_second = (one[0] / (beta * h10), one[1] / (beta * h10))
    back = times(of_second, h00)
    of_first = (zero[0] / beta - back[0], zero[1] / beta - back[1])
    return of_first, of_second


def combine(first, second, guess, u0, u1):
    u0_real, u0_imag = u0[..., :HALF], u0[..., HALF:]
    u1_real, u1_imag = u1[..., :HALF], u1[..., HALF:]
    real = guess[..., :HALF] + (first[0] * u0_real - first[1] * u0_imag)
    imag = guess[..., HALF:] + (first[0] * u0_imag + first[1] * u0_real)
    real = real + (second[0] * u1_real - second[1] * u1_imag)
    imag = imag + (second[0] * u1_imag + second[1] * u1_real)
    return real, imag


def solution_kernel(
    gram_ref, x_ref, u0_ref, u1_ref, s_ref, s0_ref, s1_ref,
    volume_ref, surface_ref, row_ref, stored,
):
    total = jnp.sum(gram_ref[...], axis=0)
    sums = [total[:, row * HALF : (row + 1) * HALF] for row in range(9)]
    first, second = coefficients(sums)
    n_theta = x_ref.shape[0]

    def store(a):
        return pltpu.make_async_copy(row_ref.at[a], volume_ref.at[a], stored.at[a])

    for a in range(n_theta):
        real, imag = combine(first, second, x_ref[a], u0_ref[a], u1_ref[a])
        row_ref[a, :, :, :HALF] = real
        row_ref[a, :, :, HALF:] = imag
        store(a).start()
    real, imag = combine(first, second, s_ref[...], s0_ref[...], s1_ref[...])
    surface_ref[..., :HALF] = real
    surface_ref[..., HALF:] = imag
    for a in range(n_theta):
        store(a).wait()


def final_solution(gram_all, x, u0, u1, s, s0, s1):
    return call(
        solution_kernel,
        (shape(*x.shape), shape(*s.shape)),
        0,
        7,
        scratch=[pltpu.VMEM(x.shape, F32), pltpu.SemaphoreType.DMA((x.shape[0],))],
        name="final_solution",
        out_specs=(ANYWHERE, WHOLE),
    )(gram_all, x, u0, u1, s, s0, s1)


def power_scale(bound):
    return 2.0 ** math.floor(math.log2(60000.0 / bound))


def to_wire(values, scale):
    return (values * scale).astype(WIRE)


def from_wire(values, scale):
    return values.astype(F32) * (1.0 / scale)


def partner(index, distance, peers):
    if peers & (peers - 1) == 0:
        return index ^ distance
    return lax.rem(index + distance, peers)


def partner_perm(peers, distance):
    if peers & (peers - 1) == 0:
        return [(i, i ^ distance) for i in range(peers)]
    return [(i, (i + distance) % peers) for i in range(peers)]


def slab_exchange(messages):
    slabs = lax.axis_size("slab")
    received = [
        lax.ppermute(messages[distance], "slab", partner_perm(slabs, distance))
        for distance in reversed(range(1, slabs))
    ]
    return received[::-1]


def neighbour_swap(axis, first, last, scale, wrap):
    peers = lax.axis_size(axis)
    odd = lax.rem(lax.axis_index(axis), 2) == 1
    first, last = to_wire(first, scale), to_wire(last, scale)
    within = [(i, i ^ 1) for i in range(peers)]
    across = [
        pair
        for i in range(1, peers if wrap else peers - 1, 2)
        for pair in ((i, (i + 1) % peers), ((i + 1) % peers, i))
    ]
    inner = lax.ppermute(jnp.where(odd, first, last), axis, within)
    outer = lax.ppermute(jnp.where(odd, last, first), axis, across)
    before = from_wire(jnp.where(odd, inner, outer), scale)
    beyond = from_wire(jnp.where(odd, outer, inner), scale)
    return before, beyond


def theta_halos(layers, scale):
    return neighbour_swap("sector", *layers[:2], scale, True)


def axial_halos(layers, scale):
    return neighbour_swap("slab", *layers[2:], scale, False)


def edge_layers(volume):
    return volume[0], volume[-1], volume[:, 0], volume[:, -1]


def sibling_perm():
    return [(i, i ^ 1) for i in range(lax.axis_size("sector"))]


def sector_gather(own, scale):
    sectors = lax.axis_size("sector")
    shares = [own]
    for distance in reversed(range(1, sectors // 2)):
        perm = [
            (2 * i + core, 2 * j + core)
            for i, j in [(i, (i + distance) % (sectors // 2)) for i in range(sectors // 2)]
            for core in range(2)
        ]
        shares.append(lax.ppermute(own, "sector", perm))
    gathered = []
    for share in shares:
        gathered += [share, lax.ppermute(share, "sector", sibling_perm())]
    return [from_wire(share, scale) for share in gathered]


def gather_places(chunk):
    chips = lax.axis_size("sector") // 2
    sector = lax.axis_index("sector")
    chip, core = sector // 2, lax.rem(sector, 2)
    places = [lax.axis_index("slab")]
    for distance in [0] + list(reversed(range(1, chips))):
        source = lax.rem(chip - distance + chips, chips)
        places += [(2 * source + core) * chunk, (2 * source + 1 - core) * chunk]
    return jnp.stack([jnp.asarray(value, jnp.int32) for value in places])


def first_gather(surface, scale):
    sectors, slabs = lax.axis_size("sector"), lax.axis_size("slab")
    chips = sectors // 2
    pairs, n_axial, lanes = surface.shape
    turns = pairs // slabs
    by_owner = to_wire(surface, scale).reshape(turns, slabs, n_axial, lanes)
    by_owner = jnp.swapaxes(by_owner, 0, 1).reshape(1, slabs, turns * n_axial, lanes)
    messages = jnp.broadcast_to(by_owner, (chips,) + by_owner.shape[1:])
    groups = [
        [(2 * chip + core) * slabs + slab for chip in range(chips) for slab in range(slabs)]
        for core in range(2)
    ]
    mine = lax.all_to_all(
        messages.reshape(chips * slabs, turns * n_axial, lanes),
        ("sector", "slab"),
        split_axis=0,
        concat_axis=0,
        axis_index_groups=groups,
        tiled=True,
    )
    other = lax.ppermute(mine, "sector", sibling_perm())
    mine, other = (
        from_wire(values, scale).reshape(chips, slabs * turns * n_axial, lanes)
        for values in (mine, other)
    )
    return [values[chip] for chip in range(chips) for values in (mine, other)]


def first_places(chunk):
    sectors = lax.axis_size("sector")
    core = lax.rem(lax.axis_index("sector"), 2)
    places = [lax.axis_index("slab")]
    for chip in range(sectors // 2):
        places += [(2 * chip + core) * chunk, (2 * chip + 1 - core) * chunk]
    return jnp.stack([jnp.asarray(value, jnp.int32) for value in places])


def scatter(parts, scale):
    messages = [None] + [to_wire(parts[which], scale) for which in range(parts.shape[0])]
    meanwhile = lax.ppermute(messages[-1][:16, :HALF], "sector", sibling_perm())
    return slab_exchange(messages), meanwhile.astype(F32)


def scatter_sum(own, received, scale):
    for message in received:
        own = own + from_wire(message, scale)
    return own


def per_device(
    volume_rhs, surface_rhs, volume_guess, surface_guess, bem_matrix, stiffness, mass_shift
):
    slabs, sectors = lax.axis_size("slab"), lax.axis_size("sector")
    slab = lax.axis_index("slab")
    n_theta, n_axial, radial, lanes = volume_guess.shape
    pairs = surface_guess.shape[0]
    axial_all = n_axial * slabs
    turns = pairs // slabs
    chunk = turns * axial_all
    unknowns = sectors * pairs * axial_all

    gain = 8.0 * math.sqrt(unknowns)
    stiff = 3 * stiffness.shape[1] * 3.0 + 6 + 3.0
    surface_0 = 6.0
    volume_0 = 6.0
    surface_1 = gain * surface_0 + 12.0
    volume_1 = 80.0 + stiff * volume_0 + surface_0
    surface_2 = gain * surface_1 + volume_1
    volume_2 = stiff * volume_1 + surface_1
    scale_s = [power_scale(bound) for bound in (surface_0, surface_1, surface_2)]
    scale_v = [power_scale(bound) for bound in (volume_0, volume_1, volume_2)]
    scale_p = [
        power_scale(gain / slabs * surface_0 + 12.0),
        power_scale(gain / slabs * surface_1 + volume_1),
        power_scale(gain / slabs * surface_2 + volume_2),
    ]

    place = gather_places(chunk)

    def surface_parts(total):
        return total[:chunk], total[chunk:].reshape(pairs, n_axial, lanes)

    gathered = first_gather(surface_guess, scale_s[0])
    mass = jnp.broadcast_to(mass_shift[..., None], mass_shift.shape + (HALF,))
    wide, narrow = volume_matrices(stiffness, n_theta, radial, after=(gathered[0],))
    layers, face = volume_edges(volume_guess)
    halos = theta_halos(layers, scale_v[0]) + axial_halos(layers, scale_v[0])
    own, parts = bem_partial(
        -1.0, True, first_places(chunk), bem_matrix, face, gathered, surface_rhs,
        after=(narrow,),
    )
    received, meanwhile = scatter(parts, scale_p[0])
    bulk, own, guess = volume_bulk(
        volume_guess, mass, wide, narrow, own, copied=True, after=(meanwhile,)
    )
    u0, face, first = finish(
        finish_first_kernel, 1, True, bulk, surface_guess, halos, volume_rhs
    )
    theta = theta_halos(edge_layers(u0), scale_v[1])
    bulk, own = volume_bulk(u0, mass, wide, narrow, own)
    s0_owner, s0 = surface_parts(scatter_sum(own, received, scale_p[0]))

    gathered = sector_gather(to_wire(s0_owner, scale_s[1]), scale_s[1])
    u0 = pass_after(u0, gathered[1])
    halos = theta + axial_halos(edge_layers(u0), scale_v[1])
    own, parts = bem_partial(1.0, False, place, bem_matrix, face, gathered)
    received, meanwhile = scatter(parts, scale_p[1])
    u1, face, second = finish(
        finish_second_kernel, 3, True, bulk, s0, halos, u0, after=(meanwhile,)
    )
    theta = theta_halos(edge_layers(u1), scale_v[2])
    bulk, own = volume_bulk(u1, mass, wide, narrow, own)
    s1_owner, s1 = surface_parts(scatter_sum(own, received, scale_p[1]))

    gathered = sector_gather(to_wire(s1_owner, scale_s[2]), scale_s[2])
    u1 = pass_after(u1, gathered[1])
    halos = theta + axial_halos(edge_layers(u1), scale_v[2])
    own, parts = bem_partial(1.0, False, place, bem_matrix, face, gathered, split=False)
    received, meanwhile = scatter(parts[:, :chunk], scale_p[2])
    (third,) = finish(
        finish_third_kernel, 5, False, bulk, s1, halos, u0, u1, after=(meanwhile,)
    )
    total = scatter_sum(own[:chunk], received, scale_p[2])

    gram = local_gram(sectors * slabs, first, second, third, s0_owner, s1_owner, total)
    gram_all = lax.all_to_all(gram, ("sector", "slab"), split_axis=0, concat_axis=0, tiled=True)
    return final_solution(gram_all, guess, u0, u1, surface_guess, s0, s1)


def solution(mesh):
    return jax.shard_map(
        per_device,
        mesh=mesh,
        in_specs=(
            P("sector", "slab", None, None),
            P("sector", "slab", None),
            P("sector", "slab", None, None),
            P("sector", "slab", None),
            P(None, "sector", "slab"),
            P(),
            P("sector", "slab", None),
        ),
        out_specs=(P("sector", "slab", None, None), P("sector", "slab", None)),
        check_vma=False,
    )
```

```python
import functools
import math

import jax
import jax.numpy as jnp
from jax import lax
from jax.experimental import pallas as pl
from jax.experimental.pallas import tpu as pltpu
from jax.sharding import PartitionSpec as P

PENALTY = 1.0
EPSILON = 1e-06
F32 = jnp.float32
BF16 = jnp.bfloat16
WIRE = jnp.float16
LANES = 256
HALF = 128
VMEM_LIMIT = 8 * 1024 * 1024
WHOLE = pl.BlockSpec(memory_space=pltpu.VMEM)
SCALARS = pl.BlockSpec(memory_space=pltpu.SMEM)
ANYWHERE = pl.BlockSpec(memory_space=pl.ANY)


def call(
    kernel, out_shape, n_scalars, n_arrays, n_anywhere=0, scratch=(), name=None, after=(), out_specs=None, aliases=None, vmem=VMEM_LIMIT,
):
    n_read = n_scalars + n_arrays + n_anywhere

    def body(*refs):
        kernel(*refs[:n_read], *refs[n_read + len(after) :])

    called = pl.pallas_call(
        body,
        out_shape=out_shape,
        in_specs=[SCALARS] * n_scalars
        + [WHOLE] * n_arrays
        + [ANYWHERE] * (n_anywhere + len(after)),
        out_specs=out_specs or jax.tree.map(lambda _: WHOLE, out_shape),
        scratch_shapes=list(scratch),
        input_output_aliases=aliases or {},
        compiler_params=pltpu.CompilerParams(vmem_limit_bytes=vmem),
        cost_estimate=pl.CostEstimate(flops=1000, bytes_accessed=1000, transcendentals=0),
        name=name,
    )
    return lambda *args: called(*args, *after)


def shape(*dims):
    return jax.ShapeDtypeStruct(dims, F32)


def split_bf16(values):
    upper = values.astype(BF16)
    lower = (values - upper.astype(F32)).astype(BF16)
    return upper, lower


def one_hot(rows, columns, pick):
    row = lax.broadcasted_iota(jnp.int32, (rows, columns), 0)
    column = lax.broadcasted_iota(jnp.int32, (rows, columns), 1)
    return (pick(row) == column).astype(F32)


def line_matrix(stiffness, order, nodes, rows, fast):
    select = one_hot(rows, order, lambda row: (row // fast) % order)
    spread = jnp.dot(select, stiffness, precision=lax.Precision.HIGHEST)
    full = lax.dot_general(
        spread, select, (((1,), (1,)), ((), ())), precision=lax.Precision.HIGHEST
    )
    row = lax.broadcasted_iota(jnp.int32, (rows, rows), 0)
    column = lax.broadcasted_iota(jnp.int32, (rows, rows), 1)
    row_node, column_node = row // fast, column // fast
    same_fast = row % fast == column % fast
    same_element = (row_node // order == column_node // order) & same_fast
    block = jnp.where(same_element, full, 0.0)
    edge = (row_node % order == 0) | (row_node % order == order - 1)
    block = block + jnp.where((row == column) & edge, PENALTY, 0.0)
    back = (row_node % order == 0) & (column_node == row_node - 1) & same_fast
    ahead = (row_node % order == order - 1) & (column_node == row_node + 1) & same_fast
    return block - jnp.where(back | ahead, PENALTY, 0.0)


def matrices_kernel(nodes, radial, stiffness_ref, wide_ref, narrow_ref):
    order = stiffness_ref.shape[1]
    rows = nodes * radial
    theta = line_matrix(stiffness_ref[0], order, nodes, rows, radial)
    axial = line_matrix(stiffness_ref[1], order, nodes, rows, radial)
    select = one_hot(rows, order, lambda row: row % radial)
    spread = jnp.dot(select, stiffness_ref[2], precision=lax.Precision.HIGHEST)
    full = lax.dot_general(
        spread, select, (((1,), (1,)), ((), ())), precision=lax.Precision.HIGHEST
    )
    row = lax.broadcasted_iota(jnp.int32, (rows, rows), 0)
    column = lax.broadcasted_iota(jnp.int32, (rows, rows), 1)
    axial = axial + jnp.where(row // radial == column // radial, full, 0.0)
    edge = (row % radial == 0) | (row % radial == radial - 1)
    axial = axial + jnp.where((row == column) & edge, PENALTY, 0.0)
    for index, matrix in enumerate((theta, axial)):
        upper, lower = split_bf16(matrix)
        wide_ref[index, :, :rows] = upper
        wide_ref[index, :, rows:] = upper
        narrow_ref[index] = lower


def volume_matrices(stiffness, nodes, radial, after=()):
    rows = nodes * radial
    return call(
        functools.partial(matrices_kernel, nodes, radial),
        (
            jax.ShapeDtypeStruct((2, rows, 2 * rows), BF16),
            jax.ShapeDtypeStruct((2, rows, rows), BF16),
        ),
        0,
        1,
        name="volume_matrices",
        after=after,
    )(stiffness)


def bulk_kernel(
    x_ref, mass_ref, wide_ref, narrow_ref, own_ref, y_ref, passed_ref, *copy_refs
):
    n_theta, n_axial, radial, lanes = x_ref.shape

    def product(index, values):
        upper, lower = split_bf16(values)
        both = jnp.concatenate([upper, lower], axis=0)
        return jnp.dot(wide_ref[index], both, preferred_element_type=F32) + jnp.dot(
            narrow_ref[index], upper, preferred_element_type=F32
        )

    def along_theta(z, carry):
        values = x_ref[:, z].reshape(n_theta * radial, lanes)
        y_ref[:, z] = product(0, values).reshape(n_theta, radial, lanes)
        return carry

    def along_axial(a, carry):
        values = x_ref[a].reshape(n_axial * radial, lanes)
        total = product(1, values).reshape(n_axial, radial, lanes)
        mass = mass_ref[a]
        old = y_ref[a] + total
        x = x_ref[a]
        y_ref[a, :, :, :HALF] = old[:, :, :HALF] + mass * x[:, :, :HALF]
        y_ref[a, :, :, HALF:] = old[:, :, HALF:] + mass * x[:, :, HALF:]
        return carry

    lax.fori_loop(0, n_axial, along_theta, 0, unroll=True)
    lax.fori_loop(0, n_theta, along_axial, 0, unroll=True)
    for copy_ref in copy_refs:
        copy_ref[...] = x_ref[...]


def volume_bulk(x, mass, wide, narrow, own, copied=False, after=()):
    outs = (shape(*x.shape), shape(*own.shape)) + ((shape(*x.shape),) if copied else ())
    return call(
        bulk_kernel,
        outs,
        0,
        5,
        name="volume_bulk",
        aliases={4: 1},
        after=after,
    )(x, mass, wide, narrow, own)


def edges_kernel(
    x_ref, first_ref, last_ref, axial_first_ref, axial_last_ref, face_ref, outer_ref, copied
):
    n_theta, n_axial, radial, _ = x_ref.shape
    copies = [
        pltpu.make_async_copy(source, target, copied.at[index])
        for index, (source, target) in enumerate(
            (
                (x_ref.at[0], first_ref),
                (x_ref.at[n_theta - 1], last_ref),
                (x_ref.at[:, 0], axial_first_ref),
                (x_ref.at[:, n_axial - 1], axial_last_ref),
                (x_ref.at[:, :, radial - 1], outer_ref),
            )
        )
    ]
    for copy in copies:
        copy.start()
    for copy in copies:
        copy.wait()
    for pair in range(face_ref.shape[0]):
        face_ref[pair] = 0.5 * (outer_ref[2 * pair] + outer_ref[2 * pair + 1])


def volume_edges(x):
    n_theta, n_axial, radial, lanes = x.shape
    theta, axial = shape(n_axial, radial, lanes), shape(n_theta, radial, lanes)
    *layers, face = call(
        edges_kernel,
        (theta, theta, axial, axial, shape(n_theta // 2, n_axial, lanes)),
        0,
        0,
        1,
        scratch=[
            pltpu.VMEM((n_theta, n_axial, lanes), F32),
            pltpu.SemaphoreType.DMA((5,)),
        ],
        name="volume_edges",
    )(x)
    return layers, face


def pass_after(values, *earlier):
    return call(
        lambda values_ref, out_ref: None,
        shape(*values.shape),
        0,
        1,
        name="pass_after",
        after=earlier,
        aliases={0: 0},
    )(values)


def pair_sums(left, right):
    left_real, left_imag = left[..., :HALF], left[..., HALF:]
    right_real, right_imag = right[..., :HALF], right[..., HALF:]
    return (
        jnp.sum(left_real * right_real + left_imag * right_imag, axis=0),
        jnp.sum(left_real * right_imag - left_imag * right_real, axis=0),
    )


def square_sums(values):
    squares = values * values
    return jnp.sum(squares[..., :HALF] + squares[..., HALF:], axis=0)


def finish_row(a, bulk, s_ref, before_ref, beyond_ref, axial_before_ref, axial_beyond_ref, n_theta):
    n_axial, radial, lanes = bulk.shape
    if isinstance(a, int) and a == 0:
        bulk = bulk - before_ref[...]
    if isinstance(a, int) and a == n_theta - 1:
        bulk = bulk - beyond_ref[...]
    outer = lax.broadcasted_iota(jnp.int32, (radial, lanes), 0) == radial - 1
    tiles = []
    for z in range(n_axial):
        tile = bulk[z]
        if z == 0:
            tile = tile - axial_before_ref[a]
        if z == n_axial - 1:
            tile = tile - axial_beyond_ref[a]
        face = jnp.broadcast_to(s_ref[a // 2, z : z + 1, :], (radial, lanes))
        tiles.append(tile + jnp.where(outer, face, 0.0))
    return jnp.stack(tiles)


def over_rows(n_theta, body):
    body(0)
    lax.fori_loop(1, n_theta - 1, lambda a, carry: (body(a), carry)[1], 0)
    body(n_theta - 1)


def put_faces(u_ref, face_ref):
    radial = u_ref.shape[2]
    for pair in range(face_ref.shape[0]):
        face_ref[pair] = 0.5 * (
            u_ref[2 * pair, :, radial - 1, :] + u_ref[2 * pair + 1, :, radial - 1, :]
        )


def finish_first_kernel(
    bulk_ref, s_ref, before_ref, beyond_ref, ax_before_ref, ax_beyond_ref, rhs_ref,
    u_ref, face_ref, sums_ref,
):
    n_theta = bulk_ref.shape[0]
    sums_ref[...] = jnp.zeros_like(sums_ref)

    def body(a):
        image = finish_row(
            a, bulk_ref[a], s_ref, before_ref, beyond_ref, ax_before_ref, ax_beyond_ref, n_theta
        )
        u = rhs_ref[a] - image
        u_ref[a] = u
        sums_ref[0] += square_sums(u)

    over_rows(n_theta, body)
    put_faces(u_ref, face_ref)


def finish_second_kernel(
    bulk_ref, s_ref, before_ref, beyond_ref, ax_before_ref, ax_beyond_ref, u0_ref,
    u_ref, face_ref, sums_ref,
):
    n_theta = bulk_ref.shape[0]
    sums_ref[...] = jnp.zeros_like(sums_ref)

    def body(a):
        u = finish_row(
            a, bulk_ref[a], s_ref, before_ref, beyond_ref, ax_before_ref, ax_beyond_ref, n_theta
        )
        u_ref[a] = u
        real, imag = pair_sums(u0_ref[a], u)
        sums_ref[0] += real
        sums_ref[1] += imag
        sums_ref[2] += square_sums(u)

    over_rows(n_theta, body)
    put_faces(u_ref, face_ref)


def finish_third_kernel(
    bulk_ref, s_ref, before_ref, beyond_ref, ax_before_ref, ax_beyond_ref, u0_ref, u1_ref,
    sums_ref,
):
    n_theta = bulk_ref.shape[0]
    sums_ref[...] = jnp.zeros_like(sums_ref)

    def body(a):
        u = finish_row(
            a, bulk_ref[a], s_ref, before_ref, beyond_ref, ax_before_ref, ax_beyond_ref, n_theta
        )
        real, imag = pair_sums(u0_ref[a], u)
        sums_ref[0] += real
        sums_ref[1] += imag
        real, imag = pair_sums(u1_ref[a], u)
        sums_ref[2] += real
        sums_ref[3] += imag
        sums_ref[4] += square_sums(u)

    over_rows(n_theta, body)


def finish(kernel, n_sums, with_result, bulk, s, halos, *others, after=()):
    n_theta, n_axial, radial, lanes = bulk.shape
    outs = (shape(n_sums, radial, HALF),)
    if with_result:
        outs = (shape(*bulk.shape), shape(n_theta // 2, n_axial, lanes)) + outs
    return call(
        kernel,
        outs,
        0,
        6 + len(others),
        name=kernel.__name__,
        after=after,
    )(bulk, s, *halos, *others)


def bem_kernel(sign, by_source, split, place_ref, m_ref, face_ref, *rest):
    own_ref, out_ref, upper_ref, lower_ref, p_ref = rest[-5:]
    out_chunk = own_ref.shape[0] // 2
    n_pieces = m_ref.shape[2] // out_chunk
    s_refs, rhs_refs = rest[:n_pieces], rest[n_pieces:-5]
    pairs, n_axial, lanes = face_ref.shape
    slabs = out_ref.shape[0] + 1
    axial_all = p_ref.shape[1]
    rows = m_ref.shape[1]
    slab = place_ref[0]
    turns = pairs // slabs

    def place_rows(s_ref, first, count, start):
        upper, lower = split_bf16(s_ref[first : first + count, :])
        at = pl.ds(pl.multiple_of(start, count), count)
        upper_ref[at, :] = upper
        if split:
            lower_ref[at, :] = lower

    for which, s_ref in enumerate(s_refs):
        start = place_ref[1 + which]
        if not by_source:
            place_rows(s_ref, 0, out_chunk, start)
            continue
        for source in range(slabs):
            for turn in range(turns):
                place_rows(
                    s_ref,
                    (source * turns + turn) * n_axial,
                    n_axial,
                    start + turn * axial_all + source * n_axial,
                )

    step = 2 * axial_all if axial_all < 128 else axial_all

    def block(index, carry):
        at = pl.ds(pl.multiple_of(index * step, step), step)
        real = m_ref[0, at, :]
        imag = m_ref[1, at, :]
        by_real = jnp.dot(real, upper_ref[...], preferred_element_type=F32)
        by_imag = jnp.dot(imag, upper_ref[...], preferred_element_type=F32)
        if split:
            by_real += jnp.dot(real, lower_ref[...], preferred_element_type=F32)
            by_imag += jnp.dot(imag, lower_ref[...], preferred_element_type=F32)
        here = pl.ds(index * (step // axial_all), step // axial_all)
        three = (step // axial_all, axial_all, HALF)
        p_ref[here, :, :HALF] = sign * (by_real[:, :HALF] - by_imag[:, HALF:]).reshape(three)
        p_ref[here, :, HALF:] = sign * (by_real[:, HALF:] + by_imag[:, :HALF]).reshape(three)
        return carry

    lax.fori_loop(0, rows // step, block, 0, unroll=True)
    own = pl.ds(pl.multiple_of(slab * n_axial, n_axial), n_axial)
    add = -sign * face_ref[...]
    for rhs_ref in rhs_refs:
        add = add + rhs_ref[...]
    p_ref[:, own, :] += add
    for shift in range(slabs):
        target = partner(slab, shift, slabs)
        part_ref = own_ref if shift == 0 else out_ref.at[shift - 1]
        for turn in range(turns):
            part_ref[turn * axial_all : (turn + 1) * axial_all, :] = p_ref[target + turn * slabs]
        there = pl.ds(pl.multiple_of(target * n_axial, n_axial), n_axial)
        part_ref[out_chunk:, :] = p_ref[:, there, :].reshape(out_chunk, lanes)


def bem_partial(sign, by_source, place, matrix, face, gathered, *rhs, split=True, after=()):
    pairs, n_axial, lanes = face.shape
    chunk = gathered[0].shape[0]
    rows, columns = matrix.shape[1:]
    axial_all = rows // pairs
    slabs = axial_all // n_axial
    return call(
        functools.partial(bem_kernel, sign, by_source, split),
        (shape(2 * chunk, lanes), shape(slabs - 1, 2 * chunk, lanes)),
        1,
        2 + len(gathered) + len(rhs),
        scratch=[
            pltpu.VMEM((columns, lanes), BF16),
            pltpu.VMEM((columns, lanes), BF16),
            pltpu.VMEM((pairs, axial_all, lanes), F32),
        ],
        name="bem_partial",
        after=after,
    )(place, matrix, face, *gathered, *rhs)


def surface_sums(u0, u1, u2):
    sums = (square_sums(u0),) + pair_sums(u0, u1) + (square_sums(u1),)
    return sums + pair_sums(u0, u2) + pair_sums(u1, u2) + (square_sums(u2),)


def gram_kernel(first_ref, second_ref, third_ref, s0_ref, s1_ref, s2_ref, out_ref):
    volume = (
        [first_ref[0]]
        + [second_ref[row] for row in range(3)]
        + [third_ref[row] for row in range(5)]
    )
    surface = surface_sums(s0_ref[...], s1_ref[...], s2_ref[...])
    for row, (one, two) in enumerate(zip(volume, surface)):
        total = jnp.sum(one, axis=0, keepdims=True) + jnp.sum(two, axis=0, keepdims=True)
        for device in range(out_ref.shape[0]):
            out_ref[device, :, row * HALF : (row + 1) * HALF] = total


def local_gram(devices, first, second, third, s0, s1, s2):
    tiles = [values.reshape(-1, 8, LANES) for values in (s0, s1, s2)]
    return call(gram_kernel, shape(devices, 1, 9 * HALF), 0, 6, name="local_gram")(
        first, second, third, *tiles
    )


def times(left, right):
    return (
        left[0] * right[0] - left[1] * right[1],
        left[0] * right[1] + left[1] * right[0],
    )


def conj_times(left, right):
    return (
        left[0] * right[0] + left[1] * right[1],
        left[0] * right[1] - left[1] * right[0],
    )


def square(value):
    return value[0] * value[0] + value[1] * value[1]


def coefficients(rows):
    g00, g11, g22 = rows[0], rows[3], rows[8]
    g01, g02, g12 = (rows[1], rows[2]), (rows[4], rows[5]), (rows[6], rows[7])
    beta_sq = g00 + EPSILON
    beta = jnp.sqrt(beta_sq)
    h00 = (g01[0] / beta_sq, g01[1] / beta_sq)
    h00_sq = square(h00)
    cross = conj_times(h00, g01)[0]
    rest = jnp.maximum(g11 - 2.0 * cross + h00_sq * g00, 0.0) / beta_sq
    h10_sq = rest + EPSILON
    h10 = jnp.sqrt(h10_sq)
    over_first = 1.0 / (beta_sq * h10)
    over_second = 1.0 / (beta_sq * h10_sq)
    h00_g01 = times(h00, g01)
    h01 = tuple((g02[k] - h00_g01[k]) * over_first for k in (0, 1))
    conj_g02 = conj_times(h00, g02)
    h11 = tuple(
        (g12[k] - h00[k] * g11 - conj_g02[k] + h00_sq * g01[k]) * over_second for k in (0, 1)
    )
    image_sq = (g22 - 2.0 * conj_times(h00, g12)[0] + h00_sq * g11) * over_second
    first_sq, second_sq = g00 / beta_sq, rest / h10_sq
    overlap = (h00[0] * EPSILON * over_first, h00[1] * EPSILON * over_first)
    mixed = conj_times(h01, times(h11, overlap))[0]
    bottom_sq = (
        jnp.maximum(
            image_sq
            - (2.0 - first_sq) * square(h01)
            - (2.0 - second_sq) * square(h11)
            + 2.0 * mixed,
            0.0,
        )
        + EPSILON
    )
    rho = jnp.sqrt(h00_sq + h10_sq)
    cos = (h00[0] / rho, h00[1] / rho)
    sine = h10 / rho
    top = conj_times(cos, h01)
    top = tuple(top[k] + sine * h11[k] for k in (0, 1))
    turn = times(cos, h11)
    turn = tuple(turn[k] - sine * h01[k] for k in (0, 1))
    lower = -sine * beta / (square(turn) + bottom_sq)
    one = (turn[0] * lower, -turn[1] * lower)
    top_one = times(top, one)
    zero = ((cos[0] * beta - top_one[0]) / rho, (-cos[1] * beta - top_one[1]) / rho)
    of_second = (one[0] / (beta * h10), one[1] / (beta * h10))
    back = times(of_second, h00)
    of_first = (zero[0] / beta - back[0], zero[1] / beta - back[1])
    return of_first, of_second


def combine(first, second, guess, u0, u1):
    u0_real, u0_imag = u0[..., :HALF], u0[..., HALF:]
    u1_real, u1_imag = u1[..., :HALF], u1[..., HALF:]
    real = guess[..., :HALF] + (first[0] * u0_real - first[1] * u0_imag)
    imag = guess[..., HALF:] + (first[0] * u0_imag + first[1] * u0_real)
    real = real + (second[0] * u1_real - second[1] * u1_imag)
    imag = imag + (second[0] * u1_imag + second[1] * u1_real)
    return real, imag


def solution_kernel(
    gram_ref, x_ref, u0_ref, u1_ref, s_ref, s0_ref, s1_ref,
    volume_ref, surface_ref, row_ref, stored,
):
    total = jnp.sum(gram_ref[...], axis=0)
    sums = [total[:, row * HALF : (row + 1) * HALF] for row in range(9)]
    first, second = coefficients(sums)
    n_theta = x_ref.shape[0]

    def store(a):
        return pltpu.make_async_copy(row_ref.at[a], volume_ref.at[a], stored.at[a])

    for a in range(n_theta):
        real, imag = combine(first, second, x_ref[a], u0_ref[a], u1_ref[a])
        row_ref[a, :, :, :HALF] = real
        row_ref[a, :, :, HALF:] = imag
        store(a).start()
    real, imag = combine(first, second, s_ref[...], s0_ref[...], s1_ref[...])
    surface_ref[..., :HALF] = real
    surface_ref[..., HALF:] = imag
    for a in range(n_theta):
        store(a).wait()


def final_solution(gram_all, x, u0, u1, s, s0, s1):
    return call(
        solution_kernel,
        (shape(*x.shape), shape(*s.shape)),
        0,
        7,
        scratch=[pltpu.VMEM(x.shape, F32), pltpu.SemaphoreType.DMA((x.shape[0],))],
        name="final_solution",
        out_specs=(ANYWHERE, WHOLE),
    )(gram_all, x, u0, u1, s, s0, s1)


def power_scale(bound):
    return 2.0 ** math.floor(math.log2(60000.0 / bound))


def to_wire(values, scale):
    return (values * scale).astype(WIRE)


def from_wire(values, scale):
    return values.astype(F32) * (1.0 / scale)


def partner(index, distance, peers):
    if peers & (peers - 1) == 0:
        return index ^ distance
    return lax.rem(index + distance, peers)


def partner_perm(peers, distance):
    if peers & (peers - 1) == 0:
        return [(i, i ^ distance) for i in range(peers)]
    return [(i, (i + distance) % peers) for i in range(peers)]


def slab_exchange(messages):
    slabs = lax.axis_size("slab")
    received = [
        lax.ppermute(messages[distance], "slab", partner_perm(slabs, distance))
        for distance in reversed(range(1, slabs))
    ]
    return received[::-1]


def neighbour_swap(axis, first, last, scale, wrap):
    peers = lax.axis_size(axis)
    odd = lax.rem(lax.axis_index(axis), 2) == 1
    first, last = to_wire(first, scale), to_wire(last, scale)
    within = [(i, i ^ 1) for i in range(peers)]
    across = [
        pair
        for i in range(1, peers if wrap else peers - 1, 2)
        for pair in ((i, (i + 1) % peers), ((i + 1) % peers, i))
    ]
    inner = lax.ppermute(jnp.where(odd, first, last), axis, within)
    outer = lax.ppermute(jnp.where(odd, last, first), axis, across)
    before = from_wire(jnp.where(odd, inner, outer), scale)
    beyond = from_wire(jnp.where(odd, outer, inner), scale)
    return before, beyond


def theta_halos(layers, scale):
    return neighbour_swap("sector", *layers[:2], scale, True)


def axial_halos(layers, scale):
    return neighbour_swap("slab", *layers[2:], scale, False)


def edge_layers(volume):
    return volume[0], volume[-1], volume[:, 0], volume[:, -1]


def sibling_perm():
    return [(i, i ^ 1) for i in range(lax.axis_size("sector"))]


def sector_gather(own, scale):
    sectors = lax.axis_size("sector")
    shares = [own]
    for distance in reversed(range(1, sectors // 2)):
        perm = [
            (2 * i + core, 2 * j + core)
            for i, j in [(i, (i + distance) % (sectors // 2)) for i in range(sectors // 2)]
            for core in range(2)
        ]
        shares.append(lax.ppermute(own, "sector", perm))
    gathered = []
    for share in shares:
        gathered += [share, lax.ppermute(share, "sector", sibling_perm())]
    return [from_wire(share, scale) for share in gathered]


def gather_places(chunk):
    chips = lax.axis_size("sector") // 2
    sector = lax.axis_index("sector")
    chip, core = sector // 2, lax.rem(sector, 2)
    places = [lax.axis_index("slab")]
    for distance in [0] + list(reversed(range(1, chips))):
        source = lax.rem(chip - distance + chips, chips)
        places += [(2 * source + core) * chunk, (2 * source + 1 - core) * chunk]
    return jnp.stack([jnp.asarray(value, jnp.int32) for value in places])


def owners_first_kernel(surface_ref, out_ref):
    chips, slabs, turns = out_ref.shape[:3]
    for chip in range(chips):
        for owner in range(slabs):
            for turn in range(turns):
                out_ref[chip, owner, turn] = surface_ref[turn * slabs + owner]


def first_gather(surface, scale):
    sectors, slabs = lax.axis_size("sector"), lax.axis_size("slab")
    chips = sectors // 2
    pairs, n_axial, lanes = surface.shape
    turns = pairs // slabs
    by_owner = call(
        owners_first_kernel,
        shape(chips, slabs, turns, n_axial, lanes),
        0,
        1,
        name="owners_first",
    )(surface)
    messages = to_wire(by_owner, scale)
    groups = [
        [(2 * chip + core) * slabs + slab for chip in range(chips) for slab in range(slabs)]
        for core in range(2)
    ]
    mine = lax.all_to_all(
        messages.reshape(chips * slabs, turns * n_axial, lanes),
        ("sector", "slab"),
        split_axis=0,
        concat_axis=0,
        axis_index_groups=groups,
        tiled=True,
    )
    other = lax.ppermute(mine, "sector", sibling_perm())
    mine, other = (
        from_wire(values, scale).reshape(chips, slabs * turns * n_axial, lanes)
        for values in (mine, other)
    )
    return [values[chip] for chip in range(chips) for values in (mine, other)]


def first_places(chunk):
    sectors = lax.axis_size("sector")
    core = lax.rem(lax.axis_index("sector"), 2)
    places = [lax.axis_index("slab")]
    for chip in range(sectors // 2):
        places += [(2 * chip + core) * chunk, (2 * chip + 1 - core) * chunk]
    return jnp.stack([jnp.asarray(value, jnp.int32) for value in places])


def scatter(parts, scale):
    messages = [None] + [to_wire(parts[which], scale) for which in range(parts.shape[0])]
    meanwhile = lax.ppermute(messages[-1][:16, :HALF], "sector", sibling_perm())
    return slab_exchange(messages), meanwhile.astype(F32)


def scatter_sum(own, received, scale):
    for message in received:
        own = own + from_wire(message, scale)
    return own


def per_device(
    volume_rhs, surface_rhs, volume_guess, surface_guess, bem_matrix, stiffness, mass_shift
):
    slabs, sectors = lax.axis_size("slab"), lax.axis_size("sector")
    slab = lax.axis_index("slab")
    n_theta, n_axial, radial, lanes = volume_guess.shape
    pairs = surface_guess.shape[0]
    axial_all = n_axial * slabs
    turns = pairs // slabs
    chunk = turns * axial_all
    unknowns = sectors * pairs * axial_all

    gain = 8.0 * math.sqrt(unknowns)
    stiff = 3 * stiffness.shape[1] * 3.0 + 6 + 3.0
    surface_0 = 6.0
    volume_0 = 6.0
    surface_1 = gain * surface_0 + 12.0
    volume_1 = 80.0 + stiff * volume_0 + surface_0
    surface_2 = gain * surface_1 + volume_1
    volume_2 = stiff * volume_1 + surface_1
    scale_s = [power_scale(bound) for bound in (surface_0, surface_1, surface_2)]
    scale_v = [power_scale(bound) for bound in (volume_0, volume_1, volume_2)]
    scale_p = [
        power_scale(gain / slabs * surface_0 + 12.0),
        power_scale(gain / slabs * surface_1 + volume_1),
        power_scale(gain / slabs * surface_2 + volume_2),
    ]

    place = gather_places(chunk)

    def surface_parts(total):
        return total[:chunk], total[chunk:].reshape(pairs, n_axial, lanes)

    gathered = first_gather(surface_guess, scale_s[0])
    mass = jnp.broadcast_to(mass_shift[..., None], mass_shift.shape + (HALF,))
    wide, narrow = volume_matrices(stiffness, n_theta, radial, after=(gathered[0],))
    layers, face = volume_edges(volume_guess)
    halos = theta_halos(layers, scale_v[0]) + axial_halos(layers, scale_v[0])
    own, parts = bem_partial(
        -1.0, True, first_places(chunk), bem_matrix, face, gathered, surface_rhs,
        after=(narrow,),
    )
    received, meanwhile = scatter(parts, scale_p[0])
    bulk, own, guess = volume_bulk(
        volume_guess, mass, wide, narrow, own, copied=True, after=(meanwhile,)
    )
    u0, face, first = finish(
        finish_first_kernel, 1, True, bulk, surface_guess, halos, volume_rhs
    )
    theta = theta_halos(edge_layers(u0), scale_v[1])
    bulk, own = volume_bulk(u0, mass, wide, narrow, own)
    s0_owner, s0 = surface_parts(scatter_sum(own, received, scale_p[0]))

    gathered = sector_gather(to_wire(s0_owner, scale_s[1]), scale_s[1])
    u0 = pass_after(u0, gathered[1])
    halos = theta + axial_halos(edge_layers(u0), scale_v[1])
    own, parts = bem_partial(1.0, False, place, bem_matrix, face, gathered)
    received, meanwhile = scatter(parts, scale_p[1])
    u1, face, second = finish(
        finish_second_kernel, 3, True, bulk, s0, halos, u0, after=(meanwhile,)
    )
    theta = theta_halos(edge_layers(u1), scale_v[2])
    bulk, own = volume_bulk(u1, mass, wide, narrow, own)
    s1_owner, s1 = surface_parts(scatter_sum(own, received, scale_p[1]))

    gathered = sector_gather(to_wire(s1_owner, scale_s[2]), scale_s[2])
    u1 = pass_after(u1, gathered[1])
    halos = theta + axial_halos(edge_layers(u1), scale_v[2])
    own, parts = bem_partial(1.0, False, place, bem_matrix, face, gathered, split=False)
    received, meanwhile = scatter(parts[:, :chunk], scale_p[2])
    (third,) = finish(
        finish_third_kernel, 5, False, bulk, s1, halos, u0, u1, after=(meanwhile,)
    )
    total = scatter_sum(own[:chunk], received, scale_p[2])

    gram = local_gram(sectors * slabs, first, second, third, s0_owner, s1_owner, total)
    gram_all = lax.all_to_all(gram, ("sector", "slab"), split_axis=0, concat_axis=0, tiled=True)
    return final_solution(gram_all, guess, u0, u1, surface_guess, s0, s1)


def solution(mesh):
    return jax.shard_map(
        per_device,
        mesh=mesh,
        in_specs=(
            P("sector", "slab", None, None),
            P("sector", "slab", None),
            P("sector", "slab", None, None),
            P("sector", "slab", None),
            P(None, "sector", "slab"),
            P(),
            P("sector", "slab", None),
        ),
        out_specs=(P("sector", "slab", None, None), P("sector", "slab", None)),
        check_vma=False,
    )
```
